32 devices in a mesh: wide: 16 (over z, y, x), narrow: 2 (over core).
Axes of the slice: x: 2, y: 2, z: 4, core: 2. Of those that a mesh axis runs over, the one named last changes fastest.
Arguments:
- inverse: bfloat16 [4096, 4096], P('wide', 'narrow')
- panel: bfloat16 [2, 4096, 4096], P(None, 'narrow', 'wide'), may hold values from -0.109375 to 0.109375
- factor_inv: bfloat16 [2, 4096, 4096], P(None, 'wide', 'narrow')
- structure: int32 [2, 12], replicated, may hold values from 0 to 15, as said below
Outputs:
- cross: bfloat16 [4096, 2, 4096], P('narrow', None, 'wide')
- variance: float32 [2, 4096], P(None, 'narrow')
The draws below stay inside these ranges and needn't reach their ends.
Inputs may be any that keep to these rules, and one draw needn't show every extreme that they name: `structure`: row k lists 12 distinct block indices in increasing order; the last, 15, is always listed.
All inputs are finite; a program needn't handle non-finite values.
Results may differ from the reference program's by a relative error of at most 0.0013.
Values may be sent and summed in bfloat16 or wider, within the bound.
No kernel may reach another device: no remote copies, remote signals or barrier semaphores. Data moves between devices by JAX's collectives and lax.ppermute only.
A program may use at most 192 MiB of HBM per device.

```python
import math
import jax
import jax.numpy as jnp

KW = 4096
BLK = 256
NSUP = 2
NB = 16
NA = 4096
NSB = 12


def draw_inverse(key, part):
    key_off = jax.random.fold_in(key, 11)
    key_diag = jax.random.fold_in(key, 12)
    rough = jax.random.normal(key_off, (NA, NA), jnp.float32)
    lowest = 8.0
    highest = 64.0
    off_part = (rough + rough.T) * (12.0 / math.sqrt(2.0 * NA))
    diagonal = jnp.exp(jax.random.uniform(key_diag, (NA,), jnp.float32, math.log(lowest), math.log(highest)))
    identity = (jnp.arange(NA)[:, None] == jnp.arange(NA)[None, :]).astype(jnp.float32)
    return (off_part + identity * diagonal[None, :]).astype(jnp.bfloat16)


def draw_factor_inv(key, part):
    key_off = jax.random.fold_in(key, 21)
    key_diag = jax.random.fold_in(key, 22)
    rough = jax.random.normal(key_off, (NSUP, KW, KW), jnp.float32)
    lower = (jnp.arange(KW)[:, None] > jnp.arange(KW)[None, :]).astype(jnp.float32)
    identity = (jnp.arange(KW)[:, None] == jnp.arange(KW)[None, :]).astype(jnp.float32)
    diagonal = jnp.exp(jax.random.uniform(key_diag, (NSUP, 1, KW), jnp.float32, math.log(0.5), math.log(2.0)))
    values = rough * (2.0 / math.sqrt(KW)) * lower[None] + identity[None] * diagonal
    return values.astype(jnp.bfloat16)


def draw_structure(key, part):
    rows_list = []
    for sup_index in range(NSUP):
        shuffled = jax.random.permutation(jax.random.fold_in(key, 31 + sup_index), NB - 1)
        chosen = jnp.sort(shuffled[:NSB - 1].astype(jnp.int32))
        last_block = jnp.full((1,), NB - 1, jnp.int32)
        rows_list.append(jnp.concatenate([chosen, last_block]).astype(jnp.int32))
    return jnp.stack(rows_list)


def level_of(own_key, dims, split, low, largest):
    def one(position, blocks):
        heights = jax.random.uniform(jax.random.fold_in(jax.random.fold_in(own_key, 6), position), (blocks,), jnp.float32, low / len(split), largest / len(split))
        return jnp.repeat(jnp.exp(heights), dims[position] // blocks).reshape((-1,) + (1,) * (len(dims) - position - 1))

    factor_of = one(*split[0])
    for cut in split[1:]:
        factor_of = factor_of * one(*cut)
    return factor_of


def scatter_about(rng, extent, width, limit, pieces=(), held_as=jnp.bfloat16):
    result = jax.random.normal(rng, extent, jnp.float32) * width
    if len(pieces) > 0:
        result = level_of(rng, extent, pieces, -0.22, 0.18) * result
    return jnp.clip(result, min=-limit, max=limit).astype(held_as)


def setup_inputs(seed: int = 0) -> dict:
    keys = jax.random.split(jax.random.key(seed), 5)
    inverse = draw_inverse(jax.random.fold_in(keys[4], 71), 0)
    panel = scatter_about(keys[1], (NSUP, NA, KW), (NSB * BLK) ** -0.5, 0.109375, ((1, 2), (2, 16)))
    factor_inv = draw_factor_inv(jax.random.fold_in(keys[4], 71), 0)
    structure = draw_structure(jax.random.fold_in(keys[4], 71), 0)
    return dict(inverse=inverse, panel=panel, factor_inv=factor_inv, structure=structure)


def reference(inverse, panel, factor_inv, structure):
    block_ids = jnp.arange(NB, dtype=jnp.int32)
    in_structure = jnp.any(structure[:, :, None] == block_ids[None, None, :], axis=1)
    cross_list = []
    variance_list = []
    for sup_index in range(NSUP):
        row_mask = jnp.repeat(in_structure[sup_index], BLK).astype(jnp.float32)
        retained = (panel[sup_index].astype(jnp.float32) * row_mask[:, None]).astype(jnp.bfloat16)
        cross_part = -row_mask[:, None] * jnp.dot(inverse, retained, preferred_element_type=jnp.float32)
        linv_part = jnp.sum(jnp.square(factor_inv[sup_index].astype(jnp.float32)), axis=0)
        variance_list.append(linv_part - jnp.sum(panel[sup_index].astype(jnp.float32) * cross_part, axis=0))
        cross_list.append(cross_part.T.astype(jnp.bfloat16))
    return jnp.stack(cross_list, axis=1), jnp.stack(variance_list)
```

```python
import jax
import jax.numpy as jnp
from jax import lax
from jax.experimental import pallas as pl
from jax.experimental.pallas import tpu as pltpu
from jax.sharding import PartitionSpec as P

BLK = 256
LANES = 128
ANY = pl.BlockSpec(memory_space=pl.ANY)


def spread(value, axis, source):
    kept = jnp.where(lax.axis_index(axis) == source, value, 0).astype(value.dtype)
    return lax.psum(kept, axis)


def block_partial(gathered, inverse, row_inside, col_inside, first_row, row_count):
    local_blocks = inverse.shape[1] // BLK
    running = jnp.zeros((row_count, BLK), jnp.float32)
    for blk_index in range(local_blocks):

        def product(blk_index=blk_index):
            panel_piece = lax.dynamic_slice(
                gathered, (blk_index * BLK, first_row), (BLK, row_count)
            )
            block_z = inverse[:, blk_index * BLK : (blk_index + 1) * BLK]
            return lax.dot_general(
                panel_piece, block_z, (((0,), (1,)), ((), ())), preferred_element_type=jnp.float32
            )

        def skipped():
            return jnp.zeros((row_count, BLK), jnp.float32)

        running = running + lax.cond(row_inside & col_inside[blk_index], product, skipped)
    return -running


def per_device_general(inverse, panel, factor_inv, structure):
    wide_count = lax.axis_size("wide")
    narrow_count = lax.axis_size("narrow")
    nsup_count = panel.shape[0]
    kw_total = panel.shape[2] * wide_count
    kw_local = kw_total // narrow_count
    local_blocks = inverse.shape[1] // BLK
    row_index = lax.axis_index("wide")
    col_first = lax.axis_index("narrow") * local_blocks
    col_ids = col_first + jnp.arange(local_blocks, dtype=jnp.int32)
    row_inside = jnp.any(structure == row_index, axis=1)
    col_inside = jnp.any(structure[:, :, None] == col_ids[None, None, :], axis=1)
    root_index = row_index // local_blocks
    offset = (row_index - root_index * local_blocks) * BLK
    cross_parts = []
    own_parts = []
    for sup_index in range(nsup_count):
        gathered_one = lax.all_gather(panel[sup_index], "wide", axis=1, tiled=True)

        def one_term(first_row, row_count, gathered_one=gathered_one, sup_index=sup_index):
            return block_partial(
                gathered_one,
                inverse,
                row_inside[sup_index],
                col_inside[sup_index],
                first_row,
                row_count,
            )

        cross_parts.append(
            lax.psum_scatter(
                one_term(jnp.int32(0), kw_local * lax.axis_size("narrow")),
                "narrow",
                scatter_dimension=0,
                tiled=True,
            )
        )
        own_parts.append(lax.dynamic_slice_in_dim(gathered_one, offset, BLK, axis=0))
    cross_f = jnp.stack(cross_parts, axis=1)
    own_rows = jnp.stack(own_parts)
    owner_panel = spread(own_rows, "narrow", root_index)
    owner_slice = lax.dynamic_slice_in_dim(
        owner_panel, lax.axis_index("narrow") * kw_local, kw_local, axis=2
    )
    weighted = jnp.einsum("kia,aki->ka", owner_slice.astype(jnp.float32), cross_f)
    linv_part = jnp.sum(jnp.square(factor_inv.astype(jnp.float32)), axis=1)
    variance = lax.psum(linv_part - weighted, "wide")
    return (cross_f.astype(jnp.bfloat16), variance)


X, Y, ZL, ZH = 1, 2, 4, 8
NGRP = 4


def swap_cores(value):
    return lax.ppermute(value, "narrow", [(0, 1), (1, 0)])


def hop(value, mask):
    size = lax.axis_size("wide")
    return lax.ppermute(value, "wide", [(i, i ^ mask) for i in range(size)])


def pack_panel(structure, panel, other):
    nblocks = structure.shape[1]
    half_blocks = panel.shape[1] // BLK

    def body(st, panel_ref, other_ref, out0, out1, sem):
        n = lax.axis_index("narrow")
        outs = (out0, out1)

        def copies(j):
            b = st[n, j]
            row = pl.multiple_of(lax.rem(b, half_blocks) * BLK, BLK)
            mine = lax.div(b, half_blocks) == n
            return mine, [
                (
                    pltpu.make_async_copy(
                        panel_ref.at[n, pl.ds(row, BLK), pl.ds(c * LANES, LANES)],
                        outs[c].at[pl.ds(j * BLK, BLK), :],
                        sem.at[j, c],
                    ),
                    pltpu.make_async_copy(
                        other_ref.at[pl.ds(row, BLK), pl.ds(c * LANES, LANES)],
                        outs[c].at[pl.ds(j * BLK, BLK), :],
                        sem.at[j, c],
                    ),
                )
                for c in range(2)
            ]

        for j in range(nblocks):
            mine, pairs = copies(j)
            for own, oth in pairs:
                pl.when(mine)(own.start)
                pl.when(jnp.logical_not(mine))(oth.start)
        for j in range(nblocks):
            mine, pairs = copies(j)
            for own, oth in pairs:
                oth.wait()

    shape = jax.ShapeDtypeStruct((nblocks * BLK, LANES), panel.dtype)
    return pl.pallas_call(
        body,
        out_shape=(shape, shape),
        grid_spec=pltpu.PrefetchScalarGridSpec(
            num_scalar_prefetch=1,
            grid=(1,),
            in_specs=[ANY, ANY],
            out_specs=[ANY, ANY],
            scratch_shapes=[pltpu.SemaphoreType.DMA((nblocks, 2))],
        ),
        name="pack_panel",
    )(structure, panel, other)


def pack_inverse(structure, owns, others):
    nblocks = structure.shape[1]
    half_blocks = owns[0].shape[1] // BLK

    def body(st, *refs):
        own_refs, oth_refs = refs[:NGRP], refs[NGRP : 2 * NGRP]
        out, sem = refs[2 * NGRP :]
        n = lax.axis_index("narrow")
        for start in (True, False):
            for j in range(nblocks):
                b = st[n, j]
                col = pl.multiple_of(lax.rem(b, half_blocks) * BLK, BLK)
                mine = lax.div(b, half_blocks) == n
                for d in range(NGRP):
                    own, oth = [
                        pltpu.make_async_copy(
                            ref.at[:, pl.ds(col, BLK)],
                            out.at[d, :, pl.ds(j * BLK, BLK)],
                            sem.at[j, d],
                        )
                        for ref in (own_refs[d], oth_refs[d])
                    ]
                    if start:
                        pl.when(mine)(own.start)
                        pl.when(jnp.logical_not(mine))(oth.start)
                    else:
                        oth.wait()

    return pl.pallas_call(
        body,
        out_shape=jax.ShapeDtypeStruct((NGRP, BLK, nblocks * BLK), owns[0].dtype),
        grid_spec=pltpu.PrefetchScalarGridSpec(
            num_scalar_prefetch=1,
            grid=(1,),
            in_specs=[ANY] * (2 * NGRP),
            out_specs=ANY,
            scratch_shapes=[pltpu.SemaphoreType.DMA((nblocks, NGRP))],
        ),
        name="pack_inverse",
    )(structure, *owns, *others)


def products(structure, sel, pieces):
    nblocks = structure.shape[1]
    depth = nblocks * BLK

    def body(st, sel_ref, b0, b1, b2, b3, out_ref, sum_ref):
        d = pl.program_id(0)
        n = lax.axis_index("narrow")
        w = lax.axis_index("wide")
        x = lax.bitwise_and(w, 1)
        zh = lax.div(w, ZH)
        mask = lax.rem(d, 2) * Y + lax.div(d, 2) * ZL
        row = lax.bitwise_xor(w, mask)
        pos = jnp.int32(0)
        inside = jnp.int32(0)
        for j in range(nblocks):
            hit = (st[n, j] == row).astype(jnp.int32)
            pos = pos + j * hit
            inside = inside + hit
        pos = pl.multiple_of(pos * BLK, BLK)
        refs = (b0, b1, b2, b3)

        @pl.when(d == 0)
        def _():
            sum_ref[...] = jnp.zeros_like(sum_ref)

        @pl.when(inside == 0)
        def _():
            out_ref[...] = jnp.zeros_like(out_ref)

        @pl.when(inside > 0)
        def _():
            for dz in range(2):
                away = (lax.bitwise_xor(zh, dz) != n).astype(jnp.int32)
                left, right = refs[2 * dz], refs[2 * dz + 1]
                acc = jnp.zeros((BLK, 2 * LANES), jnp.float32)
                acc = jnp.dot(
                    sel_ref[0],
                    jnp.concatenate([left[...], right[...]], axis=1),
                    preferred_element_type=jnp.float32,
                )
                for dx in range(2):
                    part = acc[:, dx * LANES : (dx + 1) * LANES]
                    slot = lax.bitwise_xor(x, dx)
                    rows = refs[2 * dz + dx][pl.ds(pos, BLK), :].astype(jnp.float32)
                    sum_ref[away, slot] += jnp.sum(part * rows, axis=0, keepdims=True)
                    out_ref[away, 0, slot] = (-part).T.astype(out_ref.dtype)

    whole = pl.BlockSpec((depth, LANES), lambda d, st: (0, 0))
    return pl.pallas_call(
        body,
        out_shape=(
            jax.ShapeDtypeStruct((2, NGRP, 2, LANES, BLK), sel.dtype),
            jax.ShapeDtypeStruct((2, 2, 1, LANES), jnp.float32),
        ),
        grid_spec=pltpu.PrefetchScalarGridSpec(
            num_scalar_prefetch=1,
            grid=(NGRP,),
            in_specs=[pl.BlockSpec((1, BLK, depth), lambda d, st: (d, 0, 0))] + [whole] * 4,
            out_specs=[
                pl.BlockSpec((2, 1, 2, LANES, BLK), lambda d, st: (0, d, 0, 0, 0)),
                pl.BlockSpec((2, 2, 1, LANES), lambda d, st: (0, 0, 0, 0)),
            ],
        ),
        compiler_params=pltpu.CompilerParams(vmem_limit_bytes=40 * 1024 * 1024),
        cost_estimate=pl.CostEstimate(
            flops=2 * NGRP * BLK * depth * 4 * LANES,
            bytes_accessed=2 * (NGRP * BLK * depth + 4 * depth * LANES),
            transcendentals=0,
        ),
        name="products",
    )(structure, sel, *pieces)


def assemble(messages, chunk, held):
    tall = 4 * LANES
    rows_total = 2 * 2 * NGRP * tall

    def body(*refs):
        msg_refs = refs[:NGRP]
        out, wide_buf, narrow_buf, sem = refs[-4:]
        n = lax.axis_index("narrow")
        w = lax.axis_index("wide")
        copies = []
        for d in range(NGRP):
            source = lax.bitwise_xor(lax.rem(lax.div(w, Y), NGRP), d)
            for xx in range(2):
                slot = 2 * d + xx
                for k in range(2):
                    which = (n != k).astype(jnp.int32)
                    value = msg_refs[d][which, xx].astype(jnp.float32)
                    for lt in range(2):
                        wide_buf[slot, pl.ds(2 * lt + k, LANES, stride=4), :] = value[
                            :, lt * LANES : (lt + 1) * LANES
                        ]
                narrow_buf[slot] = wide_buf[slot].astype(narrow_buf.dtype)
                row = pl.multiple_of(((source * 2 + xx) * 2 + chunk) * tall, tall)
                copy = pltpu.make_async_copy(
                    narrow_buf.at[slot], out.at[pl.ds(row, tall), :], sem.at[slot]
                )
                copy.start()
                copies.append(copy)
        for copy in copies:
            copy.wait()

    vmem = pl.BlockSpec(memory_space=pltpu.VMEM)
    extra = () if held is None else (held,)
    return pl.pallas_call(
        body,
        out_shape=jax.ShapeDtypeStruct((rows_total, LANES), messages[0].dtype),
        in_specs=[vmem] * NGRP + [ANY] * len(extra),
        out_specs=ANY,
        scratch_shapes=[
            pltpu.VMEM((2 * NGRP, tall, LANES), jnp.float32),
            pltpu.VMEM((2 * NGRP, tall, LANES), messages[0].dtype),
            pltpu.SemaphoreType.DMA((2 * NGRP,)),
        ],
        input_output_aliases={NGRP: 0} if extra else {},
        compiler_params=pltpu.CompilerParams(vmem_limit_bytes=16 * 1024 * 1024),
        name="assemble",
    )(*messages, *extra)


def per_device_grid(inverse, panel, factor_inv, structure):
    n = lax.axis_index("narrow")
    w = lax.axis_index("wide")
    other = swap_cores(lax.dynamic_index_in_dim(panel, 1 - n, 0, keepdims=False))
    a_y = hop(inverse, Y)
    a_z = hop(inverse, ZL)
    chunks = pack_panel(structure, panel, other)
    a_yz = hop(a_z, Y)
    owns = [inverse, a_y, a_z, a_yz]
    others = [swap_cores(a) for a in owns]
    linv_part = jnp.sum(jnp.square(factor_inv.astype(jnp.float32)), axis=1)
    sel = pack_inverse(structure, owns, others)
    held = None
    sums = []
    for c, mine in enumerate(chunks):
        b_x = hop(mine, X)
        b_z = hop(mine, ZH)
        b_xz = hop(b_z, X)
        out, sum_c = products(structure, sel, (mine, b_x, b_z, b_xz))
        sums.append(sum_c)
        kept, sent = out[0], out[1]
        back = swap_cores(sent)
        messages = []
        for d in range(NGRP):
            message = jnp.stack([kept[d], back[d]])
            if d:
                message = hop(message, (d % 2) * Y + (d // 2) * ZL)
            messages.append(message)
        held = assemble(messages, c, held)
    half = panel.shape[2] * lax.axis_size("wide") // 2
    cross = held.reshape(half, 2, 2, LANES).transpose(0, 2, 1, 3).reshape(half, 2, BLK)
    both = jnp.concatenate(sums, axis=2)
    kept, sent = both[0].reshape(-1), both[1].reshape(-1)
    back = swap_cores(sent)
    pair = jnp.where(n == 0, jnp.stack([kept, back]), jnp.stack([back, kept]))
    group = lax.rem(lax.div(w, Y), NGRP)
    spots = jnp.arange(NGRP, dtype=jnp.int32)[None, :, None] == group
    placed = jnp.where(spots, pair[:, None, :], 0.0).reshape(2, half)
    variance = linv_part + placed
    for mask in (Y, ZL, X, ZH):
        variance = variance + hop(variance, mask)
    return cross, variance


def solution(mesh):
    in_specs = (P("wide", "narrow"), P(None, "narrow", "wide"), P(None, "wide", "narrow"), P())
    out_specs = (P("narrow", None, "wide"), P(None, "narrow"))

    def run(inverse, panel, factor_inv, structure):
        fits = (
            mesh.shape["wide"] == 16
            and mesh.shape["narrow"] == 2 == panel.shape[0]
            and panel.shape[2] == 16 * BLK == inverse.shape[0]
        )
        return jax.shard_map(
            per_device_grid if fits else per_device_general,
            mesh=mesh,
            in_specs=in_specs,
            out_specs=out_specs,
            check_vma=False,
        )(inverse, panel, factor_inv, structure)

    return run
```

```python
import jax
import jax.numpy as jnp
from jax import lax
from jax.experimental import pallas as pl
from jax.experimental.pallas import tpu as pltpu
from jax.sharding import PartitionSpec as P

BLK = 256
LANES = 128
ANY = pl.BlockSpec(memory_space=pl.ANY)
VMEM = pl.BlockSpec(memory_space=pltpu.VMEM)
SMEM = pl.BlockSpec(memory_space=pltpu.SMEM)


def spread(value, axis, source):
    kept = jnp.where(lax.axis_index(axis) == source, value, 0).astype(value.dtype)
    return lax.psum(kept, axis)


def block_partial(gathered, inverse, row_inside, col_inside, first_row, row_count):
    local_blocks = inverse.shape[1] // BLK
    running = jnp.zeros((row_count, BLK), jnp.float32)
    for blk_index in range(local_blocks):

        def product(blk_index=blk_index):
            panel_piece = lax.dynamic_slice(
                gathered, (blk_index * BLK, first_row), (BLK, row_count)
            )
            block_z = inverse[:, blk_index * BLK : (blk_index + 1) * BLK]
            return lax.dot_general(
                panel_piece, block_z, (((0,), (1,)), ((), ())), preferred_element_type=jnp.float32
            )

        def skipped():
            return jnp.zeros((row_count, BLK), jnp.float32)

        running = running + lax.cond(row_inside & col_inside[blk_index], product, skipped)
    return -running


def per_device_general(inverse, panel, factor_inv, structure):
    wide_count = lax.axis_size("wide")
    narrow_count = lax.axis_size("narrow")
    nsup_count = panel.shape[0]
    kw_total = panel.shape[2] * wide_count
    kw_local = kw_total // narrow_count
    local_blocks = inverse.shape[1] // BLK
    row_index = lax.axis_index("wide")
    col_first = lax.axis_index("narrow") * local_blocks
    col_ids = col_first + jnp.arange(local_blocks, dtype=jnp.int32)
    row_inside = jnp.any(structure == row_index, axis=1)
    col_inside = jnp.any(structure[:, :, None] == col_ids[None, None, :], axis=1)
    root_index = row_index // local_blocks
    offset = (row_index - root_index * local_blocks) * BLK
    cross_parts = []
    own_parts = []
    for sup_index in range(nsup_count):
        gathered_one = lax.all_gather(panel[sup_index], "wide", axis=1, tiled=True)

        def one_term(first_row, row_count, gathered_one=gathered_one, sup_index=sup_index):
            return block_partial(
                gathered_one,
                inverse,
                row_inside[sup_index],
                col_inside[sup_index],
                first_row,
                row_count,
            )

        cross_parts.append(
            lax.psum_scatter(
                one_term(jnp.int32(0), kw_local * lax.axis_size("narrow")),
                "narrow",
                scatter_dimension=0,
                tiled=True,
            )
        )
        own_parts.append(lax.dynamic_slice_in_dim(gathered_one, offset, BLK, axis=0))
    cross_f = jnp.stack(cross_parts, axis=1)
    own_rows = jnp.stack(own_parts)
    owner_panel = spread(own_rows, "narrow", root_index)
    owner_slice = lax.dynamic_slice_in_dim(
        owner_panel, lax.axis_index("narrow") * kw_local, kw_local, axis=2
    )
    weighted = jnp.einsum("kia,aki->ka", owner_slice.astype(jnp.float32), cross_f)
    linv_part = jnp.sum(jnp.square(factor_inv.astype(jnp.float32)), axis=1)
    variance = lax.psum(linv_part - weighted, "wide")
    return (cross_f.astype(jnp.bfloat16), variance)


X, Y, ZL, ZH = 1, 2, 4, 8
NGRP = 4


def swap_cores(value, name):
    with jax.named_scope(name):
        return lax.ppermute(value, "narrow", [(0, 1), (1, 0)])


def hop(value, mask, name):
    size = lax.axis_size("wide")
    with jax.named_scope(name):
        return lax.ppermute(value, "wide", [(i, i ^ mask) for i in range(size)])


def after(value, *earlier):
    return lax.optimization_barrier((value, *earlier))[0]


def pick(structure_ref, n, j, first):
    nblocks = structure_ref.shape[1]
    start = jnp.where(n == 0, 0, nblocks - first)
    return structure_ref[n, lax.rem(start + j, nblocks)]


def pack_first(structure, panel, first):
    half_blocks = panel.shape[1] // BLK

    def body(st, panel_ref, out):
        n = lax.axis_index("narrow")
        for j in range(first):
            row = pl.multiple_of(lax.rem(pick(st, n, j, first), half_blocks) * BLK, BLK)
            out[j * BLK : (j + 1) * BLK, :] = panel_ref[n, pl.ds(row, BLK), :]

    return pl.pallas_call(
        body,
        out_shape=jax.ShapeDtypeStruct((first * BLK, panel.shape[2]), panel.dtype),
        in_specs=[SMEM, VMEM],
        out_specs=VMEM,
        compiler_params=pltpu.CompilerParams(vmem_limit_bytes=16 * 1024 * 1024),
        name="pack_first",
    )(structure, panel)


def pack_rest(structure, panel, other, first):
    nblocks = structure.shape[1]
    half_blocks = panel.shape[1] // BLK

    def body(st, panel_ref, other_ref, out0, out1):
        n = lax.axis_index("narrow")
        for j in range(nblocks - first):
            b = pick(st, n, first + j, first)
            row = pl.multiple_of(lax.rem(b, half_blocks) * BLK, BLK)
            mine = lax.div(b, half_blocks) == n
            rows = slice(j * BLK, (j + 1) * BLK)

            @pl.when(mine)
            def _():
                out0[rows, :] = panel_ref[n, pl.ds(row, BLK), :LANES]
                out1[rows, :] = panel_ref[n, pl.ds(row, BLK), LANES:]

            @pl.when(jnp.logical_not(mine))
            def _():
                out0[rows, :] = other_ref[pl.ds(row, BLK), :LANES]
                out1[rows, :] = other_ref[pl.ds(row, BLK), LANES:]

    shape = jax.ShapeDtypeStruct(((nblocks - first) * BLK, LANES), panel.dtype)
    return pl.pallas_call(
        body,
        out_shape=(shape, shape),
        in_specs=[SMEM, VMEM, VMEM],
        out_specs=[VMEM, VMEM],
        compiler_params=pltpu.CompilerParams(vmem_limit_bytes=16 * 1024 * 1024),
        cost_estimate=pl.CostEstimate(flops=2 * 10**10, bytes_accessed=0, transcendentals=0),
        name="pack_rest",
    )(structure, panel, other)


def pack_inverse(structure, owns, others, first):
    nblocks = structure.shape[1]
    half_blocks = owns[0].shape[1] // BLK

    def body(st, *refs):
        own_refs, oth_refs = refs[:NGRP], refs[NGRP : 2 * NGRP]
        out = refs[2 * NGRP]
        n = lax.axis_index("narrow")
        for j in range(nblocks):
            b = pick(st, n, j, first)
            col = pl.multiple_of(lax.rem(b, half_blocks) * BLK, BLK)
            mine = lax.div(b, half_blocks) == n

            def move(sources, j=j, col=col):
                for d in range(NGRP):
                    out[d, :, j * BLK : (j + 1) * BLK] = sources[d][:, pl.ds(col, BLK)]

            pl.when(mine)(lambda move=move: move(own_refs))
            pl.when(jnp.logical_not(mine))(lambda move=move: move(oth_refs))

    return pl.pallas_call(
        body,
        out_shape=jax.ShapeDtypeStruct((NGRP, BLK, nblocks * BLK), owns[0].dtype),
        in_specs=[SMEM] + [VMEM] * (2 * NGRP),
        out_specs=VMEM,
        compiler_params=pltpu.CompilerParams(vmem_limit_bytes=32 * 1024 * 1024),
        name="pack_inverse",
    )(structure, *owns, *others)


def products(structure, sel, firsts, rests, chunk, dz):
    nblocks = structure.shape[1]
    early = firsts[0].shape[0]
    late = rests[0].shape[0]
    first = early // BLK

    def body(st, sel_ref, f0, f1, r0, r1, out_ref, sum_ref):
        d = pl.program_id(0)
        n = lax.axis_index("narrow")
        w = lax.axis_index("wide")
        x = lax.bitwise_and(w, 1)
        mask = lax.rem(d, 2) * Y + lax.div(d, 2) * ZL
        row = lax.bitwise_xor(w, mask)
        pos = jnp.int32(0)
        inside = jnp.int32(0)
        for j in range(nblocks):
            hit = (pick(st, n, j, first) == row).astype(jnp.int32)
            pos = pos + j * hit
            inside = inside + hit

        @pl.when(d == 0)
        def _():
            sum_ref[...] = jnp.zeros_like(sum_ref)

        @pl.when(inside == 0)
        def _():
            out_ref[...] = jnp.zeros_like(out_ref)

        @pl.when(inside > 0)
        def _():
            acc = jnp.dot(
                sel_ref[0, :, :early],
                jnp.concatenate([f0[...], f1[...]], axis=1),
                preferred_element_type=jnp.float32,
            ) + jnp.dot(
                sel_ref[0, :, early:],
                jnp.concatenate([r0[...], r1[...]], axis=1),
                preferred_element_type=jnp.float32,
            )
            for dx in range(2):
                part = acc[:, dx * LANES : (dx + 1) * LANES]
                slot = lax.bitwise_xor(x, dx)

                def weigh(rows, part=part, slot=slot):
                    total = jnp.sum(part * rows.astype(jnp.float32), axis=0, keepdims=True)
                    sum_ref[slot] += total

                @pl.when(pos < first)
                def _():
                    at = pl.multiple_of(pos * BLK, BLK)
                    weigh((f0, f1)[dx][pl.ds(at, BLK), :])

                @pl.when(pos >= first)
                def _():
                    at = pl.multiple_of((pos - first) * BLK, BLK)
                    weigh((r0, r1)[dx][pl.ds(at, BLK), :])

                out_ref[0, slot] = (-part).T.astype(out_ref.dtype)

    front = pl.BlockSpec((early, LANES), lambda d, st: (0, chunk))
    back = pl.BlockSpec((late, LANES), lambda d, st: (0, 0))
    return pl.pallas_call(
        body,
        out_shape=(
            jax.ShapeDtypeStruct((NGRP, 2, LANES, BLK), sel.dtype),
            jax.ShapeDtypeStruct((2, 1, LANES), jnp.float32),
        ),
        grid_spec=pltpu.PrefetchScalarGridSpec(
            num_scalar_prefetch=1,
            grid=(NGRP,),
            in_specs=[
                pl.BlockSpec((1, BLK, early + late), lambda d, st: (d, 0, 0)),
                front,
                front,
                back,
                back,
            ],
            out_specs=[
                pl.BlockSpec((1, 2, LANES, BLK), lambda d, st: (d, 0, 0, 0)),
                pl.BlockSpec((2, 1, LANES), lambda d, st: (0, 0, 0)),
            ],
        ),
        compiler_params=pltpu.CompilerParams(vmem_limit_bytes=32 * 1024 * 1024),
        cost_estimate=pl.CostEstimate(
            flops=2 * NGRP * BLK * (early + late) * 2 * LANES,
            bytes_accessed=2 * (NGRP * BLK + 2 * LANES) * (early + late),
            transcendentals=0,
        ),
        name="products",
    )(structure, sel, *firsts, *rests)


def assemble(messages, chunk, held):
    tall = 4 * LANES
    rows_total = 2 * 2 * NGRP * tall

    def body(*refs):
        msg_refs = refs[:NGRP]
        out, wide_buf, narrow_buf, sem = refs[-4:]
        n = lax.axis_index("narrow")
        w = lax.axis_index("wide")
        copies = []
        for d in range(NGRP):
            source = lax.bitwise_xor(lax.rem(lax.div(w, Y), NGRP), d)
            for xx in range(2):
                slot = 2 * d + xx
                for k in range(2):
                    which = (n != k).astype(jnp.int32)
                    value = msg_refs[d][which, xx].astype(jnp.float32)
                    for lt in range(2):
                        wide_buf[slot, pl.ds(2 * lt + k, LANES, stride=4), :] = value[
                            :, lt * LANES : (lt + 1) * LANES
                        ]
                narrow_buf[slot] = wide_buf[slot].astype(narrow_buf.dtype)
                row = pl.multiple_of(((source * 2 + xx) * 2 + chunk) * tall, tall)
                copy = pltpu.make_async_copy(
                    narrow_buf.at[slot], out.at[pl.ds(row, tall), :], sem.at[slot]
                )
                copy.start()
                copies.append(copy)
        for copy in copies:
            copy.wait()

    extra = () if held is None else (held,)
    return pl.pallas_call(
        body,
        out_shape=jax.ShapeDtypeStruct((rows_total, LANES), messages[0].dtype),
        in_specs=[VMEM] * NGRP + [ANY] * len(extra),
        out_specs=ANY,
        scratch_shapes=[
            pltpu.VMEM((2 * NGRP, tall, LANES), jnp.float32),
            pltpu.VMEM((2 * NGRP, tall, LANES), messages[0].dtype),
            pltpu.SemaphoreType.DMA((2 * NGRP,)),
        ],
        input_output_aliases={NGRP: 0} if extra else {},
        compiler_params=pltpu.CompilerParams(vmem_limit_bytes=16 * 1024 * 1024),
        name="assemble",
    )(*messages, *extra)


def per_device_grid(inverse, panel, factor_inv, structure):
    n = lax.axis_index("narrow")
    w = lax.axis_index("wide")
    zh = lax.div(w, ZH)
    first = structure.shape[1] - panel.shape[1] // BLK
    f_own = pack_first(structure, panel, first)
    other = swap_cores(lax.dynamic_index_in_dim(panel, 1 - n, 0, keepdims=False), "panel_swap")
    r_own = pack_rest(structure, panel, after(other, f_own), first)
    f_z = hop(f_own, ZH, "first_z")
    f_x = hop(f_own, X, "first_x")
    ahead = after(inverse, f_own)
    a_y = hop(ahead, Y, "inv_y")
    a_z = hop(ahead, ZL, "inv_z")
    s_own = swap_cores(after(inverse, *r_own), "inv_swap")
    r_x0 = hop(after(r_own[0], f_x, s_own), X, "rest0_x")
    f_z, r_x0, a_y, a_z = lax.optimization_barrier((f_z, r_x0, a_y, a_z))
    r_z0 = hop(after(r_own[0], f_z), ZH, "rest0_z")
    r_x1 = hop(after(r_own[1], f_z), X, "rest1_x")
    f_xz = hop(f_z, X, "first_xz")
    a_yz = hop(a_z, Y, "inv_yz")
    s_y = swap_cores(a_y, "inv_swap_y")
    r_z0, r_x1, f_xz, a_yz, s_y = lax.optimization_barrier((r_z0, r_x1, f_xz, a_yz, s_y))
    r_z1 = hop(after(r_own[1], r_z0), ZH, "rest1_z")
    r_xz0 = hop(r_z0, X, "rest0_xz")
    s_z = swap_cores(after(a_z, r_z0), "inv_swap_z")
    s_yz = swap_cores(a_yz, "inv_swap_yz")
    owns = [inverse, a_y, a_z, a_yz]
    others = [s_own, s_y, s_z, s_yz]
    linv_part = jnp.sum(jnp.square(factor_inv.astype(jnp.float32)), axis=1)
    sel = pack_inverse(structure, owns, others, first)
    stay = n == zh

    def parts(near, far):
        return jnp.where(stay, near, far), jnp.where(stay, far, near)

    def deliver(near, far, c):
        kept, sent = parts(near, far)
        back = swap_cores(sent, f"cross{c}_swap")
        messages = [jnp.stack([kept[d], back[d]]) for d in range(NGRP)]
        return messages[:1] + [
            hop(messages[d], (d % 2) * Y + (d // 2) * ZL, f"cross{c}_{d}") for d in range(1, NGRP)
        ]

    near, near_sum = products(structure, sel, (f_own, f_x), (r_own[0], r_x0), 0, 0)
    far, far_sum = products(structure, sel, (f_z, f_xz), (r_z0, r_xz0), 0, 1)
    sums = [parts(near_sum, far_sum)]
    messages = deliver(near, far, 0)
    near, near_sum = products(structure, sel, (f_own, f_x), (r_own[1], r_x1), 1, 0)
    r_xz1 = hop(after(r_z1, near), X, "rest1_xz")
    r_xz1, *messages = lax.optimization_barrier((r_xz1, *messages))
    far, far_sum = products(structure, sel, (f_z, f_xz), (r_z1, r_xz1), 1, 1)
    sums.append(parts(near_sum, far_sum))
    held = assemble(messages, 0, None)
    held = assemble(deliver(near, far, 1), 1, held)
    half = panel.shape[2] * lax.axis_size("wide") // 2
    cross = held.reshape(half, 2, 2, LANES).transpose(0, 2, 1, 3).reshape(half, 2, BLK)
    kept, sent = [jnp.concatenate([sums[0][i], sums[1][i]], axis=1).reshape(-1) for i in (0, 1)]
    back = swap_cores(sent, "sums_swap")
    pair = jnp.where(n == 0, jnp.stack([kept, back]), jnp.stack([back, kept]))
    group = lax.rem(lax.div(w, Y), NGRP)
    spots = jnp.arange(NGRP, dtype=jnp.int32)[None, :, None] == group
    placed = jnp.where(spots, pair[:, None, :], 0.0).reshape(2, half)
    variance = linv_part + placed
    for mask in (Y, ZL, X, ZH):
        variance = variance + hop(variance, mask, f"variance_{mask}")
    return cross, variance


def solution(mesh):
    in_specs = (P("wide", "narrow"), P(None, "narrow", "wide"), P(None, "wide", "narrow"), P())
    out_specs = (P("narrow", None, "wide"), P(None, "narrow"))

    def run(inverse, panel, factor_inv, structure):
        fits = (
            mesh.shape["wide"] == 16
            and mesh.shape["narrow"] == 2 == panel.shape[0]
            and panel.shape[2] == 16 * BLK == inverse.shape[0]
        )
        return jax.shard_map(
            per_device_grid if fits else per_device_general,
            mesh=mesh,
            in_specs=in_specs,
            out_specs=out_specs,
            check_vma=False,
        )(inverse, panel, factor_inv, structure)

    return run
```

```python
import jax
import jax.numpy as jnp
from jax import lax
from jax.experimental import pallas as pl
from jax.experimental.pallas import tpu as pltpu
from jax.sharding import PartitionSpec as P

BLK = 256
LANES = 128
ANY = pl.BlockSpec(memory_space=pl.ANY)
VMEM = pl.BlockSpec(memory_space=pltpu.VMEM)
SMEM = pl.BlockSpec(memory_space=pltpu.SMEM)


def spread(value, axis, source):
    kept = jnp.where(lax.axis_index(axis) == source, value, 0).astype(value.dtype)
    return lax.psum(kept, axis)


def block_partial(gathered, inverse, row_inside, col_inside, first_row, row_count):
    local_blocks = inverse.shape[1] // BLK
    running = jnp.zeros((row_count, BLK), jnp.float32)
    for blk_index in range(local_blocks):

        def product(blk_index=blk_index):
            panel_piece = lax.dynamic_slice(
                gathered, (blk_index * BLK, first_row), (BLK, row_count)
            )
            block_z = inverse[:, blk_index * BLK : (blk_index + 1) * BLK]
            return lax.dot_general(
                panel_piece, block_z, (((0,), (1,)), ((), ())), preferred_element_type=jnp.float32
            )

        def skipped():
            return jnp.zeros((row_count, BLK), jnp.float32)

        running = running + lax.cond(row_inside & col_inside[blk_index], product, skipped)
    return -running


def per_device_general(inverse, panel, factor_inv, structure):
    wide_count = lax.axis_size("wide")
    narrow_count = lax.axis_size("narrow")
    nsup_count = panel.shape[0]
    kw_total = panel.shape[2] * wide_count
    kw_local = kw_total // narrow_count
    local_blocks = inverse.shape[1] // BLK
    row_index = lax.axis_index("wide")
    col_first = lax.axis_index("narrow") * local_blocks
    col_ids = col_first + jnp.arange(local_blocks, dtype=jnp.int32)
    row_inside = jnp.any(structure == row_index, axis=1)
    col_inside = jnp.any(structure[:, :, None] == col_ids[None, None, :], axis=1)
    root_index = row_index // local_blocks
    offset = (row_index - root_index * local_blocks) * BLK
    cross_parts = []
    own_parts = []
    for sup_index in range(nsup_count):
        gathered_one = lax.all_gather(panel[sup_index], "wide", axis=1, tiled=True)

        def one_term(first_row, row_count, gathered_one=gathered_one, sup_index=sup_index):
            return block_partial(
                gathered_one,
                inverse,
                row_inside[sup_index],
                col_inside[sup_index],
                first_row,
                row_count,
            )

        cross_parts.append(
            lax.psum_scatter(
                one_term(jnp.int32(0), kw_local * lax.axis_size("narrow")),
                "narrow",
                scatter_dimension=0,
                tiled=True,
            )
        )
        own_parts.append(lax.dynamic_slice_in_dim(gathered_one, offset, BLK, axis=0))
    cross_f = jnp.stack(cross_parts, axis=1)
    own_rows = jnp.stack(own_parts)
    owner_panel = spread(own_rows, "narrow", root_index)
    owner_slice = lax.dynamic_slice_in_dim(
        owner_panel, lax.axis_index("narrow") * kw_local, kw_local, axis=2
    )
    weighted = jnp.einsum("kia,aki->ka", owner_slice.astype(jnp.float32), cross_f)
    linv_part = jnp.sum(jnp.square(factor_inv.astype(jnp.float32)), axis=1)
    variance = lax.psum(linv_part - weighted, "wide")
    return (cross_f.astype(jnp.bfloat16), variance)


X, Y, ZL, ZH = 1, 2, 4, 8
NGRP = 4
SPLIT = 192


def swap_cores(value, name):
    with jax.named_scope(name):
        return lax.ppermute(value, "narrow", [(0, 1), (1, 0)])


def hop(value, mask, name):
    size = lax.axis_size("wide")
    with jax.named_scope(name):
        return lax.ppermute(value, "wide", [(i, i ^ mask) for i in range(size)])


def after(value, *earlier):
    return lax.optimization_barrier((value, *earlier))[0]


def pick(structure_ref, n, j, first):
    nblocks = structure_ref.shape[1]
    start = jnp.where(n == 0, 0, nblocks - first)
    return structure_ref[n, lax.rem(start + j, nblocks)]


def pack_first(structure, panel, first):
    half_blocks = panel.shape[1] // BLK

    def body(st, panel_ref, out):
        n = lax.axis_index("narrow")
        for j in range(first):
            row = pl.multiple_of(lax.rem(pick(st, n, j, first), half_blocks) * BLK, BLK)
            out[j * BLK : (j + 1) * BLK, :] = panel_ref[n, pl.ds(row, BLK), :]

    return pl.pallas_call(
        body,
        out_shape=jax.ShapeDtypeStruct((first * BLK, panel.shape[2]), panel.dtype),
        in_specs=[SMEM, VMEM],
        out_specs=VMEM,
        compiler_params=pltpu.CompilerParams(vmem_limit_bytes=6 * 1024 * 1024),
        name="pack_first",
    )(structure, panel)


def pack_rest(structure, panel, other, first):
    nblocks = structure.shape[1]
    half_blocks = panel.shape[1] // BLK

    def body(st, panel_ref, other_ref, out0, out1):
        n = lax.axis_index("narrow")
        for j in range(nblocks - first):
            b = pick(st, n, first + j, first)
            row = pl.multiple_of(lax.rem(b, half_blocks) * BLK, BLK)
            mine = lax.div(b, half_blocks) == n
            rows = slice(j * BLK, (j + 1) * BLK)

            @pl.when(mine)
            def _():
                out0[rows, :] = panel_ref[n, pl.ds(row, BLK), :LANES]
                out1[rows, :] = panel_ref[n, pl.ds(row, BLK), LANES:]

            @pl.when(jnp.logical_not(mine))
            def _():
                out0[rows, :] = other_ref[pl.ds(row, BLK), :LANES]
                out1[rows, :] = other_ref[pl.ds(row, BLK), LANES:]

    shape = jax.ShapeDtypeStruct(((nblocks - first) * BLK, LANES), panel.dtype)
    return pl.pallas_call(
        body,
        out_shape=(shape, shape),
        in_specs=[SMEM, VMEM, VMEM],
        out_specs=[VMEM, VMEM],
        compiler_params=pltpu.CompilerParams(vmem_limit_bytes=8 * 1024 * 1024),
        name="pack_rest",
    )(structure, panel, other)


def pack_inverse(structure, owns, others, first):
    nblocks = structure.shape[1]
    half_blocks = owns[0].shape[1] // BLK
    count = len(owns)

    def body(st, *refs):
        own_refs, oth_refs, out = refs[:count], refs[count : 2 * count], refs[2 * count]
        n = lax.axis_index("narrow")
        for j in range(nblocks):
            b = pick(st, n, j, first)
            col = pl.multiple_of(lax.rem(b, half_blocks) * BLK, BLK)
            mine = lax.div(b, half_blocks) == n

            def move(sources, j=j, col=col):
                d = 0
                for source in sources:
                    for at in range(0, source.shape[0], BLK):
                        out[d, :, j * BLK : (j + 1) * BLK] = source[at : at + BLK, pl.ds(col, BLK)]
                        d += 1

            pl.when(mine)(lambda move=move: move(own_refs))
            pl.when(jnp.logical_not(mine))(lambda move=move: move(oth_refs))

    return pl.pallas_call(
        body,
        out_shape=jax.ShapeDtypeStruct((NGRP, BLK, nblocks * BLK), owns[0].dtype),
        in_specs=[SMEM] + [VMEM] * (2 * count),
        out_specs=VMEM,
        compiler_params=pltpu.CompilerParams(vmem_limit_bytes=20 * 1024 * 1024),
        name="pack_inverse",
    )(structure, *owns, *others)


def products(structure, sel, firsts, rests, chunk, dz):
    nblocks = structure.shape[1]
    early = firsts[0].shape[0]
    late = rests[0].shape[0]
    first = early // BLK

    def body(st, sel_ref, f0, f1, r0, r1, out_ref, sum_ref):
        d = pl.program_id(0)
        n = lax.axis_index("narrow")
        w = lax.axis_index("wide")
        x = lax.bitwise_and(w, 1)
        mask = lax.rem(d, 2) * Y + lax.div(d, 2) * ZL
        row = lax.bitwise_xor(w, mask)
        pos = jnp.int32(0)
        inside = jnp.int32(0)
        for j in range(nblocks):
            hit = (pick(st, n, j, first) == row).astype(jnp.int32)
            pos = pos + j * hit
            inside = inside + hit

        @pl.when(d == 0)
        def _():
            sum_ref[...] = jnp.zeros_like(sum_ref)

        @pl.when(inside == 0)
        def _():
            out_ref[...] = jnp.zeros_like(out_ref)

        @pl.when(inside > 0)
        def _():
            acc = jnp.dot(
                sel_ref[0, :, :early],
                jnp.concatenate([f0[...], f1[...]], axis=1),
                preferred_element_type=jnp.float32,
            ) + jnp.dot(
                sel_ref[0, :, early:],
                jnp.concatenate([r0[...], r1[...]], axis=1),
                preferred_element_type=jnp.float32,
            )
            for dx in range(2):
                part = acc[:, dx * LANES : (dx + 1) * LANES]
                slot = lax.bitwise_xor(x, dx)

                def weigh(rows, part=part, slot=slot):
                    total = jnp.sum(part * rows.astype(jnp.float32), axis=0, keepdims=True)
                    sum_ref[slot] += total

                @pl.when(pos < first)
                def _():
                    at = pl.multiple_of(pos * BLK, BLK)
                    weigh((f0, f1)[dx][pl.ds(at, BLK), :])

                @pl.when(pos >= first)
                def _():
                    at = pl.multiple_of((pos - first) * BLK, BLK)
                    weigh((r0, r1)[dx][pl.ds(at, BLK), :])

                out_ref[0, slot] = (-part).T.astype(out_ref.dtype)

    front = pl.BlockSpec((early, LANES), lambda d, st: (0, chunk))
    back = pl.BlockSpec((late, LANES), lambda d, st: (0, 0))
    return pl.pallas_call(
        body,
        out_shape=(
            jax.ShapeDtypeStruct((NGRP, 2, LANES, BLK), sel.dtype),
            jax.ShapeDtypeStruct((2, 1, LANES), jnp.float32),
        ),
        grid_spec=pltpu.PrefetchScalarGridSpec(
            num_scalar_prefetch=1,
            grid=(NGRP,),
            in_specs=[
                pl.BlockSpec((1, BLK, early + late), lambda d, st: (d, 0, 0)),
                front,
                front,
                back,
                back,
            ],
            out_specs=[
                pl.BlockSpec((1, 2, LANES, BLK), lambda d, st: (d, 0, 0, 0)),
                pl.BlockSpec((2, 1, LANES), lambda d, st: (0, 0, 0)),
            ],
        ),
        compiler_params=pltpu.CompilerParams(vmem_limit_bytes=16 * 1024 * 1024),
        cost_estimate=pl.CostEstimate(flops=0, bytes_accessed=0, transcendentals=0),
        name="products",
    )(structure, sel, *firsts, *rests)


def assemble(messages, chunk, held):
    tall = 4 * LANES
    rows_total = 2 * 2 * NGRP * tall

    def body(*refs):
        msg_refs = refs[:NGRP]
        out, wide_buf, narrow_buf, sem = refs[-4:]
        n = lax.axis_index("narrow")
        w = lax.axis_index("wide")
        copies = []
        for d in range(NGRP):
            source = lax.bitwise_xor(lax.rem(lax.div(w, Y), NGRP), d)
            for xx in range(2):
                slot = 2 * d + xx
                for k in range(2):
                    which = (n != k).astype(jnp.int32)
                    value = msg_refs[d][which, xx].astype(jnp.float32)
                    for lt in range(2):
                        wide_buf[slot, pl.ds(2 * lt + k, LANES, stride=4), :] = value[
                            :, lt * LANES : (lt + 1) * LANES
                        ]
                narrow_buf[slot] = wide_buf[slot].astype(narrow_buf.dtype)
                row = pl.multiple_of(((source * 2 + xx) * 2 + chunk) * tall, tall)
                copy = pltpu.make_async_copy(
                    narrow_buf.at[slot], out.at[pl.ds(row, tall), :], sem.at[slot]
                )
                copy.start()
                copies.append(copy)
        for copy in copies:
            copy.wait()

    extra = () if held is None else (held,)
    return pl.pallas_call(
        body,
        out_shape=jax.ShapeDtypeStruct((rows_total, LANES), messages[0].dtype),
        in_specs=[VMEM] * NGRP + [ANY] * len(extra),
        out_specs=ANY,
        scratch_shapes=[
            pltpu.VMEM((2 * NGRP, tall, LANES), jnp.float32),
            pltpu.VMEM((2 * NGRP, tall, LANES), messages[0].dtype),
            pltpu.SemaphoreType.DMA((2 * NGRP,)),
        ],
        input_output_aliases={NGRP: 0} if extra else {},
        compiler_params=pltpu.CompilerParams(vmem_limit_bytes=16 * 1024 * 1024),
        name="assemble",
    )(*messages, *extra)


def per_device_grid(inverse, panel, factor_inv, structure):
    n = lax.axis_index("narrow")
    w = lax.axis_index("wide")
    zh = lax.div(w, ZH)
    first = structure.shape[1] - panel.shape[1] // BLK
    f_own = pack_first(structure, panel, first)
    other = swap_cores(
        lax.dynamic_index_in_dim(after(panel, f_own), 1 - n, 0, keepdims=False), "panel_swap"
    )
    r_own = pack_rest(structure, panel, other, first)
    f_z = hop(f_own, ZH, "first_z")
    f_x = hop(f_own, X, "first_x")
    ahead = after(inverse, f_own)
    top, bottom = ahead[:SPLIT], ahead[SPLIT:]
    a_y = hop(ahead, Y, "inv_y")
    a_z0 = hop(top, ZL, "inv_z0")
    s_own = swap_cores(after(inverse, other), "inv_swap")
    f_z, f_x, a_y, a_z0, s_own, *r_own = lax.optimization_barrier(
        (f_z, f_x, a_y, a_z0, s_own, *r_own)
    )
    r_z0 = hop(r_own[0], ZH, "rest0_z")
    a_z1 = hop(after(bottom, f_z), ZL, "inv_z1")
    f_xz = hop(f_z, X, "first_xz")
    a_yz0 = hop(a_z0, Y, "inv_yz0")
    a_yz1 = hop(a_z1, Y, "inv_yz1")
    r_x0 = hop(after(r_own[0], f_z), X, "rest0_x")
    r_z0, f_xz, a_yz0, a_yz1, r_x0 = lax.optimization_barrier((r_z0, f_xz, a_yz0, a_yz1, r_x0))
    r_z1 = hop(after(r_own[1], r_z0), ZH, "rest1_z")
    r_xz0 = hop(r_z0, X, "rest0_xz")
    more = jnp.concatenate([after(a_y, r_z0), a_z0, a_z1, a_yz0, a_yz1])
    s_more = swap_cores(more, "inv_swap_more")
    owns = [inverse, more]
    others = [s_own, s_more]
    linv_part = jnp.sum(jnp.square(factor_inv.astype(jnp.float32)), axis=1)
    sel = pack_inverse(structure, owns, others, first)
    stay = n == zh

    def parts(near, far):
        return jnp.where(stay, near, far), jnp.where(stay, far, near)

    def deliver(near, far, c):
        kept, sent = parts(near, far)
        back = swap_cores(sent, f"cross{c}_swap")
        messages = [jnp.stack([kept[d], back[d]]) for d in range(NGRP)]
        return messages[:1] + [
            hop(messages[d], (d % 2) * Y + (d // 2) * ZL, f"cross{c}_{d}") for d in range(1, NGRP)
        ]

    near, near_sum = products(structure, sel, (f_own, f_x), (r_own[0], r_x0), 0, 0)
    far, far_sum = products(structure, sel, (f_z, f_xz), (r_z0, r_xz0), 0, 1)
    sums = [parts(near_sum, far_sum)]
    messages = deliver(near, far, 0)
    r_x1 = hop(after(r_own[1], sel), X, "rest1_x")
    near, near_sum = products(structure, sel, (f_own, f_x), (r_own[1], r_x1), 1, 0)
    r_xz1 = hop(r_z1, X, "rest1_xz")
    r_xz1, *messages = lax.optimization_barrier((r_xz1, *messages))
    far, far_sum = products(structure, sel, (f_z, f_xz), (r_z1, r_xz1), 1, 1)
    sums.append(parts(near_sum, far_sum))
    held = assemble(messages, 0, None)
    held = assemble(deliver(near, far, 1), 1, held)
    half = panel.shape[2] * lax.axis_size("wide") // 2
    cross = held.reshape(half, 2, 2, LANES).transpose(0, 2, 1, 3).reshape(half, 2, BLK)
    kept, sent = [jnp.concatenate([sums[0][i], sums[1][i]], axis=1).reshape(-1) for i in (0, 1)]
    back = swap_cores(sent, "sums_swap")
    pair = jnp.where(n == 0, jnp.stack([kept, back]), jnp.stack([back, kept]))
    group = lax.rem(lax.div(w, Y), NGRP)
    spots = jnp.arange(NGRP, dtype=jnp.int32)[None, :, None] == group
    placed = jnp.where(spots, pair[:, None, :], 0.0).reshape(2, half)
    variance = linv_part + placed
    for mask in (X, ZH, Y, ZL):
        variance = variance + hop(variance, mask, f"variance_{mask}")
    return cross, variance


def solution(mesh):
    in_specs = (P("wide", "narrow"), P(None, "narrow", "wide"), P(None, "wide", "narrow"), P())
    out_specs = (P("narrow", None, "wide"), P(None, "narrow"))

    def run(inverse, panel, factor_inv, structure):
        fits = (
            mesh.shape["wide"] == 16
            and mesh.shape["narrow"] == 2 == panel.shape[0]
            and panel.shape[2] == 16 * BLK == inverse.shape[0]
        )
        return jax.shard_map(
            per_device_grid if fits else per_device_general,
            mesh=mesh,
            in_specs=in_specs,
            out_specs=out_specs,
            check_vma=False,
        )(inverse, panel, factor_inv, structure)

    return run
```

```python
import jax
import jax.numpy as jnp
from jax import lax
from jax.experimental import pallas as pl
from jax.experimental.pallas import tpu as pltpu
from jax.sharding import PartitionSpec as P

BLK = 256
LANES = 128
ANY = pl.BlockSpec(memory_space=pl.ANY)
VMEM = pl.BlockSpec(memory_space=pltpu.VMEM)
SMEM = pl.BlockSpec(memory_space=pltpu.SMEM)


def spread(value, axis, source):
    kept = jnp.where(lax.axis_index(axis) == source, value, 0).astype(value.dtype)
    return lax.psum(kept, axis)


def block_partial(gathered, inverse, row_inside, col_inside, first_row, row_count):
    local_blocks = inverse.shape[1] // BLK
    running = jnp.zeros((row_count, BLK), jnp.float32)
    for blk_index in range(local_blocks):

        def product(blk_index=blk_index):
            panel_piece = lax.dynamic_slice(
                gathered, (blk_index * BLK, first_row), (BLK, row_count)
            )
            block_z = inverse[:, blk_index * BLK : (blk_index + 1) * BLK]
            return lax.dot_general(
                panel_piece, block_z, (((0,), (1,)), ((), ())), preferred_element_type=jnp.float32
            )

        def skipped():
            return jnp.zeros((row_count, BLK), jnp.float32)

        running = running + lax.cond(row_inside & col_inside[blk_index], product, skipped)
    return -running


def per_device_general(inverse, panel, factor_inv, structure):
    wide_count = lax.axis_size("wide")
    narrow_count = lax.axis_size("narrow")
    nsup_count = panel.shape[0]
    kw_total = panel.shape[2] * wide_count
    kw_local = kw_total // narrow_count
    local_blocks = inverse.shape[1] // BLK
    row_index = lax.axis_index("wide")
    col_first = lax.axis_index("narrow") * local_blocks
    col_ids = col_first + jnp.arange(local_blocks, dtype=jnp.int32)
    row_inside = jnp.any(structure == row_index, axis=1)
    col_inside = jnp.any(structure[:, :, None] == col_ids[None, None, :], axis=1)
    root_index = row_index // local_blocks
    offset = (row_index - root_index * local_blocks) * BLK
    cross_parts = []
    own_parts = []
    for sup_index in range(nsup_count):
        gathered_one = lax.all_gather(panel[sup_index], "wide", axis=1, tiled=True)

        def one_term(first_row, row_count, gathered_one=gathered_one, sup_index=sup_index):
            return block_partial(
                gathered_one,
                inverse,
                row_inside[sup_index],
                col_inside[sup_index],
                first_row,
                row_count,
            )

        cross_parts.append(
            lax.psum_scatter(
                one_term(jnp.int32(0), kw_local * lax.axis_size("narrow")),
                "narrow",
                scatter_dimension=0,
                tiled=True,
            )
        )
        own_parts.append(lax.dynamic_slice_in_dim(gathered_one, offset, BLK, axis=0))
    cross_f = jnp.stack(cross_parts, axis=1)
    own_rows = jnp.stack(own_parts)
    owner_panel = spread(own_rows, "narrow", root_index)
    owner_slice = lax.dynamic_slice_in_dim(
        owner_panel, lax.axis_index("narrow") * kw_local, kw_local, axis=2
    )
    weighted = jnp.einsum("kia,aki->ka", owner_slice.astype(jnp.float32), cross_f)
    linv_part = jnp.sum(jnp.square(factor_inv.astype(jnp.float32)), axis=1)
    variance = lax.psum(linv_part - weighted, "wide")
    return (cross_f.astype(jnp.bfloat16), variance)


X, Y, ZL, ZH = 1, 2, 4, 8
NGRP = 4
MIB = 1024 * 1024


def swap_cores(value, name):
    with jax.named_scope(name):
        return lax.ppermute(value, "narrow", [(0, 1), (1, 0)])


def hop(value, mask, name):
    size = lax.axis_size("wide")
    with jax.named_scope(name):
        return lax.ppermute(value, "wide", [(i, i ^ mask) for i in range(size)])


def after(value, *earlier):
    return lax.optimization_barrier((value, *earlier))[0]


def pick(structure_ref, n, j, first):
    nblocks = structure_ref.shape[1]
    start = jnp.where(n == 0, 0, nblocks - first)
    return structure_ref[n, lax.rem(start + j, nblocks)]


def pack_first(structure, panel, first):
    half_blocks = panel.shape[1] // BLK

    def body(st, panel_ref, out):
        n = lax.axis_index("narrow")
        for j in range(first):
            row = pl.multiple_of(lax.rem(pick(st, n, j, first), half_blocks) * BLK, BLK)
            out[j * BLK : (j + 1) * BLK, :] = panel_ref[n, pl.ds(row, BLK), :]

    return pl.pallas_call(
        body,
        out_shape=jax.ShapeDtypeStruct((first * BLK, panel.shape[2]), panel.dtype),
        in_specs=[SMEM, VMEM],
        out_specs=VMEM,
        compiler_params=pltpu.CompilerParams(vmem_limit_bytes=6 * MIB),
        name="pack_first",
    )(structure, panel)


def pack_rest(structure, panel, other, first):
    nblocks = structure.shape[1]
    half_blocks = panel.shape[1] // BLK

    def body(st, panel_ref, other_ref, out0, out1):
        n = lax.axis_index("narrow")
        for j in range(nblocks - first):
            b = pick(st, n, first + j, first)
            row = pl.multiple_of(lax.rem(b, half_blocks) * BLK, BLK)
            mine = lax.div(b, half_blocks) == n
            rows = slice(j * BLK, (j + 1) * BLK)

            @pl.when(mine)
            def _():
                out0[rows, :] = panel_ref[n, pl.ds(row, BLK), :LANES]
                out1[rows, :] = panel_ref[n, pl.ds(row, BLK), LANES:]

            @pl.when(jnp.logical_not(mine))
            def _():
                out0[rows, :] = other_ref[pl.ds(row, BLK), :LANES]
                out1[rows, :] = other_ref[pl.ds(row, BLK), LANES:]

    shape = jax.ShapeDtypeStruct(((nblocks - first) * BLK, LANES), panel.dtype)
    return pl.pallas_call(
        body,
        out_shape=(shape, shape),
        in_specs=[SMEM, VMEM, VMEM],
        out_specs=[VMEM, VMEM],
        compiler_params=pltpu.CompilerParams(vmem_limit_bytes=8 * MIB),
        name="pack_rest",
    )(structure, panel, other)


def pack_inverse(structure, own, other, first):
    nblocks = structure.shape[1]
    half_blocks = own.shape[2] // BLK

    def body(st, own_ref, oth_ref, out):
        n = lax.axis_index("narrow")
        group = lax.rem(lax.div(lax.axis_index("wide"), Y), NGRP)
        for j in range(nblocks):
            b = pick(st, n, j, first)
            col = pl.multiple_of(lax.rem(b, half_blocks) * BLK, BLK)
            mine = lax.div(b, half_blocks) == n

            def move(source, j=j, col=col):
                for d in range(NGRP):
                    out[d, :, j * BLK : (j + 1) * BLK] = source[
                        lax.bitwise_xor(group, d), :, pl.ds(col, BLK)
                    ]

            pl.when(mine)(lambda move=move: move(own_ref))
            pl.when(jnp.logical_not(mine))(lambda move=move: move(oth_ref))

    return pl.pallas_call(
        body,
        out_shape=jax.ShapeDtypeStruct((NGRP, BLK, nblocks * BLK), own.dtype),
        in_specs=[SMEM, VMEM, VMEM],
        out_specs=VMEM,
        compiler_params=pltpu.CompilerParams(vmem_limit_bytes=18 * MIB),
        name="pack_inverse",
    )(structure, own, other)


def products(structure, sel, firsts, rests, chunk, near=None):
    nblocks = structure.shape[1]
    early = firsts[0].shape[0]
    late = rests[0].shape[0]
    first = early // BLK

    def body(st, sel_ref, f0, f1, r0, r1, *refs):
        d = pl.program_id(0)
        n = lax.axis_index("narrow")
        w = lax.axis_index("wide")
        x = lax.bitwise_and(w, 1)
        mask = lax.rem(d, 2) * Y + lax.div(d, 2) * ZL
        row = lax.bitwise_xor(w, mask)
        pos = jnp.int32(0)
        inside = jnp.int32(0)
        for j in range(nblocks):
            hit = (pick(st, n, j, first) == row).astype(jnp.int32)
            pos = pos + j * hit
            inside = inside + hit

        def compute(out_ref, sum_ref):
            @pl.when(d == 0)
            def _():
                sum_ref[...] = jnp.zeros_like(sum_ref)

            @pl.when(inside == 0)
            def _():
                out_ref[...] = jnp.zeros_like(out_ref)

            @pl.when(inside > 0)
            def _():
                acc = jnp.dot(
                    sel_ref[0, :, :early],
                    jnp.concatenate([f0[...], f1[...]], axis=1),
                    preferred_element_type=jnp.float32,
                ) + jnp.dot(
                    sel_ref[0, :, early:],
                    jnp.concatenate([r0[...], r1[...]], axis=1),
                    preferred_element_type=jnp.float32,
                )
                for dx in range(2):
                    part = acc[:, dx * LANES : (dx + 1) * LANES]
                    slot = lax.bitwise_xor(x, dx)

                    def weigh(rows, part=part, slot=slot):
                        total = jnp.sum(part * rows.astype(jnp.float32), axis=0, keepdims=True)
                        sum_ref[slot] += total

                    @pl.when(pos < first)
                    def _():
                        at = pl.multiple_of(pos * BLK, BLK)
                        weigh((f0, f1)[dx][pl.ds(at, BLK), :])

                    @pl.when(pos >= first)
                    def _():
                        at = pl.multiple_of((pos - first) * BLK, BLK)
                        weigh((r0, r1)[dx][pl.ds(at, BLK), :])

                    out_ref[0, slot] = (-part).T.astype(out_ref.dtype)

        if near is None:
            compute(*refs)
            return
        near_ref, near_sum, kept, sent, kept_sum, sent_sum = refs
        stay = n == lax.div(w, ZH)

        @pl.when(stay)
        def _():
            kept[...] = near_ref[...]
            kept_sum[...] = near_sum[...]
            compute(sent, sent_sum)

        @pl.when(jnp.logical_not(stay))
        def _():
            sent[...] = near_ref[...]
            sent_sum[...] = near_sum[...]
            compute(kept, kept_sum)

    front = pl.BlockSpec((early, LANES), lambda d, st: (0, chunk))
    back = pl.BlockSpec((late, LANES), lambda d, st: (0, 0))
    block = pl.BlockSpec((1, 2, LANES, BLK), lambda d, st: (d, 0, 0, 0))
    total = pl.BlockSpec((2, 1, LANES), lambda d, st: (0, 0, 0))
    outs = [
        jax.ShapeDtypeStruct((NGRP, 2, LANES, BLK), sel.dtype),
        jax.ShapeDtypeStruct((2, 1, LANES), jnp.float32),
    ]
    again = () if near is None else tuple(near)
    return pl.pallas_call(
        body,
        out_shape=outs if near is None else [outs[0], outs[0], outs[1], outs[1]],
        grid_spec=pltpu.PrefetchScalarGridSpec(
            num_scalar_prefetch=1,
            grid=(NGRP,),
            in_specs=[
                pl.BlockSpec((1, BLK, early + late), lambda d, st: (d, 0, 0)),
                front,
                front,
                back,
                back,
            ]
            + [block, total][: len(again)],
            out_specs=[block, total] if near is None else [block, block, total, total],
        ),
        compiler_params=pltpu.CompilerParams(vmem_limit_bytes=14 * MIB),
        cost_estimate=pl.CostEstimate(flops=0, bytes_accessed=0, transcendentals=0),
        name="products",
    )(structure, sel, *firsts, *rests, *again)


def bundle(kept, back):
    def body(kept_ref, back_ref, *outs):
        for d, out in enumerate(outs):
            out[0] = kept_ref[d]
            out[1] = back_ref[d]

    shape = jax.ShapeDtypeStruct((2, *kept.shape[1:]), kept.dtype)
    return pl.pallas_call(
        body,
        out_shape=[shape] * NGRP,
        in_specs=[VMEM, VMEM],
        out_specs=[VMEM] * NGRP,
        compiler_params=pltpu.CompilerParams(vmem_limit_bytes=8 * MIB),
        name="bundle",
    )(kept, back)


def squares(factor_inv):
    sups, rows, cols = factor_inv.shape
    half = cols // 2

    def body(in_ref, out_ref):
        for k in range(sups):
            value = in_ref[k].astype(jnp.float32)
            out_ref[k : k + 1, :] = jnp.sum(value * value, axis=0, keepdims=True)

    return pl.pallas_call(
        body,
        out_shape=jax.ShapeDtypeStruct((sups, cols), jnp.float32),
        grid=(2,),
        in_specs=[pl.BlockSpec((sups, rows, half), lambda c: (0, 0, c))],
        out_specs=pl.BlockSpec((sups, half), lambda c: (0, c)),
        compiler_params=pltpu.CompilerParams(vmem_limit_bytes=8 * MIB),
        name="squares",
    )(factor_inv)


def place_sums(linv, kept, back):
    cols = linv.shape[1]

    def body(linv_ref, kept0, kept1, back0, back1, out):
        n = lax.axis_index("narrow")
        group = lax.rem(lax.div(lax.axis_index("wide"), Y), NGRP)
        out[...] = linv_ref[...]
        for c, (ours, theirs) in enumerate(((kept0, back0), (kept1, back1))):
            for xx in range(2):
                at = pl.multiple_of(group * (cols // NGRP) + (2 * xx + c) * LANES, LANES)
                for k in range(2):
                    value = jnp.where(n == k, ours[xx], theirs[xx])
                    out[k : k + 1, pl.ds(at, LANES)] += value

    return pl.pallas_call(
        body,
        out_shape=jax.ShapeDtypeStruct(linv.shape, jnp.float32),
        in_specs=[VMEM] * 5,
        out_specs=VMEM,
        compiler_params=pltpu.CompilerParams(vmem_limit_bytes=4 * MIB),
        name="place_sums",
    )(linv, *kept, *back)


def assemble(messages, chunk, held):
    tall = 4 * LANES
    rows_total = 2 * 2 * NGRP * tall

    def body(*refs):
        msg_refs = refs[:NGRP]
        out, wide_buf, narrow_buf, sem = refs[-4:]
        n = lax.axis_index("narrow")
        w = lax.axis_index("wide")
        copies = []
        for d in range(NGRP):
            source = lax.bitwise_xor(lax.rem(lax.div(w, Y), NGRP), d)
            for xx in range(2):
                slot = 2 * d + xx
                for k in range(2):
                    which = (n != k).astype(jnp.int32)
                    value = msg_refs[d][which, xx].astype(jnp.float32)
                    for lt in range(2):
                        wide_buf[slot, pl.ds(2 * lt + k, LANES, stride=4), :] = value[
                            :, lt * LANES : (lt + 1) * LANES
                        ]
                narrow_buf[slot] = wide_buf[slot].astype(narrow_buf.dtype)
                row = pl.multiple_of(((source * 2 + xx) * 2 + chunk) * tall, tall)
                copy = pltpu.make_async_copy(
                    narrow_buf.at[slot], out.at[pl.ds(row, tall), :], sem.at[slot]
                )
                copy.start()
                copies.append(copy)
        for copy in copies:
            copy.wait()

    extra = () if held is None else (held,)
    return pl.pallas_call(
        body,
        out_shape=jax.ShapeDtypeStruct((rows_total, LANES), messages[0].dtype),
        in_specs=[VMEM] * NGRP + [ANY] * len(extra),
        out_specs=ANY,
        scratch_shapes=[
            pltpu.VMEM((2 * NGRP, tall, LANES), jnp.float32),
            pltpu.VMEM((2 * NGRP, tall, LANES), messages[0].dtype),
            pltpu.SemaphoreType.DMA((2 * NGRP,)),
        ],
        input_output_aliases={NGRP: 0} if extra else {},
        compiler_params=pltpu.CompilerParams(vmem_limit_bytes=8 * MIB),
        name="assemble",
    )(*messages, *extra)


def per_device_grid(inverse, panel, factor_inv, structure):
    n = lax.axis_index("narrow")
    first = structure.shape[1] - panel.shape[1] // BLK
    size = lax.axis_size("wide")
    groups = [
        [base + spot * Y for spot in range(NGRP)] for base in range(size) if base & (Y | ZL) == 0
    ]
    f_own = pack_first(structure, panel, first)
    other = swap_cores(lax.dynamic_index_in_dim(panel, 1 - n, 0, keepdims=False), "panel_swap")
    r_own = pack_rest(structure, panel, other, first)
    with jax.named_scope("inverse_rows"):
        own = lax.all_gather(inverse, "wide", axis_index_groups=groups)
    linv = squares(factor_inv)
    f_z = hop(f_own, ZH, "first_z")
    f_x = hop(f_own, X, "first_x")
    f_z, f_x, linv, *r_own = lax.optimization_barrier((f_z, f_x, linv, *r_own))
    r_z0 = hop(r_own[0], ZH, "rest0_z")
    f_xz = hop(f_z, X, "first_xz")
    r_x0 = hop(r_own[0], X, "rest0_x")
    r_z0, f_xz, r_x0, own, *r_own = lax.optimization_barrier((r_z0, f_xz, r_x0, own, *r_own))
    r_z1 = hop(r_own[1], ZH, "rest1_z")
    r_xz0 = hop(r_z0, X, "rest0_xz")
    r_x1 = hop(r_own[1], X, "rest1_x")
    sel = pack_inverse(structure, own, swap_cores(own, "inverse_swap"), first)

    def deliver(kept, sent, c):
        messages = bundle(kept, swap_cores(sent, f"cross{c}_swap"))
        return [messages[0]] + [
            hop(messages[d], (d % 2) * Y + (d // 2) * ZL, f"cross{c}_{d}") for d in range(1, NGRP)
        ]

    near = products(structure, sel, (f_own, f_x), (r_own[0], r_x0), 0)
    kept, sent, kept_sum0, sent_sum0 = products(
        structure, sel, (f_z, f_xz), (r_z0, r_xz0), 0, near
    )
    messages = deliver(kept, sent, 0)
    r_xz1 = hop(r_z1, X, "rest1_xz")
    near = products(structure, sel, (f_own, f_x), (r_own[1], r_x1), 1)
    r_xz1, *messages = lax.optimization_barrier((r_xz1, *messages))
    kept, sent, kept_sum1, sent_sum1 = products(
        structure, sel, (f_z, f_xz), (r_z1, r_xz1), 1, near
    )
    held = assemble(messages, 0, None)
    held = assemble(deliver(kept, sent, 1), 1, held)
    half = panel.shape[2] * size // 2
    cross = held.reshape(half, 2, 2, LANES).transpose(0, 2, 1, 3).reshape(half, 2, BLK)
    back = [swap_cores(total, "sums_swap") for total in (sent_sum0, sent_sum1)]
    variance = place_sums(linv, (kept_sum0, kept_sum1), back)
    for mask in (X, ZH, Y, ZL):
        variance = variance + hop(variance, mask, f"variance_{mask}")
    return cross, variance


def solution(mesh):
    in_specs = (P("wide", "narrow"), P(None, "narrow", "wide"), P(None, "wide", "narrow"), P())
    out_specs = (P("narrow", None, "wide"), P(None, "narrow"))

    def run(inverse, panel, factor_inv, structure):
        fits = (
            mesh.shape["wide"] == 16
            and mesh.shape["narrow"] == 2 == panel.shape[0]
            and panel.shape[2] == 16 * BLK == inverse.shape[0]
        )
        return jax.shard_map(
            per_device_grid if fits else per_device_general,
            mesh=mesh,
            in_specs=in_specs,
            out_specs=out_specs,
            check_vma=False,
        )(inverse, panel, factor_inv, structure)

    return run
```

```python
import jax
import jax.numpy as jnp
from jax import lax
from jax.experimental import pallas as pl
from jax.experimental.pallas import tpu as pltpu
from jax.sharding import PartitionSpec as P

BLK = 256
LANES = 128
ANY = pl.BlockSpec(memory_space=pl.ANY)
VMEM = pl.BlockSpec(memory_space=pltpu.VMEM)
SMEM = pl.BlockSpec(memory_space=pltpu.SMEM)


def spread(value, axis, source):
    kept = jnp.where(lax.axis_index(axis) == source, value, 0).astype(value.dtype)
    return lax.psum(kept, axis)


def block_partial(gathered, inverse, row_inside, col_inside, first_row, row_count):
    local_blocks = inverse.shape[1] // BLK
    running = jnp.zeros((row_count, BLK), jnp.float32)
    for blk_index in range(local_blocks):

        def product(blk_index=blk_index):
            panel_piece = lax.dynamic_slice(
                gathered, (blk_index * BLK, first_row), (BLK, row_count)
            )
            block_z = inverse[:, blk_index * BLK : (blk_index + 1) * BLK]
            return lax.dot_general(
                panel_piece, block_z, (((0,), (1,)), ((), ())), preferred_element_type=jnp.float32
            )

        def skipped():
            return jnp.zeros((row_count, BLK), jnp.float32)

        running = running + lax.cond(row_inside & col_inside[blk_index], product, skipped)
    return -running


def per_device_general(inverse, panel, factor_inv, structure):
    wide_count = lax.axis_size("wide")
    narrow_count = lax.axis_size("narrow")
    nsup_count = panel.shape[0]
    kw_total = panel.shape[2] * wide_count
    kw_local = kw_total // narrow_count
    local_blocks = inverse.shape[1] // BLK
    row_index = lax.axis_index("wide")
    col_first = lax.axis_index("narrow") * local_blocks
    col_ids = col_first + jnp.arange(local_blocks, dtype=jnp.int32)
    row_inside = jnp.any(structure == row_index, axis=1)
    col_inside = jnp.any(structure[:, :, None] == col_ids[None, None, :], axis=1)
    root_index = row_index // local_blocks
    offset = (row_index - root_index * local_blocks) * BLK
    cross_parts = []
    own_parts = []
    for sup_index in range(nsup_count):
        gathered_one = lax.all_gather(panel[sup_index], "wide", axis=1, tiled=True)

        def one_term(first_row, row_count, gathered_one=gathered_one, sup_index=sup_index):
            return block_partial(
                gathered_one,
                inverse,
                row_inside[sup_index],
                col_inside[sup_index],
                first_row,
                row_count,
            )

        cross_parts.append(
            lax.psum_scatter(
                one_term(jnp.int32(0), kw_local * lax.axis_size("narrow")),
                "narrow",
                scatter_dimension=0,
                tiled=True,
            )
        )
        own_parts.append(lax.dynamic_slice_in_dim(gathered_one, offset, BLK, axis=0))
    cross_f = jnp.stack(cross_parts, axis=1)
    own_rows = jnp.stack(own_parts)
    owner_panel = spread(own_rows, "narrow", root_index)
    owner_slice = lax.dynamic_slice_in_dim(
        owner_panel, lax.axis_index("narrow") * kw_local, kw_local, axis=2
    )
    weighted = jnp.einsum("kia,aki->ka", owner_slice.astype(jnp.float32), cross_f)
    linv_part = jnp.sum(jnp.square(factor_inv.astype(jnp.float32)), axis=1)
    variance = lax.psum(linv_part - weighted, "wide")
    return (cross_f.astype(jnp.bfloat16), variance)


X, Y, ZL, ZH = 1, 2, 4, 8
NGRP = 4
MIB = 1024 * 1024


def swap_cores(value, name):
    with jax.named_scope(name):
        return lax.ppermute(value, "narrow", [(0, 1), (1, 0)])


def hop(value, mask, name):
    size = lax.axis_size("wide")
    with jax.named_scope(name):
        return lax.ppermute(value, "wide", [(i, i ^ mask) for i in range(size)])


def after(value, *earlier):
    return lax.optimization_barrier((value, *earlier))[0]


def pick(structure_ref, n, j, first):
    nblocks = structure_ref.shape[1]
    start = jnp.where(n == 0, 0, nblocks - first)
    return structure_ref[n, lax.rem(start + j, nblocks)]


def pack_first(structure, panel, first):
    half_blocks = panel.shape[1] // BLK

    def body(st, panel_ref, out):
        n = lax.axis_index("narrow")
        for j in range(first):
            row = pl.multiple_of(lax.rem(pick(st, n, j, first), half_blocks) * BLK, BLK)
            out[j * BLK : (j + 1) * BLK, :] = panel_ref[n, pl.ds(row, BLK), :]

    return pl.pallas_call(
        body,
        out_shape=jax.ShapeDtypeStruct((first * BLK, panel.shape[2]), panel.dtype),
        in_specs=[SMEM, VMEM],
        out_specs=VMEM,
        compiler_params=pltpu.CompilerParams(vmem_limit_bytes=6 * MIB),
        name="pack_first",
    )(structure, panel)


def pack_rest(structure, panel, other, first):
    nblocks = structure.shape[1]
    half_blocks = panel.shape[1] // BLK

    def body(st, panel_ref, other_ref, out0, out1):
        n = lax.axis_index("narrow")
        for j in range(nblocks - first):
            b = pick(st, n, first + j, first)
            row = pl.multiple_of(lax.rem(b, half_blocks) * BLK, BLK)
            mine = lax.div(b, half_blocks) == n
            rows = slice(j * BLK, (j + 1) * BLK)

            @pl.when(mine)
            def _():
                out0[rows, :] = panel_ref[n, pl.ds(row, BLK), :LANES]
                out1[rows, :] = panel_ref[n, pl.ds(row, BLK), LANES:]

            @pl.when(jnp.logical_not(mine))
            def _():
                out0[rows, :] = other_ref[pl.ds(row, BLK), :LANES]
                out1[rows, :] = other_ref[pl.ds(row, BLK), LANES:]

    shape = jax.ShapeDtypeStruct(((nblocks - first) * BLK, LANES), panel.dtype)
    return pl.pallas_call(
        body,
        out_shape=(shape, shape),
        in_specs=[SMEM, VMEM, VMEM],
        out_specs=[VMEM, VMEM],
        compiler_params=pltpu.CompilerParams(vmem_limit_bytes=8 * MIB),
        name="pack_rest",
    )(structure, panel, other)


def pack_inverse(structure, owns, others, first):
    nblocks = structure.shape[1]
    half_blocks = owns[0].shape[1] // BLK

    def body(st, *refs):
        own_refs, oth_refs, out = refs[:NGRP], refs[NGRP : 2 * NGRP], refs[2 * NGRP]
        n = lax.axis_index("narrow")
        for j in range(nblocks):
            b = pick(st, n, j, first)
            col = pl.multiple_of(lax.rem(b, half_blocks) * BLK, BLK)
            mine = lax.div(b, half_blocks) == n

            def move(sources, j=j, col=col):
                for d in range(NGRP):
                    out[d, :, j * BLK : (j + 1) * BLK] = sources[d][:, pl.ds(col, BLK)]

            pl.when(mine)(lambda move=move: move(own_refs))
            pl.when(jnp.logical_not(mine))(lambda move=move: move(oth_refs))

    return pl.pallas_call(
        body,
        out_shape=jax.ShapeDtypeStruct((NGRP, BLK, nblocks * BLK), owns[0].dtype),
        in_specs=[SMEM] + [VMEM] * (2 * NGRP),
        out_specs=VMEM,
        compiler_params=pltpu.CompilerParams(vmem_limit_bytes=18 * MIB),
        name="pack_inverse",
    )(structure, *owns, *others)


def products(structure, sel, firsts, rests, chunk, near=None):
    nblocks = structure.shape[1]
    early = firsts[0].shape[0]
    late = rests[0].shape[0]
    first = early // BLK

    def body(st, sel_ref, f0, f1, r0, r1, *refs):
        d = pl.program_id(0)
        n = lax.axis_index("narrow")
        w = lax.axis_index("wide")
        x = lax.bitwise_and(w, 1)
        mask = lax.rem(d, 2) * Y + lax.div(d, 2) * ZL
        row = lax.bitwise_xor(w, mask)
        pos = jnp.int32(0)
        inside = jnp.int32(0)
        for j in range(nblocks):
            hit = (pick(st, n, j, first) == row).astype(jnp.int32)
            pos = pos + j * hit
            inside = inside + hit

        def compute(out_ref, sum_ref):
            @pl.when(d == 0)
            def _():
                sum_ref[...] = jnp.zeros_like(sum_ref)

            @pl.when(inside == 0)
            def _():
                out_ref[...] = jnp.zeros_like(out_ref)

            @pl.when(inside > 0)
            def _():
                acc = jnp.dot(
                    sel_ref[0, :, :early],
                    jnp.concatenate([f0[...], f1[...]], axis=1),
                    preferred_element_type=jnp.float32,
                ) + jnp.dot(
                    sel_ref[0, :, early:],
                    jnp.concatenate([r0[...], r1[...]], axis=1),
                    preferred_element_type=jnp.float32,
                )
                for dx in range(2):
                    part = acc[:, dx * LANES : (dx + 1) * LANES]
                    slot = lax.bitwise_xor(x, dx)

                    def weigh(rows, part=part, slot=slot):
                        total = jnp.sum(part * rows.astype(jnp.float32), axis=0, keepdims=True)
                        sum_ref[slot] += total

                    @pl.when(pos < first)
                    def _():
                        at = pl.multiple_of(pos * BLK, BLK)
                        weigh((f0, f1)[dx][pl.ds(at, BLK), :])

                    @pl.when(pos >= first)
                    def _():
                        at = pl.multiple_of((pos - first) * BLK, BLK)
                        weigh((r0, r1)[dx][pl.ds(at, BLK), :])

                    out_ref[0, slot] = (-part).T.astype(out_ref.dtype)

        if near is None:
            compute(*refs)
            return
        near_ref, near_sum, kept, sent, kept_sum, sent_sum = refs
        stay = n == lax.div(w, ZH)

        @pl.when(stay)
        def _():
            kept[...] = near_ref[...]
            kept_sum[...] = near_sum[...]
            compute(sent, sent_sum)

        @pl.when(jnp.logical_not(stay))
        def _():
            sent[...] = near_ref[...]
            sent_sum[...] = near_sum[...]
            compute(kept, kept_sum)

    front = pl.BlockSpec((early, LANES), lambda d, st: (0, chunk))
    back = pl.BlockSpec((late, LANES), lambda d, st: (0, 0))
    block = pl.BlockSpec((1, 2, LANES, BLK), lambda d, st: (d, 0, 0, 0))
    total = pl.BlockSpec((2, 1, LANES), lambda d, st: (0, 0, 0))
    outs = [
        jax.ShapeDtypeStruct((NGRP, 2, LANES, BLK), sel.dtype),
        jax.ShapeDtypeStruct((2, 1, LANES), jnp.float32),
    ]
    again = () if near is None else tuple(near)
    return pl.pallas_call(
        body,
        out_shape=outs if near is None else [outs[0], outs[0], outs[1], outs[1]],
        grid_spec=pltpu.PrefetchScalarGridSpec(
            num_scalar_prefetch=1,
            grid=(NGRP,),
            in_specs=[
                pl.BlockSpec((1, BLK, early + late), lambda d, st: (d, 0, 0)),
                front,
                front,
                back,
                back,
            ]
            + [block, total][: len(again)],
            out_specs=[block, total] if near is None else [block, block, total, total],
        ),
        compiler_params=pltpu.CompilerParams(vmem_limit_bytes=14 * MIB),
        cost_estimate=pl.CostEstimate(flops=0, bytes_accessed=0, transcendentals=0),
        name="products",
    )(structure, sel, *firsts, *rests, *again)


def bundle(kept, back):
    def body(kept_ref, back_ref, *outs):
        for d, out in enumerate(outs):
            out[0] = kept_ref[d]
            out[1] = back_ref[d]

    shape = jax.ShapeDtypeStruct((2, *kept.shape[1:]), kept.dtype)
    return pl.pallas_call(
        body,
        out_shape=[shape] * NGRP,
        in_specs=[VMEM, VMEM],
        out_specs=[VMEM] * NGRP,
        compiler_params=pltpu.CompilerParams(vmem_limit_bytes=8 * MIB),
        name="bundle",
    )(kept, back)


def squares(factor_inv):
    sups, rows, cols = factor_inv.shape
    half = cols // 2

    def body(in_ref, out_ref):
        for k in range(sups):
            value = in_ref[k].astype(jnp.float32)
            out_ref[k : k + 1, :] = jnp.sum(value * value, axis=0, keepdims=True)

    return pl.pallas_call(
        body,
        out_shape=jax.ShapeDtypeStruct((sups, cols), jnp.float32),
        grid=(2,),
        in_specs=[pl.BlockSpec((sups, rows, half), lambda c: (0, 0, c))],
        out_specs=pl.BlockSpec((sups, half), lambda c: (0, c)),
        compiler_params=pltpu.CompilerParams(vmem_limit_bytes=8 * MIB),
        name="squares",
    )(factor_inv)


def place_sums(linv, kept, back):
    cols = linv.shape[1]

    def body(linv_ref, kept0, kept1, back0, back1, out):
        n = lax.axis_index("narrow")
        group = lax.rem(lax.div(lax.axis_index("wide"), Y), NGRP)
        out[...] = linv_ref[...]
        for c, (ours, theirs) in enumerate(((kept0, back0), (kept1, back1))):
            for xx in range(2):
                at = pl.multiple_of(group * (cols // NGRP) + (2 * xx + c) * LANES, LANES)
                for k in range(2):
                    value = jnp.where(n == k, ours[xx], theirs[xx])
                    out[k : k + 1, pl.ds(at, LANES)] += value

    return pl.pallas_call(
        body,
        out_shape=jax.ShapeDtypeStruct(linv.shape, jnp.float32),
        in_specs=[VMEM] * 5,
        out_specs=VMEM,
        compiler_params=pltpu.CompilerParams(vmem_limit_bytes=4 * MIB),
        name="place_sums",
    )(linv, *kept, *back)


def assemble(messages, chunk, held):
    tall = 4 * LANES
    rows_total = 2 * 2 * NGRP * tall

    def body(*refs):
        msg_refs = refs[:NGRP]
        out, wide_buf, narrow_buf, sem = refs[-4:]
        n = lax.axis_index("narrow")
        w = lax.axis_index("wide")
        copies = []
        for d in range(NGRP):
            source = lax.bitwise_xor(lax.rem(lax.div(w, Y), NGRP), d)
            for xx in range(2):
                slot = 2 * d + xx
                for k in range(2):
                    which = (n != k).astype(jnp.int32)
                    value = msg_refs[d][which, xx].astype(jnp.float32)
                    for lt in range(2):
                        wide_buf[slot, pl.ds(2 * lt + k, LANES, stride=4), :] = value[
                            :, lt * LANES : (lt + 1) * LANES
                        ]
                narrow_buf[slot] = wide_buf[slot].astype(narrow_buf.dtype)
                row = pl.multiple_of(((source * 2 + xx) * 2 + chunk) * tall, tall)
                copy = pltpu.make_async_copy(
                    narrow_buf.at[slot], out.at[pl.ds(row, tall), :], sem.at[slot]
                )
                copy.start()
                copies.append(copy)
        for copy in copies:
            copy.wait()

    extra = () if held is None else (held,)
    return pl.pallas_call(
        body,
        out_shape=jax.ShapeDtypeStruct((rows_total, LANES), messages[0].dtype),
        in_specs=[VMEM] * NGRP + [ANY] * len(extra),
        out_specs=ANY,
        scratch_shapes=[
            pltpu.VMEM((2 * NGRP, tall, LANES), jnp.float32),
            pltpu.VMEM((2 * NGRP, tall, LANES), messages[0].dtype),
            pltpu.SemaphoreType.DMA((2 * NGRP,)),
        ],
        input_output_aliases={NGRP: 0} if extra else {},
        compiler_params=pltpu.CompilerParams(vmem_limit_bytes=8 * MIB),
        name="assemble",
    )(*messages, *extra)


def per_device_grid(inverse, panel, factor_inv, structure):
    n = lax.axis_index("narrow")
    first = structure.shape[1] - panel.shape[1] // BLK
    size = lax.axis_size("wide")
    f_own = pack_first(structure, panel, first)
    other = swap_cores(lax.dynamic_index_in_dim(panel, 1 - n, 0, keepdims=False), "panel_swap")
    r_own = pack_rest(structure, panel, other, first)
    linv = squares(factor_inv)
    a_z = hop(inverse, ZL, "inv_z")
    a_y = hop(inverse, Y, "inv_y")
    f_z = hop(f_own, ZH, "first_z")
    f_x = hop(f_own, X, "first_x")
    r_x0 = hop(r_own[0], X, "rest0_x")
    a_y, a_z, f_z, f_x, r_x0, linv, *r_own = lax.optimization_barrier(
        (a_y, a_z, f_z, f_x, r_x0, linv, *r_own)
    )
    r_z0 = hop(r_own[0], ZH, "rest0_z")
    f_xz = hop(f_z, X, "first_xz")
    r_x1 = hop(r_own[1], X, "rest1_x")
    a_yz = hop(a_z, Y, "inv_yz")
    s_own = swap_cores(after(inverse, a_y), "inv_swap")
    r_z0, f_xz, r_x1, a_yz, a_y, a_z, s_own, *r_own = lax.optimization_barrier(
        (r_z0, f_xz, r_x1, a_yz, a_y, a_z, s_own, *r_own)
    )
    r_z1 = hop(r_own[1], ZH, "rest1_z")
    r_xz0 = hop(r_z0, X, "rest0_xz")
    owns = [inverse, a_y, a_z, a_yz]
    others = [s_own] + [swap_cores(a, "inv_swap") for a in owns[1:]]
    sel = pack_inverse(structure, owns, others, first)

    def deliver(kept, sent, c):
        messages = bundle(kept, swap_cores(sent, f"cross{c}_swap"))
        return [messages[0]] + [
            hop(messages[d], (d % 2) * Y + (d // 2) * ZL, f"cross{c}_{d}") for d in range(1, NGRP)
        ]

    near = products(structure, sel, (f_own, f_x), (r_own[0], r_x0), 0)
    kept, sent, kept_sum0, sent_sum0 = products(
        structure, sel, (f_z, f_xz), (r_z0, r_xz0), 0, near
    )
    messages = deliver(kept, sent, 0)
    r_xz1 = hop(r_z1, X, "rest1_xz")
    near = products(structure, sel, (f_own, f_x), (r_own[1], r_x1), 1)
    r_xz1, *messages = lax.optimization_barrier((r_xz1, *messages))
    kept, sent, kept_sum1, sent_sum1 = products(
        structure, sel, (f_z, f_xz), (r_z1, r_xz1), 1, near
    )
    held = assemble(messages, 0, None)
    back = [swap_cores(total, "sums_swap") for total in (sent_sum0, sent_sum1)]
    variance = place_sums(linv, (kept_sum0, kept_sum1), back)
    for group in ((X, ZH, X | ZH), (Y, ZL, Y | ZL)):
        variance = sum((hop(variance, mask, f"variance_{mask}") for mask in group), variance)
    held = assemble(deliver(kept, sent, 1), 1, held)
    half = panel.shape[2] * size // 2
    cross = held.reshape(half, 2, 2, LANES).transpose(0, 2, 1, 3).reshape(half, 2, BLK)
    return cross, variance


def solution(mesh):
    in_specs = (P("wide", "narrow"), P(None, "narrow", "wide"), P(None, "wide", "narrow"), P())
    out_specs = (P("narrow", None, "wide"), P(None, "narrow"))

    def run(inverse, panel, factor_inv, structure):
        fits = (
            mesh.shape["wide"] == 16
            and mesh.shape["narrow"] == 2 == panel.shape[0]
            and panel.shape[2] == 16 * BLK == inverse.shape[0]
        )
        return jax.shard_map(
            per_device_grid if fits else per_device_general,
            mesh=mesh,
            in_specs=in_specs,
            out_specs=out_specs,
            check_vma=False,
        )(inverse, panel, factor_inv, structure)

    return run
```

```python
import jax
import jax.numpy as jnp
from jax import lax
from jax.experimental import pallas as pl
from jax.experimental.pallas import tpu as pltpu
from jax.sharding import PartitionSpec as P

BLK = 256
LANES = 128
ANY = pl.BlockSpec(memory_space=pl.ANY)
VMEM = pl.BlockSpec(memory_space=pltpu.VMEM)
SMEM = pl.BlockSpec(memory_space=pltpu.SMEM)


def spread(value, axis, source):
    kept = jnp.where(lax.axis_index(axis) == source, value, 0).astype(value.dtype)
    return lax.psum(kept, axis)


def block_partial(gathered, inverse, row_inside, col_inside, first_row, row_count):
    local_blocks = inverse.shape[1] // BLK
    running = jnp.zeros((row_count, BLK), jnp.float32)
    for blk_index in range(local_blocks):

        def product(blk_index=blk_index):
            panel_piece = lax.dynamic_slice(
                gathered, (blk_index * BLK, first_row), (BLK, row_count)
            )
            block_z = inverse[:, blk_index * BLK : (blk_index + 1) * BLK]
            return lax.dot_general(
                panel_piece, block_z, (((0,), (1,)), ((), ())), preferred_element_type=jnp.float32
            )

        def skipped():
            return jnp.zeros((row_count, BLK), jnp.float32)

        running = running + lax.cond(row_inside & col_inside[blk_index], product, skipped)
    return -running


def per_device_general(inverse, panel, factor_inv, structure):
    wide_count = lax.axis_size("wide")
    narrow_count = lax.axis_size("narrow")
    nsup_count = panel.shape[0]
    kw_total = panel.shape[2] * wide_count
    kw_local = kw_total // narrow_count
    local_blocks = inverse.shape[1] // BLK
    row_index = lax.axis_index("wide")
    col_first = lax.axis_index("narrow") * local_blocks
    col_ids = col_first + jnp.arange(local_blocks, dtype=jnp.int32)
    row_inside = jnp.any(structure == row_index, axis=1)
    col_inside = jnp.any(structure[:, :, None] == col_ids[None, None, :], axis=1)
    root_index = row_index // local_blocks
    offset = (row_index - root_index * local_blocks) * BLK
    cross_parts = []
    own_parts = []
    for sup_index in range(nsup_count):
        gathered_one = lax.all_gather(panel[sup_index], "wide", axis=1, tiled=True)

        def one_term(first_row, row_count, gathered_one=gathered_one, sup_index=sup_index):
            return block_partial(
                gathered_one,
                inverse,
                row_inside[sup_index],
                col_inside[sup_index],
                first_row,
                row_count,
            )

        cross_parts.append(
            lax.psum_scatter(
                one_term(jnp.int32(0), kw_local * lax.axis_size("narrow")),
                "narrow",
                scatter_dimension=0,
                tiled=True,
            )
        )
        own_parts.append(lax.dynamic_slice_in_dim(gathered_one, offset, BLK, axis=0))
    cross_f = jnp.stack(cross_parts, axis=1)
    own_rows = jnp.stack(own_parts)
    owner_panel = spread(own_rows, "narrow", root_index)
    owner_slice = lax.dynamic_slice_in_dim(
        owner_panel, lax.axis_index("narrow") * kw_local, kw_local, axis=2
    )
    weighted = jnp.einsum("kia,aki->ka", owner_slice.astype(jnp.float32), cross_f)
    linv_part = jnp.sum(jnp.square(factor_inv.astype(jnp.float32)), axis=1)
    variance = lax.psum(linv_part - weighted, "wide")
    return (cross_f.astype(jnp.bfloat16), variance)


X, Y, ZL, ZH = 1, 2, 4, 8
NGRP = 4
MIB = 1024 * 1024


def swap_cores(value, name):
    with jax.named_scope(name):
        return lax.ppermute(value, "narrow", [(0, 1), (1, 0)])


def hop(value, mask, name):
    size = lax.axis_size("wide")
    with jax.named_scope(name):
        return lax.ppermute(value, "wide", [(i, i ^ mask) for i in range(size)])


def after(value, *earlier):
    return lax.optimization_barrier((value, *earlier))[0]


def pick(structure_ref, n, j, first):
    nblocks = structure_ref.shape[1]
    start = jnp.where(n == 0, 0, nblocks - first)
    return structure_ref[n, lax.rem(start + j, nblocks)]


def pack_first(structure, panel, first):
    half_blocks = panel.shape[1] // BLK

    def body(st, panel_ref, out):
        n = lax.axis_index("narrow")
        for j in range(first):
            row = pl.multiple_of(lax.rem(pick(st, n, j, first), half_blocks) * BLK, BLK)
            out[j * BLK : (j + 1) * BLK, :] = panel_ref[n, pl.ds(row, BLK), :]

    return pl.pallas_call(
        body,
        out_shape=jax.ShapeDtypeStruct((first * BLK, panel.shape[2]), panel.dtype),
        in_specs=[SMEM, VMEM],
        out_specs=VMEM,
        compiler_params=pltpu.CompilerParams(vmem_limit_bytes=6 * MIB),
        name="pack_first",
    )(structure, panel)


def pack_rest(structure, panel, other, first):
    nblocks = structure.shape[1]
    half_blocks = panel.shape[1] // BLK

    def body(st, panel_ref, other_ref, out0, out1):
        n = lax.axis_index("narrow")
        for j in range(nblocks - first):
            b = pick(st, n, first + j, first)
            row = pl.multiple_of(lax.rem(b, half_blocks) * BLK, BLK)
            mine = lax.div(b, half_blocks) == n
            rows = slice(j * BLK, (j + 1) * BLK)

            @pl.when(mine)
            def _():
                out0[rows, :] = panel_ref[n, pl.ds(row, BLK), :LANES]
                out1[rows, :] = panel_ref[n, pl.ds(row, BLK), LANES:]

            @pl.when(jnp.logical_not(mine))
            def _():
                out0[rows, :] = other_ref[pl.ds(row, BLK), :LANES]
                out1[rows, :] = other_ref[pl.ds(row, BLK), LANES:]

    shape = jax.ShapeDtypeStruct(((nblocks - first) * BLK, LANES), panel.dtype)
    return pl.pallas_call(
        body,
        out_shape=(shape, shape),
        in_specs=[SMEM, VMEM, VMEM],
        out_specs=[VMEM, VMEM],
        compiler_params=pltpu.CompilerParams(vmem_limit_bytes=8 * MIB),
        name="pack_rest",
    )(structure, panel, other)


def pack_inverse(structure, owns, others, first):
    nblocks = structure.shape[1]
    half_blocks = owns[0].shape[1] // BLK

    def body(st, *refs):
        own_refs, oth_refs, out = refs[:NGRP], refs[NGRP : 2 * NGRP], refs[2 * NGRP]
        n = lax.axis_index("narrow")
        for j in range(nblocks):
            b = pick(st, n, j, first)
            col = pl.multiple_of(lax.rem(b, half_blocks) * BLK, BLK)
            mine = lax.div(b, half_blocks) == n

            def move(sources, j=j, col=col):
                for d in range(NGRP):
                    out[d, :, j * BLK : (j + 1) * BLK] = sources[d][:, pl.ds(col, BLK)]

            pl.when(mine)(lambda move=move: move(own_refs))
            pl.when(jnp.logical_not(mine))(lambda move=move: move(oth_refs))

    return pl.pallas_call(
        body,
        out_shape=jax.ShapeDtypeStruct((NGRP, BLK, nblocks * BLK), owns[0].dtype),
        in_specs=[SMEM] + [VMEM] * (2 * NGRP),
        out_specs=VMEM,
        compiler_params=pltpu.CompilerParams(vmem_limit_bytes=18 * MIB),
        name="pack_inverse",
    )(structure, *owns, *others)


def products(structure, sel, firsts, rests, chunk, near=None):
    nblocks = structure.shape[1]
    early = firsts[0].shape[0]
    late = rests[0].shape[0]
    first = early // BLK

    def body(st, sel_ref, f0, f1, r0, r1, *refs):
        d = pl.program_id(0)
        n = lax.axis_index("narrow")
        w = lax.axis_index("wide")
        x = lax.bitwise_and(w, 1)
        mask = lax.rem(d, 2) * Y + lax.div(d, 2) * ZL
        row = lax.bitwise_xor(w, mask)
        pos = jnp.int32(0)
        inside = jnp.int32(0)
        for j in range(nblocks):
            hit = (pick(st, n, j, first) == row).astype(jnp.int32)
            pos = pos + j * hit
            inside = inside + hit

        def compute(out_ref, sum_ref):
            @pl.when(d == 0)
            def _():
                sum_ref[...] = jnp.zeros_like(sum_ref)

            @pl.when(inside == 0)
            def _():
                out_ref[...] = jnp.zeros_like(out_ref)

            @pl.when(inside > 0)
            def _():
                acc = jnp.dot(
                    sel_ref[0, :, :early],
                    jnp.concatenate([f0[...], f1[...]], axis=1),
                    preferred_element_type=jnp.float32,
                ) + jnp.dot(
                    sel_ref[0, :, early:],
                    jnp.concatenate([r0[...], r1[...]], axis=1),
                    preferred_element_type=jnp.float32,
                )
                for dx in range(2):
                    part = acc[:, dx * LANES : (dx + 1) * LANES]
                    slot = lax.bitwise_xor(x, dx)

                    def weigh(rows, part=part, slot=slot):
                        total = jnp.sum(part * rows.astype(jnp.float32), axis=0, keepdims=True)
                        sum_ref[slot] += total

                    @pl.when(pos < first)
                    def _():
                        at = pl.multiple_of(pos * BLK, BLK)
                        weigh((f0, f1)[dx][pl.ds(at, BLK), :])

                    @pl.when(pos >= first)
                    def _():
                        at = pl.multiple_of((pos - first) * BLK, BLK)
                        weigh((r0, r1)[dx][pl.ds(at, BLK), :])

                    out_ref[0, slot] = (-part).T.astype(out_ref.dtype)

        if near is None:
            compute(*refs)
            return
        near_ref, near_sum, kept, sent, kept_sum, sent_sum = refs
        stay = n == lax.div(w, ZH)

        @pl.when(stay)
        def _():
            kept[...] = near_ref[...]
            kept_sum[...] = near_sum[...]
            compute(sent, sent_sum)

        @pl.when(jnp.logical_not(stay))
        def _():
            sent[...] = near_ref[...]
            sent_sum[...] = near_sum[...]
            compute(kept, kept_sum)

    front = pl.BlockSpec((early, LANES), lambda d, st: (0, chunk))
    back = pl.BlockSpec((late, LANES), lambda d, st: (0, 0))
    block = pl.BlockSpec((1, 2, LANES, BLK), lambda d, st: (d, 0, 0, 0))
    total = pl.BlockSpec((2, 1, LANES), lambda d, st: (0, 0, 0))
    outs = [
        jax.ShapeDtypeStruct((NGRP, 2, LANES, BLK), sel.dtype),
        jax.ShapeDtypeStruct((2, 1, LANES), jnp.float32),
    ]
    again = () if near is None else tuple(near)
    return pl.pallas_call(
        body,
        out_shape=outs if near is None else [outs[0], outs[0], outs[1], outs[1]],
        grid_spec=pltpu.PrefetchScalarGridSpec(
            num_scalar_prefetch=1,
            grid=(NGRP,),
            in_specs=[
                pl.BlockSpec((1, BLK, early + late), lambda d, st: (d, 0, 0)),
                front,
                front,
                back,
                back,
            ]
            + [block, total][: len(again)],
            out_specs=[block, total] if near is None else [block, block, total, total],
        ),
        compiler_params=pltpu.CompilerParams(vmem_limit_bytes=14 * MIB),
        cost_estimate=pl.CostEstimate(flops=0, bytes_accessed=0, transcendentals=0),
        name="products",
    )(structure, sel, *firsts, *rests, *again)


def bundle(kept, back):
    def body(kept_ref, back_ref, *outs):
        for d, out in enumerate(outs):
            out[0] = kept_ref[d]
            out[1] = back_ref[d]

    shape = jax.ShapeDtypeStruct((2, *kept.shape[1:]), kept.dtype)
    return pl.pallas_call(
        body,
        out_shape=[shape] * NGRP,
        in_specs=[VMEM, VMEM],
        out_specs=[VMEM] * NGRP,
        compiler_params=pltpu.CompilerParams(vmem_limit_bytes=8 * MIB),
        name="bundle",
    )(kept, back)


def squares(factor_inv):
    sups, rows, cols = factor_inv.shape
    half = cols // 2

    def body(in_ref, out_ref):
        for k in range(sups):
            value = in_ref[k].astype(jnp.float32)
            out_ref[k : k + 1, :] = jnp.sum(value * value, axis=0, keepdims=True)

    return pl.pallas_call(
        body,
        out_shape=jax.ShapeDtypeStruct((sups, cols), jnp.float32),
        grid=(2,),
        in_specs=[pl.BlockSpec((sups, rows, half), lambda c: (0, 0, c))],
        out_specs=pl.BlockSpec((sups, half), lambda c: (0, c)),
        compiler_params=pltpu.CompilerParams(vmem_limit_bytes=8 * MIB),
        name="squares",
    )(factor_inv)


def place_sums(linv, kept, back):
    cols = linv.shape[1]

    def body(linv_ref, kept0, kept1, back0, back1, out):
        n = lax.axis_index("narrow")
        group = lax.rem(lax.div(lax.axis_index("wide"), Y), NGRP)
        out[...] = linv_ref[...]
        for c, (ours, theirs) in enumerate(((kept0, back0), (kept1, back1))):
            for xx in range(2):
                at = pl.multiple_of(group * (cols // NGRP) + (2 * xx + c) * LANES, LANES)
                for k in range(2):
                    value = jnp.where(n == k, ours[xx], theirs[xx])
                    out[k : k + 1, pl.ds(at, LANES)] += value

    return pl.pallas_call(
        body,
        out_shape=jax.ShapeDtypeStruct(linv.shape, jnp.float32),
        in_specs=[VMEM] * 5,
        out_specs=VMEM,
        compiler_params=pltpu.CompilerParams(vmem_limit_bytes=4 * MIB),
        name="place_sums",
    )(linv, *kept, *back)


def assemble(messages, chunk, held):
    tall = 4 * LANES
    rows_total = 2 * 2 * NGRP * tall

    def body(*refs):
        msg_refs = refs[:NGRP]
        out, wide_buf, narrow_buf, sem = refs[-4:]
        n = lax.axis_index("narrow")
        w = lax.axis_index("wide")
        copies = []
        for d in range(NGRP):
            source = lax.bitwise_xor(lax.rem(lax.div(w, Y), NGRP), d)
            for xx in range(2):
                slot = 2 * d + xx
                for k in range(2):
                    which = (n != k).astype(jnp.int32)
                    value = msg_refs[d][which, xx].astype(jnp.float32)
                    for lt in range(2):
                        wide_buf[slot, pl.ds(2 * lt + k, LANES, stride=4), :] = value[
                            :, lt * LANES : (lt + 1) * LANES
                        ]
                narrow_buf[slot] = wide_buf[slot].astype(narrow_buf.dtype)
                row = pl.multiple_of(((source * 2 + xx) * 2 + chunk) * tall, tall)
                copy = pltpu.make_async_copy(
                    narrow_buf.at[slot], out.at[pl.ds(row, tall), :], sem.at[slot]
                )
                copy.start()
                copies.append(copy)
        for copy in copies:
            copy.wait()

    extra = () if held is None else (held,)
    return pl.pallas_call(
        body,
        out_shape=jax.ShapeDtypeStruct((rows_total, LANES), messages[0].dtype),
        in_specs=[VMEM] * NGRP + [ANY] * len(extra),
        out_specs=ANY,
        scratch_shapes=[
            pltpu.VMEM((2 * NGRP, tall, LANES), jnp.float32),
            pltpu.VMEM((2 * NGRP, tall, LANES), messages[0].dtype),
            pltpu.SemaphoreType.DMA((2 * NGRP,)),
        ],
        input_output_aliases={NGRP: 0} if extra else {},
        compiler_params=pltpu.CompilerParams(vmem_limit_bytes=8 * MIB),
        name="assemble",
    )(*messages, *extra)


def per_device_grid(inverse, panel, factor_inv, structure):
    n = lax.axis_index("narrow")
    first = structure.shape[1] - panel.shape[1] // BLK
    size = lax.axis_size("wide")
    f_own = pack_first(structure, panel, first)
    other = swap_cores(lax.dynamic_index_in_dim(panel, 1 - n, 0, keepdims=False), "panel_swap")
    r_own = pack_rest(structure, panel, other, first)
    linv = squares(factor_inv)
    a_z = hop(inverse, ZL, "inv_z")
    a_y = hop(inverse, Y, "inv_y")
    f_z = hop(f_own, ZH, "first_z")
    f_x = hop(f_own, X, "first_x")
    r_x0 = hop(r_own[0], X, "rest0_x")
    a_y, a_z, f_z, f_x, r_x0, linv, *r_own = lax.optimization_barrier(
        (a_y, a_z, f_z, f_x, r_x0, linv, *r_own)
    )
    r_z0 = hop(r_own[0], ZH, "rest0_z")
    f_xz = hop(f_z, X, "first_xz")
    r_x1 = hop(r_own[1], X, "rest1_x")
    a_yz = hop(a_z, Y, "inv_yz")
    s_own = swap_cores(after(inverse, a_y), "inv_swap")
    r_z0, f_xz, r_x1, a_yz, a_y, a_z, s_own, *r_own = lax.optimization_barrier(
        (r_z0, f_xz, r_x1, a_yz, a_y, a_z, s_own, *r_own)
    )
    r_z1 = hop(r_own[1], ZH, "rest1_z")
    r_xz0 = hop(r_z0, X, "rest0_xz")
    owns = [inverse, a_y, a_z, a_yz]
    others = [s_own] + [swap_cores(a, "inv_swap") for a in owns[1:]]
    sel = pack_inverse(structure, owns, others, first)

    def deliver(kept, sent, c):
        messages = bundle(kept, swap_cores(sent, f"cross{c}_swap"))
        return [messages[0]] + [
            hop(messages[d], (d % 2) * Y + (d // 2) * ZL, f"cross{c}_{d}") for d in range(1, NGRP)
        ]

    near = products(structure, sel, (f_own, f_x), (r_own[0], r_x0), 0)
    kept, sent, kept_sum0, sent_sum0 = products(
        structure, sel, (f_z, f_xz), (r_z0, r_xz0), 0, near
    )
    messages = deliver(kept, sent, 0)
    r_xz1 = hop(r_z1, X, "rest1_xz")
    near = products(structure, sel, (f_own, f_x), (r_own[1], r_x1), 1)
    r_xz1, *messages = lax.optimization_barrier((r_xz1, *messages))
    kept, sent, kept_sum1, sent_sum1 = products(
        structure, sel, (f_z, f_xz), (r_z1, r_xz1), 1, near
    )
    held = assemble(messages, 0, None)
    messages = deliver(kept, sent, 1)
    back = [
        swap_cores(after(total, messages[0]), "sums_swap") for total in (sent_sum0, sent_sum1)
    ]
    held = assemble(messages, 1, held)
    variance = place_sums(linv, (kept_sum0, kept_sum1), back)
    for mask in (X, ZH, Y, ZL):
        variance = variance + hop(variance, mask, f"variance_{mask}")
    half = panel.shape[2] * size // 2
    cross = held.reshape(half, 2, 2, LANES).transpose(0, 2, 1, 3).reshape(half, 2, BLK)
    return cross, variance


def solution(mesh):
    in_specs = (P("wide", "narrow"), P(None, "narrow", "wide"), P(None, "wide", "narrow"), P())
    out_specs = (P("narrow", None, "wide"), P(None, "narrow"))

    def run(inverse, panel, factor_inv, structure):
        fits = (
            mesh.shape["wide"] == 16
            and mesh.shape["narrow"] == 2 == panel.shape[0]
            and panel.shape[2] == 16 * BLK == inverse.shape[0]
        )
        return jax.shard_map(
            per_device_grid if fits else per_device_general,
            mesh=mesh,
            in_specs=in_specs,
            out_specs=out_specs,
            check_vma=False,
        )(inverse, panel, factor_inv, structure)

    return run
```

```python
import jax
import jax.numpy as jnp
from jax import lax
from jax.experimental import pallas as pl
from jax.experimental.pallas import tpu as pltpu
from jax.sharding import PartitionSpec as P

BLK = 256
LANES = 128
ANY = pl.BlockSpec(memory_space=pl.ANY)
VMEM = pl.BlockSpec(memory_space=pltpu.VMEM)
SMEM = pl.BlockSpec(memory_space=pltpu.SMEM)


def spread(value, axis, source):
    kept = jnp.where(lax.axis_index(axis) == source, value, 0).astype(value.dtype)
    return lax.psum(kept, axis)


def block_partial(gathered, inverse, row_inside, col_inside, first_row, row_count):
    local_blocks = inverse.shape[1] // BLK
    running = jnp.zeros((row_count, BLK), jnp.float32)
    for blk_index in range(local_blocks):

        def product(blk_index=blk_index):
            panel_piece = lax.dynamic_slice(
                gathered, (blk_index * BLK, first_row), (BLK, row_count)
            )
            block_z = inverse[:, blk_index * BLK : (blk_index + 1) * BLK]
            return lax.dot_general(
                panel_piece, block_z, (((0,), (1,)), ((), ())), preferred_element_type=jnp.float32
            )

        def skipped():
            return jnp.zeros((row_count, BLK), jnp.float32)

        running = running + lax.cond(row_inside & col_inside[blk_index], product, skipped)
    return -running


def per_device_general(inverse, panel, factor_inv, structure):
    wide_count = lax.axis_size("wide")
    narrow_count = lax.axis_size("narrow")
    nsup_count = panel.shape[0]
    kw_total = panel.shape[2] * wide_count
    kw_local = kw_total // narrow_count
    local_blocks = inverse.shape[1] // BLK
    row_index = lax.axis_index("wide")
    col_first = lax.axis_index("narrow") * local_blocks
    col_ids = col_first + jnp.arange(local_blocks, dtype=jnp.int32)
    row_inside = jnp.any(structure == row_index, axis=1)
    col_inside = jnp.any(structure[:, :, None] == col_ids[None, None, :], axis=1)
    root_index = row_index // local_blocks
    offset = (row_index - root_index * local_blocks) * BLK
    cross_parts = []
    own_parts = []
    for sup_index in range(nsup_count):
        gathered_one = lax.all_gather(panel[sup_index], "wide", axis=1, tiled=True)

        def one_term(first_row, row_count, gathered_one=gathered_one, sup_index=sup_index):
            return block_partial(
                gathered_one,
                inverse,
                row_inside[sup_index],
                col_inside[sup_index],
                first_row,
                row_count,
            )

        cross_parts.append(
            lax.psum_scatter(
                one_term(jnp.int32(0), kw_local * lax.axis_size("narrow")),
                "narrow",
                scatter_dimension=0,
                tiled=True,
            )
        )
        own_parts.append(lax.dynamic_slice_in_dim(gathered_one, offset, BLK, axis=0))
    cross_f = jnp.stack(cross_parts, axis=1)
    own_rows = jnp.stack(own_parts)
    owner_panel = spread(own_rows, "narrow", root_index)
    owner_slice = lax.dynamic_slice_in_dim(
        owner_panel, lax.axis_index("narrow") * kw_local, kw_local, axis=2
    )
    weighted = jnp.einsum("kia,aki->ka", owner_slice.astype(jnp.float32), cross_f)
    linv_part = jnp.sum(jnp.square(factor_inv.astype(jnp.float32)), axis=1)
    variance = lax.psum(linv_part - weighted, "wide")
    return (cross_f.astype(jnp.bfloat16), variance)


X, Y, ZL, ZH = 1, 2, 4, 8
NGRP = 4
SPLIT = 192
MIB = 1024 * 1024


def swap_cores(value, name):
    with jax.named_scope(name):
        return lax.ppermute(value, "narrow", [(0, 1), (1, 0)])


def hop(value, mask, name):
    size = lax.axis_size("wide")
    with jax.named_scope(name):
        return lax.ppermute(value, "wide", [(i, i ^ mask) for i in range(size)])


def after(value, *earlier):
    return lax.optimization_barrier((value, *earlier))[0]


def pick(structure_ref, n, j, first):
    nblocks = structure_ref.shape[1]
    start = jnp.where(n == 0, 0, nblocks - first)
    return structure_ref[n, lax.rem(start + j, nblocks)]


def pack_first(structure, panel, inverse, first):
    half_blocks = panel.shape[1] // BLK

    def body(st, panel_ref, inv_ref, out, *pieces):
        n = lax.axis_index("narrow")
        for j in range(first):
            row = pl.multiple_of(lax.rem(pick(st, n, j, first), half_blocks) * BLK, BLK)
            out[j * BLK : (j + 1) * BLK, :] = panel_ref[n, pl.ds(row, BLK), :]
        pieces[0][...] = inv_ref[:SPLIT, :]
        pieces[1][...] = inv_ref[SPLIT:, :]

    width = inverse.shape[1]
    return pl.pallas_call(
        body,
        out_shape=[
            jax.ShapeDtypeStruct((first * BLK, panel.shape[2]), panel.dtype),
            jax.ShapeDtypeStruct((SPLIT, width), inverse.dtype),
            jax.ShapeDtypeStruct((BLK - SPLIT, width), inverse.dtype),
        ],
        in_specs=[SMEM, VMEM, VMEM],
        out_specs=[VMEM] * 3,
        compiler_params=pltpu.CompilerParams(vmem_limit_bytes=8 * MIB),
        name="pack_first",
    )(structure, panel, inverse)


def pack_rest(structure, panel, other, first):
    nblocks = structure.shape[1]
    half_blocks = panel.shape[1] // BLK

    def body(st, panel_ref, other_ref, out0, out1):
        n = lax.axis_index("narrow")
        for j in range(nblocks - first):
            b = pick(st, n, first + j, first)
            row = pl.multiple_of(lax.rem(b, half_blocks) * BLK, BLK)
            mine = lax.div(b, half_blocks) == n
            rows = slice(j * BLK, (j + 1) * BLK)

            @pl.when(mine)
            def _():
                out0[rows, :] = panel_ref[n, pl.ds(row, BLK), :LANES]
                out1[rows, :] = panel_ref[n, pl.ds(row, BLK), LANES:]

            @pl.when(jnp.logical_not(mine))
            def _():
                out0[rows, :] = other_ref[pl.ds(row, BLK), :LANES]
                out1[rows, :] = other_ref[pl.ds(row, BLK), LANES:]

    shape = jax.ShapeDtypeStruct(((nblocks - first) * BLK, LANES), panel.dtype)
    return pl.pallas_call(
        body,
        out_shape=(shape, shape),
        in_specs=[SMEM, VMEM, VMEM],
        out_specs=[VMEM, VMEM],
        compiler_params=pltpu.CompilerParams(vmem_limit_bytes=8 * MIB),
        name="pack_rest",
    )(structure, panel, other)


def stack_rows(pieces):
    rows = sum(piece.shape[0] for piece in pieces)

    def body(*refs):
        at = 0
        for ref in refs[:-1]:
            refs[-1][at : at + ref.shape[0], :] = ref[...]
            at += ref.shape[0]

    return pl.pallas_call(
        body,
        out_shape=jax.ShapeDtypeStruct((rows, pieces[0].shape[1]), pieces[0].dtype),
        in_specs=[VMEM] * len(pieces),
        out_specs=VMEM,
        compiler_params=pltpu.CompilerParams(vmem_limit_bytes=8 * MIB),
        name="stack_rows",
    )(*pieces)


def pack_inverse(structure, owns, others, first):
    nblocks = structure.shape[1]
    half_blocks = owns[0].shape[1] // BLK
    count = len(owns)
    runs, row = [], 0
    for p, own in enumerate(owns):
        at = 0
        while at < own.shape[0]:
            rows = min(own.shape[0] - at, BLK - row % BLK)
            runs.append((p, at, row // BLK, row % BLK, rows))
            at, row = at + rows, row + rows

    def body(st, *refs):
        out = refs[2 * count]
        n = lax.axis_index("narrow")
        for j in range(nblocks):
            b = pick(st, n, j, first)
            col = pl.multiple_of(lax.rem(b, half_blocks) * BLK, BLK)
            mine = lax.div(b, half_blocks) == n

            def move(sources, j=j, col=col):
                for p, at, d, top, rows in runs:
                    out[d, top : top + rows, j * BLK : (j + 1) * BLK] = sources[p][
                        at : at + rows, pl.ds(col, BLK)
                    ]

            pl.when(mine)(lambda move=move: move(refs[:count]))
            pl.when(jnp.logical_not(mine))(lambda move=move: move(refs[count : 2 * count]))

    return pl.pallas_call(
        body,
        out_shape=jax.ShapeDtypeStruct((NGRP, BLK, nblocks * BLK), owns[0].dtype),
        in_specs=[SMEM] + [VMEM] * (2 * count),
        out_specs=VMEM,
        compiler_params=pltpu.CompilerParams(vmem_limit_bytes=18 * MIB),
        name="pack_inverse",
    )(structure, *owns, *others)


def products(structure, sel, firsts, rests, chunk, near=None):
    nblocks = structure.shape[1]
    early = firsts[0].shape[0]
    late = rests[0].shape[0]
    first = early // BLK

    def body(st, sel_ref, f0, f1, r0, r1, *refs):
        d = pl.program_id(0)
        n = lax.axis_index("narrow")
        w = lax.axis_index("wide")
        x = lax.bitwise_and(w, 1)
        mask = lax.rem(d, 2) * Y + lax.div(d, 2) * ZL
        row = lax.bitwise_xor(w, mask)
        pos = jnp.int32(0)
        inside = jnp.int32(0)
        for j in range(nblocks):
            hit = (pick(st, n, j, first) == row).astype(jnp.int32)
            pos = pos + j * hit
            inside = inside + hit

        def compute(out_ref, sum_ref):
            @pl.when(d == 0)
            def _():
                sum_ref[...] = jnp.zeros_like(sum_ref)

            @pl.when(inside == 0)
            def _():
                out_ref[...] = jnp.zeros_like(out_ref)

            @pl.when(inside > 0)
            def _():
                acc = jnp.dot(
                    sel_ref[0, :, :early],
                    jnp.concatenate([f0[...], f1[...]], axis=1),
                    preferred_element_type=jnp.float32,
                ) + jnp.dot(
                    sel_ref[0, :, early:],
                    jnp.concatenate([r0[...], r1[...]], axis=1),
                    preferred_element_type=jnp.float32,
                )
                for dx in range(2):
                    part = acc[:, dx * LANES : (dx + 1) * LANES]
                    slot = lax.bitwise_xor(x, dx)

                    def weigh(rows, part=part, slot=slot):
                        total = jnp.sum(part * rows.astype(jnp.float32), axis=0, keepdims=True)
                        sum_ref[slot] += total

                    @pl.when(pos < first)
                    def _():
                        at = pl.multiple_of(pos * BLK, BLK)
                        weigh((f0, f1)[dx][pl.ds(at, BLK), :])

                    @pl.when(pos >= first)
                    def _():
                        at = pl.multiple_of((pos - first) * BLK, BLK)
                        weigh((r0, r1)[dx][pl.ds(at, BLK), :])

                    out_ref[0, slot] = (-part).T.astype(out_ref.dtype)

        if near is None:
            compute(*refs)
            return
        near_ref, near_sum, kept, sent, kept_sum, sent_sum = refs
        stay = n == lax.div(w, ZH)

        @pl.when(stay)
        def _():
            kept[...] = near_ref[...]
            kept_sum[...] = near_sum[...]
            compute(sent, sent_sum)

        @pl.when(jnp.logical_not(stay))
        def _():
            sent[...] = near_ref[...]
            sent_sum[...] = near_sum[...]
            compute(kept, kept_sum)

    front = pl.BlockSpec((early, LANES), lambda d, st: (0, chunk))
    back = pl.BlockSpec((late, LANES), lambda d, st: (0, 0))
    block = pl.BlockSpec((1, 2, LANES, BLK), lambda d, st: (d, 0, 0, 0))
    total = pl.BlockSpec((2, 1, LANES), lambda d, st: (0, 0, 0))
    outs = [
        jax.ShapeDtypeStruct((NGRP, 2, LANES, BLK), sel.dtype),
        jax.ShapeDtypeStruct((2, 1, LANES), jnp.float32),
    ]
    again = () if near is None else tuple(near)
    return pl.pallas_call(
        body,
        out_shape=outs if near is None else [outs[0], outs[0], outs[1], outs[1]],
        grid_spec=pltpu.PrefetchScalarGridSpec(
            num_scalar_prefetch=1,
            grid=(NGRP,),
            in_specs=[
                pl.BlockSpec((1, BLK, early + late), lambda d, st: (d, 0, 0)),
                front,
                front,
                back,
                back,
            ]
            + [block, total][: len(again)],
            out_specs=[block, total] if near is None else [block, block, total, total],
        ),
        compiler_params=pltpu.CompilerParams(vmem_limit_bytes=14 * MIB),
        cost_estimate=pl.CostEstimate(flops=0, bytes_accessed=0, transcendentals=0),
        name="products",
    )(structure, sel, *firsts, *rests, *again)


def bundle(kept, back):
    def body(kept_ref, back_ref, *outs):
        for d, out in enumerate(outs):
            out[0] = kept_ref[d]
            out[1] = back_ref[d]

    shape = jax.ShapeDtypeStruct((2, *kept.shape[1:]), kept.dtype)
    return pl.pallas_call(
        body,
        out_shape=[shape] * NGRP,
        in_specs=[VMEM, VMEM],
        out_specs=[VMEM] * NGRP,
        compiler_params=pltpu.CompilerParams(vmem_limit_bytes=8 * MIB),
        name="bundle",
    )(kept, back)


def squares(factor_inv):
    sups, rows, cols = factor_inv.shape
    half = cols // 2

    def body(in_ref, out_ref):
        for k in range(sups):
            value = in_ref[k].astype(jnp.float32)
            out_ref[k : k + 1, :] = jnp.sum(value * value, axis=0, keepdims=True)

    return pl.pallas_call(
        body,
        out_shape=jax.ShapeDtypeStruct((sups, cols), jnp.float32),
        grid=(2,),
        in_specs=[pl.BlockSpec((sups, rows, half), lambda c: (0, 0, c))],
        out_specs=pl.BlockSpec((sups, half), lambda c: (0, c)),
        compiler_params=pltpu.CompilerParams(vmem_limit_bytes=8 * MIB),
        name="squares",
    )(factor_inv)


def place_sums(linv, kept, back):
    cols = linv.shape[1]

    def body(linv_ref, kept0, kept1, back0, back1, out):
        n = lax.axis_index("narrow")
        group = lax.rem(lax.div(lax.axis_index("wide"), Y), NGRP)
        out[...] = linv_ref[...]
        for c, (ours, theirs) in enumerate(((kept0, back0), (kept1, back1))):
            for xx in range(2):
                at = pl.multiple_of(group * (cols // NGRP) + (2 * xx + c) * LANES, LANES)
                for k in range(2):
                    value = jnp.where(n == k, ours[xx], theirs[xx])
                    out[k : k + 1, pl.ds(at, LANES)] += value

    return pl.pallas_call(
        body,
        out_shape=jax.ShapeDtypeStruct(linv.shape, jnp.float32),
        in_specs=[VMEM] * 5,
        out_specs=VMEM,
        compiler_params=pltpu.CompilerParams(vmem_limit_bytes=4 * MIB),
        name="place_sums",
    )(linv, *kept, *back)


def assemble(messages, chunk, held):
    tall = 4 * LANES
    rows_total = 2 * 2 * NGRP * tall

    def body(*refs):
        msg_refs = refs[:NGRP]
        out, wide_buf, narrow_buf, sem = refs[-4:]
        n = lax.axis_index("narrow")
        w = lax.axis_index("wide")
        copies = []
        for d in range(NGRP):
            source = lax.bitwise_xor(lax.rem(lax.div(w, Y), NGRP), d)
            for xx in range(2):
                slot = 2 * d + xx
                for k in range(2):
                    which = (n != k).astype(jnp.int32)
                    value = msg_refs[d][which, xx].astype(jnp.float32)
                    for lt in range(2):
                        wide_buf[slot, pl.ds(2 * lt + k, LANES, stride=4), :] = value[
                            :, lt * LANES : (lt + 1) * LANES
                        ]
                narrow_buf[slot] = wide_buf[slot].astype(narrow_buf.dtype)
                row = pl.multiple_of(((source * 2 + xx) * 2 + chunk) * tall, tall)
                copy = pltpu.make_async_copy(
                    narrow_buf.at[slot], out.at[pl.ds(row, tall), :], sem.at[slot]
                )
                copy.start()
                copies.append(copy)
        for copy in copies:
            copy.wait()

    extra = () if held is None else (held,)
    return pl.pallas_call(
        body,
        out_shape=jax.ShapeDtypeStruct((rows_total, LANES), messages[0].dtype),
        in_specs=[VMEM] * NGRP + [ANY] * len(extra),
        out_specs=ANY,
        scratch_shapes=[
            pltpu.VMEM((2 * NGRP, tall, LANES), jnp.float32),
            pltpu.VMEM((2 * NGRP, tall, LANES), messages[0].dtype),
            pltpu.SemaphoreType.DMA((2 * NGRP,)),
        ],
        input_output_aliases={NGRP: 0} if extra else {},
        compiler_params=pltpu.CompilerParams(vmem_limit_bytes=8 * MIB),
        name="assemble",
    )(*messages, *extra)


def per_device_grid(inverse, panel, factor_inv, structure):
    n = lax.axis_index("narrow")
    first = structure.shape[1] - panel.shape[1] // BLK
    size = lax.axis_size("wide")
    f_own, top, bottom = pack_first(structure, panel, inverse, first)
    other = swap_cores(lax.dynamic_index_in_dim(panel, 1 - n, 0, keepdims=False), "panel_swap")
    r_own = pack_rest(structure, panel, other, first)
    linv = squares(factor_inv)
    f_z = hop(f_own, ZH, "first_z")
    f_x = hop(f_own, X, "first_x")
    a_z0 = hop(top, ZL, "inv_z0")
    a_y = hop(inverse, Y, "inv_y")
    r_x0 = hop(r_own[0], X, "rest0_x")
    a_y, a_z0, f_z, f_x, r_x0, linv, *r_own = lax.optimization_barrier(
        (a_y, a_z0, f_z, f_x, r_x0, linv, *r_own)
    )
    r_z0 = hop(r_own[0], ZH, "rest0_z")
    a_z1 = hop(after(bottom, f_z), ZL, "inv_z1")
    f_xz = hop(f_z, X, "first_xz")
    a_yz0 = hop(a_z0, Y, "inv_yz0")
    a_yz1 = hop(a_z1, Y, "inv_yz1")
    most = stack_rows([inverse, a_y, a_z0])
    s_most = swap_cores(most, "inv_swap")
    r_z0, f_xz, a_z1, a_yz0, a_yz1, s_most, *r_own = lax.optimization_barrier(
        (r_z0, f_xz, a_z1, a_yz0, a_yz1, s_most, *r_own)
    )
    r_z1 = hop(r_own[1], ZH, "rest1_z")
    r_xz0 = hop(r_z0, X, "rest0_xz")
    r_x1 = hop(r_own[1], X, "rest1_x")
    more = stack_rows([a_z1, a_yz0, a_yz1])
    s_more = swap_cores(more, "inv_swap_more")
    sel = pack_inverse(structure, (most, more), (s_most, s_more), first)
    r_z1, r_x1 = lax.optimization_barrier((r_z1, r_x1))

    def deliver(kept, sent, c):
        messages = bundle(kept, swap_cores(sent, f"cross{c}_swap"))
        return [messages[0]] + [
            hop(messages[d], (d % 2) * Y + (d // 2) * ZL, f"cross{c}_{d}") for d in range(1, NGRP)
        ]

    near = products(structure, sel, (f_own, f_x), (r_own[0], r_x0), 0)
    kept, sent, kept_sum0, sent_sum0 = products(
        structure, sel, (f_z, f_xz), (r_z0, r_xz0), 0, near
    )
    messages = deliver(kept, sent, 0)
    r_xz1 = hop(r_z1, X, "rest1_xz")
    near = products(structure, sel, (f_own, f_x), (r_own[1], r_x1), 1)
    r_xz1, *messages = lax.optimization_barrier((r_xz1, *messages))
    kept, sent, kept_sum1, sent_sum1 = products(
        structure, sel, (f_z, f_xz), (r_z1, r_xz1), 1, near
    )
    held = assemble(messages, 0, None)
    messages = deliver(kept, sent, 1)
    back = [
        swap_cores(after(total, messages[0]), "sums_swap") for total in (sent_sum0, sent_sum1)
    ]
    held = assemble(messages, 1, held)
    variance = place_sums(linv, (kept_sum0, kept_sum1), back)
    for mask in (X, ZH, Y, ZL):
        variance = variance + hop(variance, mask, f"variance_{mask}")
    half = panel.shape[2] * size // 2
    cross = held.reshape(half, 2, 2, LANES).transpose(0, 2, 1, 3).reshape(half, 2, BLK)
    return cross, variance


def solution(mesh):
    in_specs = (P("wide", "narrow"), P(None, "narrow", "wide"), P(None, "wide", "narrow"), P())
    out_specs = (P("narrow", None, "wide"), P(None, "narrow"))

    def run(inverse, panel, factor_inv, structure):
        fits = (
            mesh.shape["wide"] == 16
            and mesh.shape["narrow"] == 2 == panel.shape[0]
            and panel.shape[2] == 16 * BLK == inverse.shape[0]
        )
        return jax.shard_map(
            per_device_grid if fits else per_device_general,
            mesh=mesh,
            in_specs=in_specs,
            out_specs=out_specs,
            check_vma=False,
        )(inverse, panel, factor_inv, structure)

    return run
```

```python
import jax
import jax.numpy as jnp
from jax import lax
from jax.experimental import pallas as pl
from jax.experimental.pallas import tpu as pltpu
from jax.sharding import PartitionSpec as P

BLK = 256
LANES = 128
ANY = pl.BlockSpec(memory_space=pl.ANY)
VMEM = pl.BlockSpec(memory_space=pltpu.VMEM)
SMEM = pl.BlockSpec(memory_space=pltpu.SMEM)


def spread(value, axis, source):
    kept = jnp.where(lax.axis_index(axis) == source, value, 0).astype(value.dtype)
    return lax.psum(kept, axis)


def block_partial(gathered, inverse, row_inside, col_inside, first_row, row_count):
    local_blocks = inverse.shape[1] // BLK
    running = jnp.zeros((row_count, BLK), jnp.float32)
    for blk_index in range(local_blocks):

        def product(blk_index=blk_index):
            panel_piece = lax.dynamic_slice(
                gathered, (blk_index * BLK, first_row), (BLK, row_count)
            )
            block_z = inverse[:, blk_index * BLK : (blk_index + 1) * BLK]
            return lax.dot_general(
                panel_piece, block_z, (((0,), (1,)), ((), ())), preferred_element_type=jnp.float32
            )

        def skipped():
            return jnp.zeros((row_count, BLK), jnp.float32)

        running = running + lax.cond(row_inside & col_inside[blk_index], product, skipped)
    return -running


def per_device_general(inverse, panel, factor_inv, structure):
    wide_count = lax.axis_size("wide")
    narrow_count = lax.axis_size("narrow")
    nsup_count = panel.shape[0]
    kw_total = panel.shape[2] * wide_count
    kw_local = kw_total // narrow_count
    local_blocks = inverse.shape[1] // BLK
    row_index = lax.axis_index("wide")
    col_first = lax.axis_index("narrow") * local_blocks
    col_ids = col_first + jnp.arange(local_blocks, dtype=jnp.int32)
    row_inside = jnp.any(structure == row_index, axis=1)
    col_inside = jnp.any(structure[:, :, None] == col_ids[None, None, :], axis=1)
    root_index = row_index // local_blocks
    offset = (row_index - root_index * local_blocks) * BLK
    cross_parts = []
    own_parts = []
    for sup_index in range(nsup_count):
        gathered_one = lax.all_gather(panel[sup_index], "wide", axis=1, tiled=True)

        def one_term(first_row, row_count, gathered_one=gathered_one, sup_index=sup_index):
            return block_partial(
                gathered_one,
                inverse,
                row_inside[sup_index],
                col_inside[sup_index],
                first_row,
                row_count,
            )

        cross_parts.append(
            lax.psum_scatter(
                one_term(jnp.int32(0), kw_local * lax.axis_size("narrow")),
                "narrow",
                scatter_dimension=0,
                tiled=True,
            )
        )
        own_parts.append(lax.dynamic_slice_in_dim(gathered_one, offset, BLK, axis=0))
    cross_f = jnp.stack(cross_parts, axis=1)
    own_rows = jnp.stack(own_parts)
    owner_panel = spread(own_rows, "narrow", root_index)
    owner_slice = lax.dynamic_slice_in_dim(
        owner_panel, lax.axis_index("narrow") * kw_local, kw_local, axis=2
    )
    weighted = jnp.einsum("kia,aki->ka", owner_slice.astype(jnp.float32), cross_f)
    linv_part = jnp.sum(jnp.square(factor_inv.astype(jnp.float32)), axis=1)
    variance = lax.psum(linv_part - weighted, "wide")
    return (cross_f.astype(jnp.bfloat16), variance)


X, Y, ZL, ZH = 1, 2, 4, 8
NGRP = 4
SPLIT = 192
MIB = 1024 * 1024


def swap_cores(value, name):
    with jax.named_scope(name):
        return lax.ppermute(value, "narrow", [(0, 1), (1, 0)])


def hop(value, mask, name):
    size = lax.axis_size("wide")
    with jax.named_scope(name):
        return lax.ppermute(value, "wide", [(i, i ^ mask) for i in range(size)])


def after(value, *earlier):
    return lax.optimization_barrier((value, *earlier))[0]


def pick(structure_ref, n, j, first):
    nblocks = structure_ref.shape[1]
    start = jnp.where(n == 0, 0, nblocks - first)
    return structure_ref[n, lax.rem(start + j, nblocks)]


def pack_first(structure, panel, inverse, first):
    half_blocks = panel.shape[1] // BLK

    def body(st, panel_ref, inv_ref, out, *pieces):
        n = lax.axis_index("narrow")
        for j in range(first):
            row = pl.multiple_of(lax.rem(pick(st, n, j, first), half_blocks) * BLK, BLK)
            out[j * BLK : (j + 1) * BLK, :] = panel_ref[n, pl.ds(row, BLK), :]
        pieces[0][...] = inv_ref[:SPLIT, :]
        pieces[1][...] = inv_ref[SPLIT:, :]

    width = inverse.shape[1]
    return pl.pallas_call(
        body,
        out_shape=[
            jax.ShapeDtypeStruct((first * BLK, panel.shape[2]), panel.dtype),
            jax.ShapeDtypeStruct((SPLIT, width), inverse.dtype),
            jax.ShapeDtypeStruct((BLK - SPLIT, width), inverse.dtype),
        ],
        in_specs=[SMEM, VMEM, VMEM],
        out_specs=[VMEM] * 3,
        compiler_params=pltpu.CompilerParams(vmem_limit_bytes=8 * MIB),
        name="pack_first",
    )(structure, panel, inverse)


def pack_rest(structure, panel, other, first):
    nblocks = structure.shape[1]
    half_blocks = panel.shape[1] // BLK

    def body(st, panel_ref, other_ref, out0, out1):
        n = lax.axis_index("narrow")
        for j in range(nblocks - first):
            b = pick(st, n, first + j, first)
            row = pl.multiple_of(lax.rem(b, half_blocks) * BLK, BLK)
            mine = lax.div(b, half_blocks) == n
            rows = slice(j * BLK, (j + 1) * BLK)

            @pl.when(mine)
            def _():
                out0[rows, :] = panel_ref[n, pl.ds(row, BLK), :LANES]
                out1[rows, :] = panel_ref[n, pl.ds(row, BLK), LANES:]

            @pl.when(jnp.logical_not(mine))
            def _():
                out0[rows, :] = other_ref[pl.ds(row, BLK), :LANES]
                out1[rows, :] = other_ref[pl.ds(row, BLK), LANES:]

    shape = jax.ShapeDtypeStruct(((nblocks - first) * BLK, LANES), panel.dtype)
    return pl.pallas_call(
        body,
        out_shape=(shape, shape),
        in_specs=[SMEM, VMEM, VMEM],
        out_specs=[VMEM, VMEM],
        compiler_params=pltpu.CompilerParams(vmem_limit_bytes=8 * MIB),
        name="pack_rest",
    )(structure, panel, other)


def stack_rows(pieces):
    rows = sum(piece.shape[0] for piece in pieces)

    def body(*refs):
        at = 0
        for ref in refs[:-1]:
            refs[-1][at : at + ref.shape[0], :] = ref[...]
            at += ref.shape[0]

    return pl.pallas_call(
        body,
        out_shape=jax.ShapeDtypeStruct((rows, pieces[0].shape[1]), pieces[0].dtype),
        in_specs=[VMEM] * len(pieces),
        out_specs=VMEM,
        compiler_params=pltpu.CompilerParams(vmem_limit_bytes=8 * MIB),
        name="stack_rows",
    )(*pieces)


def pack_inverse(structure, owns, others, first):
    nblocks = structure.shape[1]
    half_blocks = owns[0].shape[1] // BLK
    count = len(owns)
    runs, row = [], 0
    for p, own in enumerate(owns):
        at = 0
        while at < own.shape[0]:
            rows = min(own.shape[0] - at, BLK - row % BLK)
            runs.append((p, at, row // BLK, row % BLK, rows))
            at, row = at + rows, row + rows

    def body(st, *refs):
        out = refs[2 * count]
        n = lax.axis_index("narrow")
        for j in range(nblocks):
            b = pick(st, n, j, first)
            col = pl.multiple_of(lax.rem(b, half_blocks) * BLK, BLK)
            mine = lax.div(b, half_blocks) == n

            def move(sources, j=j, col=col):
                for p, at, d, top, rows in runs:
                    out[d, top : top + rows, j * BLK : (j + 1) * BLK] = sources[p][
                        at : at + rows, pl.ds(col, BLK)
                    ]

            pl.when(mine)(lambda move=move: move(refs[:count]))
            pl.when(jnp.logical_not(mine))(lambda move=move: move(refs[count : 2 * count]))

    return pl.pallas_call(
        body,
        out_shape=jax.ShapeDtypeStruct((NGRP, BLK, nblocks * BLK), owns[0].dtype),
        in_specs=[SMEM] + [VMEM] * (2 * count),
        out_specs=VMEM,
        compiler_params=pltpu.CompilerParams(vmem_limit_bytes=18 * MIB),
        name="pack_inverse",
    )(structure, *owns, *others)


def products(structure, sel, firsts, rests, chunk, near=None):
    nblocks = structure.shape[1]
    early = firsts[0].shape[0]
    late = rests[0].shape[0]
    first = early // BLK

    def body(st, sel_ref, f0, f1, r0, r1, *refs):
        d = pl.program_id(0)
        n = lax.axis_index("narrow")
        w = lax.axis_index("wide")
        x = lax.bitwise_and(w, 1)
        mask = lax.rem(d, 2) * Y + lax.div(d, 2) * ZL
        row = lax.bitwise_xor(w, mask)
        pos = jnp.int32(0)
        inside = jnp.int32(0)
        for j in range(nblocks):
            hit = (pick(st, n, j, first) == row).astype(jnp.int32)
            pos = pos + j * hit
            inside = inside + hit

        def compute(out_ref, sum_ref):
            @pl.when(d == 0)
            def _():
                sum_ref[...] = jnp.zeros_like(sum_ref)

            @pl.when(inside == 0)
            def _():
                out_ref[...] = jnp.zeros_like(out_ref)

            @pl.when(inside > 0)
            def _():
                acc = jnp.dot(
                    sel_ref[0, :, :early],
                    jnp.concatenate([f0[...], f1[...]], axis=1),
                    preferred_element_type=jnp.float32,
                ) + jnp.dot(
                    sel_ref[0, :, early:],
                    jnp.concatenate([r0[...], r1[...]], axis=1),
                    preferred_element_type=jnp.float32,
                )
                for dx in range(2):
                    part = acc[:, dx * LANES : (dx + 1) * LANES]
                    slot = lax.bitwise_xor(x, dx)

                    def weigh(rows, part=part, slot=slot):
                        total = jnp.sum(part * rows.astype(jnp.float32), axis=0, keepdims=True)
                        sum_ref[slot] += total

                    @pl.when(pos < first)
                    def _():
                        at = pl.multiple_of(pos * BLK, BLK)
                        weigh((f0, f1)[dx][pl.ds(at, BLK), :])

                    @pl.when(pos >= first)
                    def _():
                        at = pl.multiple_of((pos - first) * BLK, BLK)
                        weigh((r0, r1)[dx][pl.ds(at, BLK), :])

                    out_ref[0, slot] = (-part).T.astype(out_ref.dtype)

        if near is None:
            compute(*refs)
            return
        near_ref, near_sum, kept, sent, kept_sum, sent_sum = refs
        stay = n == lax.div(w, ZH)

        @pl.when(stay)
        def _():
            kept[...] = near_ref[...]
            kept_sum[...] = near_sum[...]
            compute(sent, sent_sum)

        @pl.when(jnp.logical_not(stay))
        def _():
            sent[...] = near_ref[...]
            sent_sum[...] = near_sum[...]
            compute(kept, kept_sum)

    front = pl.BlockSpec((early, LANES), lambda d, st: (0, chunk))
    back = pl.BlockSpec((late, LANES), lambda d, st: (0, 0))
    block = pl.BlockSpec((1, 2, LANES, BLK), lambda d, st: (d, 0, 0, 0))
    total = pl.BlockSpec((2, 1, LANES), lambda d, st: (0, 0, 0))
    outs = [
        jax.ShapeDtypeStruct((NGRP, 2, LANES, BLK), sel.dtype),
        jax.ShapeDtypeStruct((2, 1, LANES), jnp.float32),
    ]
    again = () if near is None else tuple(near)
    return pl.pallas_call(
        body,
        out_shape=outs if near is None else [outs[0], outs[0], outs[1], outs[1]],
        grid_spec=pltpu.PrefetchScalarGridSpec(
            num_scalar_prefetch=1,
            grid=(NGRP,),
            in_specs=[
                pl.BlockSpec((1, BLK, early + late), lambda d, st: (d, 0, 0)),
                front,
                front,
                back,
                back,
            ]
            + [block, total][: len(again)],
            out_specs=[block, total] if near is None else [block, block, total, total],
        ),
        compiler_params=pltpu.CompilerParams(vmem_limit_bytes=14 * MIB),
        cost_estimate=pl.CostEstimate(flops=0, bytes_accessed=0, transcendentals=0),
        name="products",
    )(structure, sel, *firsts, *rests, *again)


def bundle(kept, back):
    def body(kept_ref, back_ref, *outs):
        for d, out in enumerate(outs):
            out[0] = kept_ref[d]
            out[1] = back_ref[d]

    shape = jax.ShapeDtypeStruct((2, *kept.shape[1:]), kept.dtype)
    return pl.pallas_call(
        body,
        out_shape=[shape] * NGRP,
        in_specs=[VMEM, VMEM],
        out_specs=[VMEM] * NGRP,
        compiler_params=pltpu.CompilerParams(vmem_limit_bytes=8 * MIB),
        name="bundle",
    )(kept, back)


def squares(factor_inv):
    sups, rows, cols = factor_inv.shape
    half = cols // 2

    def body(in_ref, out_ref):
        for k in range(sups):
            value = in_ref[k].astype(jnp.float32)
            out_ref[k : k + 1, :] = jnp.sum(value * value, axis=0, keepdims=True)

    return pl.pallas_call(
        body,
        out_shape=jax.ShapeDtypeStruct((sups, cols), jnp.float32),
        grid=(2,),
        in_specs=[pl.BlockSpec((sups, rows, half), lambda c: (0, 0, c))],
        out_specs=pl.BlockSpec((sups, half), lambda c: (0, c)),
        compiler_params=pltpu.CompilerParams(vmem_limit_bytes=8 * MIB),
        name="squares",
    )(factor_inv)


def place_sums(linv, kept, back):
    cols = linv.shape[1]

    def body(linv_ref, kept0, kept1, back0, back1, out):
        n = lax.axis_index("narrow")
        group = lax.rem(lax.div(lax.axis_index("wide"), Y), NGRP)
        out[...] = linv_ref[...]
        for c, (ours, theirs) in enumerate(((kept0, back0), (kept1, back1))):
            for xx in range(2):
                at = pl.multiple_of(group * (cols // NGRP) + (2 * xx + c) * LANES, LANES)
                for k in range(2):
                    value = jnp.where(n == k, ours[xx], theirs[xx])
                    out[k : k + 1, pl.ds(at, LANES)] += value

    return pl.pallas_call(
        body,
        out_shape=jax.ShapeDtypeStruct(linv.shape, jnp.float32),
        in_specs=[VMEM] * 5,
        out_specs=VMEM,
        compiler_params=pltpu.CompilerParams(vmem_limit_bytes=4 * MIB),
        name="place_sums",
    )(linv, *kept, *back)


def assemble(messages, chunk, held):
    tall = 4 * LANES
    rows_total = 2 * 2 * NGRP * tall

    def body(*refs):
        msg_refs = refs[:NGRP]
        out, wide_buf, narrow_buf, sem = refs[-4:]
        n = lax.axis_index("narrow")
        w = lax.axis_index("wide")
        copies = []
        for d in range(NGRP):
            source = lax.bitwise_xor(lax.rem(lax.div(w, Y), NGRP), d)
            for xx in range(2):
                slot = 2 * d + xx
                for k in range(2):
                    which = (n != k).astype(jnp.int32)
                    value = msg_refs[d][which, xx].astype(jnp.float32)
                    for lt in range(2):
                        wide_buf[slot, pl.ds(2 * lt + k, LANES, stride=4), :] = value[
                            :, lt * LANES : (lt + 1) * LANES
                        ]
                narrow_buf[slot] = wide_buf[slot].astype(narrow_buf.dtype)
                row = pl.multiple_of(((source * 2 + xx) * 2 + chunk) * tall, tall)
                copy = pltpu.make_async_copy(
                    narrow_buf.at[slot], out.at[pl.ds(row, tall), :], sem.at[slot]
                )
                copy.start()
                copies.append(copy)
        for copy in copies:
            copy.wait()

    extra = () if held is None else (held,)
    return pl.pallas_call(
        body,
        out_shape=jax.ShapeDtypeStruct((rows_total, LANES), messages[0].dtype),
        in_specs=[VMEM] * NGRP + [ANY] * len(extra),
        out_specs=ANY,
        scratch_shapes=[
            pltpu.VMEM((2 * NGRP, tall, LANES), jnp.float32),
            pltpu.VMEM((2 * NGRP, tall, LANES), messages[0].dtype),
            pltpu.SemaphoreType.DMA((2 * NGRP,)),
        ],
        input_output_aliases={NGRP: 0} if extra else {},
        compiler_params=pltpu.CompilerParams(vmem_limit_bytes=8 * MIB),
        name="assemble",
    )(*messages, *extra)


def per_device_grid(inverse, panel, factor_inv, structure):
    n = lax.axis_index("narrow")
    first = structure.shape[1] - panel.shape[1] // BLK
    size = lax.axis_size("wide")
    f_own, top, bottom = pack_first(structure, panel, inverse, first)
    other = swap_cores(lax.dynamic_index_in_dim(panel, 1 - n, 0, keepdims=False), "panel_swap")
    r_own = pack_rest(structure, panel, other, first)
    linv = squares(factor_inv)
    f_z = hop(f_own, ZH, "first_z")
    f_x = hop(f_own, X, "first_x")
    a_z0 = hop(top, ZL, "inv_z0")
    a_y = hop(inverse, Y, "inv_y")
    a_y, a_z0, f_z, f_x, linv, *r_own = lax.optimization_barrier(
        (a_y, a_z0, f_z, f_x, linv, *r_own)
    )
    r_z0 = hop(r_own[0], ZH, "rest0_z")
    a_z1 = hop(after(bottom, f_z), ZL, "inv_z1")
    f_xz = hop(f_z, X, "first_xz")
    r_x0 = hop(r_own[0], X, "rest0_x")
    a_yz0 = hop(a_z0, Y, "inv_yz0")
    a_yz1 = hop(a_z1, Y, "inv_yz1")
    most = stack_rows([inverse, a_y, a_z0])
    r_z0, r_x0, f_xz, a_z1, a_yz0, a_yz1, most, *r_own = lax.optimization_barrier(
        (r_z0, r_x0, f_xz, a_z1, a_yz0, a_yz1, most, *r_own)
    )
    r_z1 = hop(r_own[1], ZH, "rest1_z")
    r_xz0 = hop(r_z0, X, "rest0_xz")
    r_x1 = hop(r_own[1], X, "rest1_x")
    more = stack_rows([a_z1, a_yz0, a_yz1])
    s_most = swap_cores(most, "inv_swap")
    s_more = swap_cores(more, "inv_swap_more")
    sel = pack_inverse(structure, (most, more), (s_most, s_more), first)
    r_z1, r_x1 = lax.optimization_barrier((r_z1, r_x1))

    def deliver(kept, sent, c):
        messages = bundle(kept, swap_cores(sent, f"cross{c}_swap"))
        return [messages[0]] + [
            hop(messages[d], (d % 2) * Y + (d // 2) * ZL, f"cross{c}_{d}") for d in range(1, NGRP)
        ]

    near = products(structure, sel, (f_own, f_x), (r_own[0], r_x0), 0)
    kept, sent, kept_sum0, sent_sum0 = products(
        structure, sel, (f_z, f_xz), (r_z0, r_xz0), 0, near
    )
    messages = deliver(kept, sent, 0)
    r_xz1 = hop(r_z1, X, "rest1_xz")
    near = products(structure, sel, (f_own, f_x), (r_own[1], r_x1), 1)
    r_xz1, *messages = lax.optimization_barrier((r_xz1, *messages))
    kept, sent, kept_sum1, sent_sum1 = products(
        structure, sel, (f_z, f_xz), (r_z1, r_xz1), 1, near
    )
    held = assemble(messages, 0, None)
    back = [swap_cores(total, "sums_swap") for total in (sent_sum0, sent_sum1)]
    variance = place_sums(linv, (kept_sum0, kept_sum1), back)
    variance = variance + hop(variance, X, "variance_x")
    held = assemble(deliver(after(kept, variance), sent, 1), 1, held)
    for mask in (ZH, Y, ZL):
        variance = variance + hop(variance, mask, f"variance_{mask}")
    half = panel.shape[2] * size // 2
    cross = held.reshape(half, 2, 2, LANES).transpose(0, 2, 1, 3).reshape(half, 2, BLK)
    return cross, variance


def solution(mesh):
    in_specs = (P("wide", "narrow"), P(None, "narrow", "wide"), P(None, "wide", "narrow"), P())
    out_specs = (P("narrow", None, "wide"), P(None, "narrow"))

    def run(inverse, panel, factor_inv, structure):
        fits = (
            mesh.shape["wide"] == 16
            and mesh.shape["narrow"] == 2 == panel.shape[0]
            and panel.shape[2] == 16 * BLK == inverse.shape[0]
        )
        return jax.shard_map(
            per_device_grid if fits else per_device_general,
            mesh=mesh,
            in_specs=in_specs,
            out_specs=out_specs,
            check_vma=False,
        )(inverse, panel, factor_inv, structure)

    return run
```

```python
import jax
import jax.numpy as jnp
from jax import lax
from jax.experimental import pallas as pl
from jax.experimental.pallas import tpu as pltpu
from jax.sharding import PartitionSpec as P

BLK = 256
LANES = 128
ANY = pl.BlockSpec(memory_space=pl.ANY)
VMEM = pl.BlockSpec(memory_space=pltpu.VMEM)
SMEM = pl.BlockSpec(memory_space=pltpu.SMEM)


def spread(value, axis, source):
    kept = jnp.where(lax.axis_index(axis) == source, value, 0).astype(value.dtype)
    return lax.psum(kept, axis)


def block_partial(gathered, inverse, row_inside, col_inside, first_row, row_count):
    local_blocks = inverse.shape[1] // BLK
    running = jnp.zeros((row_count, BLK), jnp.float32)
    for blk_index in range(local_blocks):

        def product(blk_index=blk_index):
            panel_piece = lax.dynamic_slice(
                gathered, (blk_index * BLK, first_row), (BLK, row_count)
            )
            block_z = inverse[:, blk_index * BLK : (blk_index + 1) * BLK]
            return lax.dot_general(
                panel_piece, block_z, (((0,), (1,)), ((), ())), preferred_element_type=jnp.float32
            )

        def skipped():
            return jnp.zeros((row_count, BLK), jnp.float32)

        running = running + lax.cond(row_inside & col_inside[blk_index], product, skipped)
    return -running


def per_device_general(inverse, panel, factor_inv, structure):
    wide_count = lax.axis_size("wide")
    narrow_count = lax.axis_size("narrow")
    nsup_count = panel.shape[0]
    kw_total = panel.shape[2] * wide_count
    kw_local = kw_total // narrow_count
    local_blocks = inverse.shape[1] // BLK
    row_index = lax.axis_index("wide")
    col_first = lax.axis_index("narrow") * local_blocks
    col_ids = col_first + jnp.arange(local_blocks, dtype=jnp.int32)
    row_inside = jnp.any(structure == row_index, axis=1)
    col_inside = jnp.any(structure[:, :, None] == col_ids[None, None, :], axis=1)
    root_index = row_index // local_blocks
    offset = (row_index - root_index * local_blocks) * BLK
    cross_parts = []
    own_parts = []
    for sup_index in range(nsup_count):
        gathered_one = lax.all_gather(panel[sup_index], "wide", axis=1, tiled=True)

        def one_term(first_row, row_count, gathered_one=gathered_one, sup_index=sup_index):
            return block_partial(
                gathered_one,
                inverse,
                row_inside[sup_index],
                col_inside[sup_index],
                first_row,
                row_count,
            )

        cross_parts.append(
            lax.psum_scatter(
                one_term(jnp.int32(0), kw_local * lax.axis_size("narrow")),
                "narrow",
                scatter_dimension=0,
                tiled=True,
            )
        )
        own_parts.append(lax.dynamic_slice_in_dim(gathered_one, offset, BLK, axis=0))
    cross_f = jnp.stack(cross_parts, axis=1)
    own_rows = jnp.stack(own_parts)
    owner_panel = spread(own_rows, "narrow", root_index)
    owner_slice = lax.dynamic_slice_in_dim(
        owner_panel, lax.axis_index("narrow") * kw_local, kw_local, axis=2
    )
    weighted = jnp.einsum("kia,aki->ka", owner_slice.astype(jnp.float32), cross_f)
    linv_part = jnp.sum(jnp.square(factor_inv.astype(jnp.float32)), axis=1)
    variance = lax.psum(linv_part - weighted, "wide")
    return (cross_f.astype(jnp.bfloat16), variance)


X, Y, ZL, ZH = 1, 2, 4, 8
NGRP = 4
SPLIT = 192
TAIL = 16
MIB = 1024 * 1024


def swap_cores(value, name):
    with jax.named_scope(name):
        return lax.ppermute(value, "narrow", [(0, 1), (1, 0)])


def hop(value, mask, name):
    size = lax.axis_size("wide")
    with jax.named_scope(name):
        return lax.ppermute(value, "wide", [(i, i ^ mask) for i in range(size)])


def after(value, *earlier):
    return lax.optimization_barrier((value, *earlier))[0]


def pick(structure_ref, n, j, first):
    nblocks = structure_ref.shape[1]
    start = jnp.where(n == 0, 0, nblocks - first)
    return structure_ref[n, lax.rem(start + j, nblocks)]


def pack_first(structure, panel, inverse, first):
    half_blocks = panel.shape[1] // BLK

    def body(st, panel_ref, inv_ref, out, *pieces):
        n = lax.axis_index("narrow")
        for j in range(first):
            row = pl.multiple_of(lax.rem(pick(st, n, j, first), half_blocks) * BLK, BLK)
            out[j * BLK : (j + 1) * BLK, :] = panel_ref[n, pl.ds(row, BLK), :]
        pieces[0][...] = inv_ref[:SPLIT, :]
        pieces[1][...] = inv_ref[SPLIT:, :]

    width = inverse.shape[1]
    return pl.pallas_call(
        body,
        out_shape=[
            jax.ShapeDtypeStruct((first * BLK, panel.shape[2]), panel.dtype),
            jax.ShapeDtypeStruct((SPLIT, width), inverse.dtype),
            jax.ShapeDtypeStruct((BLK - SPLIT, width), inverse.dtype),
        ],
        in_specs=[SMEM, VMEM, VMEM],
        out_specs=[VMEM] * 3,
        compiler_params=pltpu.CompilerParams(vmem_limit_bytes=8 * MIB),
        name="pack_first",
    )(structure, panel, inverse)


def pack_rest(structure, panel, other, first):
    nblocks = structure.shape[1]
    half_blocks = panel.shape[1] // BLK

    def body(st, panel_ref, other_ref, out0, out1):
        n = lax.axis_index("narrow")
        for j in range(nblocks - first):
            b = pick(st, n, first + j, first)
            row = pl.multiple_of(lax.rem(b, half_blocks) * BLK, BLK)
            mine = lax.div(b, half_blocks) == n
            rows = slice(j * BLK, (j + 1) * BLK)

            @pl.when(mine)
            def _():
                out0[rows, :] = panel_ref[n, pl.ds(row, BLK), :LANES]
                out1[rows, :] = panel_ref[n, pl.ds(row, BLK), LANES:]

            @pl.when(jnp.logical_not(mine))
            def _():
                out0[rows, :] = other_ref[pl.ds(row, BLK), :LANES]
                out1[rows, :] = other_ref[pl.ds(row, BLK), LANES:]

    shape = jax.ShapeDtypeStruct(((nblocks - first) * BLK, LANES), panel.dtype)
    return pl.pallas_call(
        body,
        out_shape=(shape, shape),
        in_specs=[SMEM, VMEM, VMEM],
        out_specs=[VMEM, VMEM],
        compiler_params=pltpu.CompilerParams(vmem_limit_bytes=8 * MIB),
        name="pack_rest",
    )(structure, panel, other)


def stack_rows(pieces):
    rows = sum(piece.shape[0] for piece in pieces)

    def body(*refs):
        at = 0
        for ref in refs[:-1]:
            refs[-1][at : at + ref.shape[0], :] = ref[...]
            at += ref.shape[0]

    return pl.pallas_call(
        body,
        out_shape=jax.ShapeDtypeStruct((rows, pieces[0].shape[1]), pieces[0].dtype),
        in_specs=[VMEM] * len(pieces),
        out_specs=VMEM,
        compiler_params=pltpu.CompilerParams(vmem_limit_bytes=8 * MIB),
        name="stack_rows",
    )(*pieces)


def pack_inverse(structure, owns, others, first):
    nblocks = structure.shape[1]
    half_blocks = owns[0].shape[1] // BLK
    count = len(owns)
    runs, row = [], 0
    for p, own in enumerate(owns):
        at = 0
        while at < own.shape[0]:
            rows = min(own.shape[0] - at, BLK - row % BLK)
            runs.append((p, at, row // BLK, row % BLK, rows))
            at, row = at + rows, row + rows

    def body(st, *refs):
        out = refs[2 * count]
        n = lax.axis_index("narrow")
        for j in range(nblocks):
            b = pick(st, n, j, first)
            col = pl.multiple_of(lax.rem(b, half_blocks) * BLK, BLK)
            mine = lax.div(b, half_blocks) == n

            def move(sources, j=j, col=col):
                for p, at, d, top, rows in runs:
                    out[d, top : top + rows, j * BLK : (j + 1) * BLK] = sources[p][
                        at : at + rows, pl.ds(col, BLK)
                    ]

            pl.when(mine)(lambda move=move: move(refs[:count]))
            pl.when(jnp.logical_not(mine))(lambda move=move: move(refs[count : 2 * count]))

    return pl.pallas_call(
        body,
        out_shape=jax.ShapeDtypeStruct((NGRP, BLK, nblocks * BLK), owns[0].dtype),
        in_specs=[SMEM] + [VMEM] * (2 * count),
        out_specs=VMEM,
        compiler_params=pltpu.CompilerParams(vmem_limit_bytes=18 * MIB),
        name="pack_inverse",
    )(structure, *owns, *others)


def products(structure, sel, firsts, rests, chunk, near=None):
    nblocks = structure.shape[1]
    early = firsts[0].shape[0]
    first = early // BLK
    spot = slice(chunk * LANES, (chunk + 1) * LANES)

    def body(st, sel_ref, f0, f1, r0, r1, *refs):
        result, total = refs[-2:]
        n = lax.axis_index("narrow")
        w = lax.axis_index("wide")
        x = lax.bitwise_and(w, 1)
        total[...] = jnp.zeros_like(total)
        for d in range(NGRP):
            row = lax.bitwise_xor(w, (d % 2) * Y + (d // 2) * ZL)
            pos = jnp.int32(0)
            inside = jnp.int32(0)
            for j in range(nblocks):
                hit = (pick(st, n, j, first) == row).astype(jnp.int32)
                pos = pos + j * hit
                inside = inside + hit

            @pl.when(inside == 0)
            def _(d=d):
                result[d] = jnp.zeros(result.shape[1:], result.dtype)

            @pl.when(inside > 0)
            def _(d=d, pos=pos):
                acc = jnp.dot(
                    sel_ref[d, :, :early],
                    jnp.concatenate([f0[:, spot], f1[:, spot]], axis=1),
                    preferred_element_type=jnp.float32,
                ) + jnp.dot(
                    sel_ref[d, :, early:],
                    jnp.concatenate([r0[...], r1[...]], axis=1),
                    preferred_element_type=jnp.float32,
                )
                for dx in range(2):
                    part = acc[:, dx * LANES : (dx + 1) * LANES]
                    slot = lax.bitwise_xor(x, dx)

                    def weigh(rows, part=part, slot=slot):
                        added = jnp.sum(part * rows.astype(jnp.float32), axis=0, keepdims=True)
                        total[slot] += added

                    @pl.when(pos < first)
                    def _():
                        at = pl.multiple_of(pos * BLK, BLK)
                        weigh((f0, f1)[dx][pl.ds(at, BLK), spot])

                    @pl.when(pos >= first)
                    def _():
                        at = pl.multiple_of((pos - first) * BLK, BLK)
                        weigh((r0, r1)[dx][pl.ds(at, BLK), :])

                    at = pl.multiple_of(slot * LANES, LANES)
                    result[d, pl.ds(at, LANES), :] = (-part).T.astype(result.dtype)

        for slot in range(2):
            left, terms = total[slot], []
            for _ in range(3):
                term = left.astype(result.dtype).astype(jnp.float32)
                terms.append(term)
                left = left - term
            tile = jnp.concatenate(terms + [jnp.zeros((TAIL - 3, LANES), jnp.float32)], axis=0)
            for d in range(NGRP):
                result[d, 2 * LANES :, slot * LANES : (slot + 1) * LANES] = tile.astype(
                    result.dtype
                )
        if near is None:
            refs[0][...] = result[...]
            return
        near_ref, kept, sent = refs[:3]
        stay = n == lax.div(w, ZH)

        @pl.when(stay)
        def _():
            kept[...] = near_ref[...]
            sent[...] = result[...]

        @pl.when(jnp.logical_not(stay))
        def _():
            kept[...] = result[...]
            sent[...] = near_ref[...]

    out = jax.ShapeDtypeStruct((NGRP, 2 * LANES + TAIL, BLK), sel.dtype)
    again = () if near is None else (near,)
    return pl.pallas_call(
        body,
        out_shape=out if near is None else [out, out],
        in_specs=[SMEM] + [VMEM] * (5 + len(again)),
        out_specs=VMEM if near is None else [VMEM, VMEM],
        scratch_shapes=[pltpu.VMEM(out.shape, out.dtype), pltpu.VMEM((2, 1, LANES), jnp.float32)],
        compiler_params=pltpu.CompilerParams(vmem_limit_bytes=16 * MIB),
        cost_estimate=pl.CostEstimate(flops=0, bytes_accessed=0, transcendentals=0),
        name="products",
    )(structure, sel, *firsts, *rests, *again)


def bundle(kept, back):
    def body(kept_ref, back_ref, *outs):
        for d, out in enumerate(outs):
            out[0] = kept_ref[d]
            out[1] = back_ref[d]

    shape = jax.ShapeDtypeStruct((2, *kept.shape[1:]), kept.dtype)
    return pl.pallas_call(
        body,
        out_shape=[shape] * NGRP,
        in_specs=[VMEM, VMEM],
        out_specs=[VMEM] * NGRP,
        compiler_params=pltpu.CompilerParams(vmem_limit_bytes=8 * MIB),
        name="bundle",
    )(kept, back)


def squares(factor_inv):
    sups, rows, cols = factor_inv.shape
    half = cols // 2

    def body(in_ref, out_ref):
        for k in range(sups):
            value = in_ref[k].astype(jnp.float32)
            out_ref[k : k + 1, :] = jnp.sum(value * value, axis=0, keepdims=True)

    return pl.pallas_call(
        body,
        out_shape=jax.ShapeDtypeStruct((sups, cols), jnp.float32),
        grid=(2,),
        in_specs=[pl.BlockSpec((sups, rows, half), lambda c: (0, 0, c))],
        out_specs=pl.BlockSpec((sups, half), lambda c: (0, c)),
        compiler_params=pltpu.CompilerParams(vmem_limit_bytes=8 * MIB),
        name="squares",
    )(factor_inv)


def add_sums(base, messages, chunk):
    cols = base.shape[1]

    def body(base_ref, *refs):
        out = refs[-1]
        n = lax.axis_index("narrow")
        group = lax.rem(lax.div(lax.axis_index("wide"), Y), NGRP)
        out[...] = base_ref[...]
        for d in range(NGRP):
            source = lax.bitwise_xor(group, d)
            for k in range(2):
                which = (n != k).astype(jnp.int32)
                tile = refs[d][which, 2 * LANES :, :].astype(jnp.float32)
                value = tile[0:1] + (tile[1:2] + tile[2:3])
                for xx in range(2):
                    at = source * (cols // NGRP) + (2 * xx + chunk) * LANES
                    spot = pl.ds(pl.multiple_of(at, LANES), LANES)
                    out[k : k + 1, spot] += value[:, xx * LANES : (xx + 1) * LANES]

    return pl.pallas_call(
        body,
        out_shape=jax.ShapeDtypeStruct(base.shape, jnp.float32),
        in_specs=[VMEM] * (1 + NGRP),
        out_specs=VMEM,
        compiler_params=pltpu.CompilerParams(vmem_limit_bytes=4 * MIB),
        name="add_sums",
    )(base, *messages)


def assemble(messages, chunk, held):
    tall = 4 * LANES
    rows_total = 2 * 2 * NGRP * tall

    def body(*refs):
        msg_refs = refs[:NGRP]
        out, wide_buf, narrow_buf, sem = refs[-4:]
        n = lax.axis_index("narrow")
        w = lax.axis_index("wide")
        copies = []
        for d in range(NGRP):
            source = lax.bitwise_xor(lax.rem(lax.div(w, Y), NGRP), d)
            for xx in range(2):
                slot = 2 * d + xx
                for k in range(2):
                    which = (n != k).astype(jnp.int32)
                    value = msg_refs[d][which, xx * LANES : (xx + 1) * LANES, :].astype(
                        jnp.float32
                    )
                    for lt in range(2):
                        wide_buf[slot, pl.ds(2 * lt + k, LANES, stride=4), :] = value[
                            :, lt * LANES : (lt + 1) * LANES
                        ]
                narrow_buf[slot] = wide_buf[slot].astype(narrow_buf.dtype)
                row = pl.multiple_of(((source * 2 + xx) * 2 + chunk) * tall, tall)
                copy = pltpu.make_async_copy(
                    narrow_buf.at[slot], out.at[pl.ds(row, tall), :], sem.at[slot]
                )
                copy.start()
                copies.append(copy)
        for copy in copies:
            copy.wait()

    extra = () if held is None else (held,)
    return pl.pallas_call(
        body,
        out_shape=jax.ShapeDtypeStruct((rows_total, LANES), messages[0].dtype),
        in_specs=[VMEM] * NGRP + [ANY] * len(extra),
        out_specs=ANY,
        scratch_shapes=[
            pltpu.VMEM((2 * NGRP, tall, LANES), jnp.float32),
            pltpu.VMEM((2 * NGRP, tall, LANES), messages[0].dtype),
            pltpu.SemaphoreType.DMA((2 * NGRP,)),
        ],
        input_output_aliases={NGRP: 0} if extra else {},
        compiler_params=pltpu.CompilerParams(vmem_limit_bytes=8 * MIB),
        name="assemble",
    )(*messages, *extra)


def per_device_grid(inverse, panel, factor_inv, structure):
    n = lax.axis_index("narrow")
    first = structure.shape[1] - panel.shape[1] // BLK
    size = lax.axis_size("wide")
    f_own, top, bottom = pack_first(structure, panel, inverse, first)
    other = swap_cores(lax.dynamic_index_in_dim(panel, 1 - n, 0, keepdims=False), "panel_swap")
    r_own = pack_rest(structure, panel, other, first)
    linv = squares(factor_inv)
    f_z = hop(f_own, ZH, "first_z")
    f_x = hop(f_own, X, "first_x")
    a_z0 = hop(top, ZL, "inv_z0")
    a_y = hop(inverse, Y, "inv_y")
    a_y, a_z0, f_z, f_x, linv, *r_own = lax.optimization_barrier(
        (a_y, a_z0, f_z, f_x, linv, *r_own)
    )
    r_z0 = hop(r_own[0], ZH, "rest0_z")
    a_z1 = hop(after(bottom, f_z), ZL, "inv_z1")
    f_xz = hop(f_z, X, "first_xz")
    r_x0 = hop(r_own[0], X, "rest0_x")
    a_yz0 = hop(a_z0, Y, "inv_yz0")
    a_yz1 = hop(a_z1, Y, "inv_yz1")
    most = stack_rows([inverse, a_y, a_z0])
    r_z0, r_x0, f_xz, a_z1, a_yz0, a_yz1, most, linv, *r_own = lax.optimization_barrier(
        (r_z0, r_x0, f_xz, a_z1, a_yz0, a_yz1, most, linv, *r_own)
    )
    r_z1 = hop(r_own[1], ZH, "rest1_z")
    r_xz0 = hop(r_z0, X, "rest0_xz")
    r_x1 = hop(r_own[1], X, "rest1_x")
    more = stack_rows([a_z1, a_yz0, a_yz1])
    s_most = swap_cores(most, "inv_swap")
    s_more = swap_cores(more, "inv_swap_more")
    sel = pack_inverse(structure, (most, more), (s_most, s_more), first)
    for mask in (Y, ZL):
        linv = linv + hop(linv, mask, f"squares_{mask}")
    r_z1, r_x1, linv = lax.optimization_barrier((r_z1, r_x1, linv))

    def deliver(kept, sent, c):
        messages = bundle(kept, swap_cores(sent, f"cross{c}_swap"))
        return [messages[0]] + [
            hop(messages[d], (d % 2) * Y + (d // 2) * ZL, f"cross{c}_{d}") for d in range(1, NGRP)
        ]

    near = products(structure, sel, (f_own, f_x), (r_own[0], r_x0), 0)
    kept, sent = products(structure, sel, (f_z, f_xz), (r_z0, r_xz0), 0, near)
    messages = deliver(kept, sent, 0)
    r_xz1 = hop(r_z1, X, "rest1_xz")
    near = products(structure, sel, (f_own, f_x), (r_own[1], r_x1), 1)
    r_xz1, *messages = lax.optimization_barrier((r_xz1, *messages))
    kept, sent = products(structure, sel, (f_z, f_xz), (r_z1, r_xz1), 1, near)
    held = assemble(messages, 0, None)
    variance = add_sums(linv, messages, 0)
    messages = deliver(kept, sent, 1)
    variance = add_sums(variance, messages, 1)
    held = assemble(messages, 1, held)
    hops = [hop(variance, mask, f"variance_{mask}") for mask in (X, ZH, X | ZH)]
    variance = variance + hops[0] + hops[1] + hops[2]
    half = panel.shape[2] * size // 2
    cross = held.reshape(half, 2, 2, LANES).transpose(0, 2, 1, 3).reshape(half, 2, BLK)
    return cross, variance


def solution(mesh):
    in_specs = (P("wide", "narrow"), P(None, "narrow", "wide"), P(None, "wide", "narrow"), P())
    out_specs = (P("narrow", None, "wide"), P(None, "narrow"))

    def run(inverse, panel, factor_inv, structure):
        fits = (
            mesh.shape["wide"] == 16
            and mesh.shape["narrow"] == 2 == panel.shape[0]
            and panel.shape[2] == 16 * BLK == inverse.shape[0]
        )
        return jax.shard_map(
            per_device_grid if fits else per_device_general,
            mesh=mesh,
            in_specs=in_specs,
            out_specs=out_specs,
            check_vma=False,
        )(inverse, panel, factor_inv, structure)

    return run
```

```python
import jax
import jax.numpy as jnp
from jax import lax
from jax.experimental import pallas as pl
from jax.experimental.pallas import tpu as pltpu
from jax.sharding import PartitionSpec as P

BLK = 256
LANES = 128
ANY = pl.BlockSpec(memory_space=pl.ANY)
VMEM = pl.BlockSpec(memory_space=pltpu.VMEM)
SMEM = pl.BlockSpec(memory_space=pltpu.SMEM)


def spread(value, axis, source):
    kept = jnp.where(lax.axis_index(axis) == source, value, 0).astype(value.dtype)
    return lax.psum(kept, axis)


def block_partial(gathered, inverse, row_inside, col_inside, first_row, row_count):
    local_blocks = inverse.shape[1] // BLK
    running = jnp.zeros((row_count, BLK), jnp.float32)
    for blk_index in range(local_blocks):

        def product(blk_index=blk_index):
            panel_piece = lax.dynamic_slice(
                gathered, (blk_index * BLK, first_row), (BLK, row_count)
            )
            block_z = inverse[:, blk_index * BLK : (blk_index + 1) * BLK]
            return lax.dot_general(
                panel_piece, block_z, (((0,), (1,)), ((), ())), preferred_element_type=jnp.float32
            )

        def skipped():
            return jnp.zeros((row_count, BLK), jnp.float32)

        running = running + lax.cond(row_inside & col_inside[blk_index], product, skipped)
    return -running


def per_device_general(inverse, panel, factor_inv, structure):
    wide_count = lax.axis_size("wide")
    narrow_count = lax.axis_size("narrow")
    nsup_count = panel.shape[0]
    kw_total = panel.shape[2] * wide_count
    kw_local = kw_total // narrow_count
    local_blocks = inverse.shape[1] // BLK
    row_index = lax.axis_index("wide")
    col_first = lax.axis_index("narrow") * local_blocks
    col_ids = col_first + jnp.arange(local_blocks, dtype=jnp.int32)
    row_inside = jnp.any(structure == row_index, axis=1)
    col_inside = jnp.any(structure[:, :, None] == col_ids[None, None, :], axis=1)
    root_index = row_index // local_blocks
    offset = (row_index - root_index * local_blocks) * BLK
    cross_parts = []
    own_parts = []
    for sup_index in range(nsup_count):
        gathered_one = lax.all_gather(panel[sup_index], "wide", axis=1, tiled=True)

        def one_term(first_row, row_count, gathered_one=gathered_one, sup_index=sup_index):
            return block_partial(
                gathered_one,
                inverse,
                row_inside[sup_index],
                col_inside[sup_index],
                first_row,
                row_count,
            )

        cross_parts.append(
            lax.psum_scatter(
                one_term(jnp.int32(0), kw_local * lax.axis_size("narrow")),
                "narrow",
                scatter_dimension=0,
                tiled=True,
            )
        )
        own_parts.append(lax.dynamic_slice_in_dim(gathered_one, offset, BLK, axis=0))
    cross_f = jnp.stack(cross_parts, axis=1)
    own_rows = jnp.stack(own_parts)
    owner_panel = spread(own_rows, "narrow", root_index)
    owner_slice = lax.dynamic_slice_in_dim(
        owner_panel, lax.axis_index("narrow") * kw_local, kw_local, axis=2
    )
    weighted = jnp.einsum("kia,aki->ka", owner_slice.astype(jnp.float32), cross_f)
    linv_part = jnp.sum(jnp.square(factor_inv.astype(jnp.float32)), axis=1)
    variance = lax.psum(linv_part - weighted, "wide")
    return (cross_f.astype(jnp.bfloat16), variance)


X, Y, ZL, ZH = 1, 2, 4, 8
NGRP = 4
SPLIT = 192
TAIL = 16
MIB = 1024 * 1024


def swap_cores(value, name):
    with jax.named_scope(name):
        return lax.ppermute(value, "narrow", [(0, 1), (1, 0)])


def hop(value, mask, name):
    size = lax.axis_size("wide")
    with jax.named_scope(name):
        return lax.ppermute(value, "wide", [(i, i ^ mask) for i in range(size)])


def after(value, *earlier):
    return lax.optimization_barrier((value, *earlier))[0]


def pick(structure_ref, n, j, first):
    nblocks = structure_ref.shape[1]
    start = jnp.where(n == 0, 0, nblocks - first)
    return structure_ref[n, lax.rem(start + j, nblocks)]


def pack_first(structure, panel, inverse, first):
    half_blocks = panel.shape[1] // BLK

    def body(st, panel_ref, inv_ref, out, rest, *pieces):
        n = lax.axis_index("narrow")
        for j in range(first):
            row = pl.multiple_of(lax.rem(pick(st, n, j, first), half_blocks) * BLK, BLK)
            out[j * BLK : (j + 1) * BLK, :] = panel_ref[n, pl.ds(row, BLK), :]
        rest[...] = panel_ref[1 - n]
        pieces[0][...] = inv_ref[:SPLIT, :]
        pieces[1][...] = inv_ref[SPLIT:, :]

    width = inverse.shape[1]
    return pl.pallas_call(
        body,
        out_shape=[
            jax.ShapeDtypeStruct((first * BLK, panel.shape[2]), panel.dtype),
            jax.ShapeDtypeStruct(panel.shape[1:], panel.dtype),
            jax.ShapeDtypeStruct((SPLIT, width), inverse.dtype),
            jax.ShapeDtypeStruct((BLK - SPLIT, width), inverse.dtype),
        ],
        in_specs=[SMEM, VMEM, VMEM],
        out_specs=[VMEM] * 4,
        compiler_params=pltpu.CompilerParams(vmem_limit_bytes=10 * MIB),
        name="pack_first",
    )(structure, panel, inverse)


def pack_rest(structure, panel, other, first):
    nblocks = structure.shape[1]
    half_blocks = panel.shape[1] // BLK

    def body(st, panel_ref, other_ref, out0, out1):
        n = lax.axis_index("narrow")
        for j in range(nblocks - first):
            b = pick(st, n, first + j, first)
            row = pl.multiple_of(lax.rem(b, half_blocks) * BLK, BLK)
            mine = lax.div(b, half_blocks) == n
            rows = slice(j * BLK, (j + 1) * BLK)

            @pl.when(mine)
            def _():
                out0[rows, :] = panel_ref[n, pl.ds(row, BLK), :LANES]
                out1[rows, :] = panel_ref[n, pl.ds(row, BLK), LANES:]

            @pl.when(jnp.logical_not(mine))
            def _():
                out0[rows, :] = other_ref[pl.ds(row, BLK), :LANES]
                out1[rows, :] = other_ref[pl.ds(row, BLK), LANES:]

    shape = jax.ShapeDtypeStruct(((nblocks - first) * BLK, LANES), panel.dtype)
    return pl.pallas_call(
        body,
        out_shape=(shape, shape),
        in_specs=[SMEM, VMEM, VMEM],
        out_specs=[VMEM, VMEM],
        compiler_params=pltpu.CompilerParams(vmem_limit_bytes=8 * MIB),
        name="pack_rest",
    )(structure, panel, other)


def stack_rows(pieces):
    rows = sum(piece.shape[0] for piece in pieces)

    def body(*refs):
        at = 0
        for ref in refs[:-1]:
            refs[-1][at : at + ref.shape[0], :] = ref[...]
            at += ref.shape[0]

    return pl.pallas_call(
        body,
        out_shape=jax.ShapeDtypeStruct((rows, pieces[0].shape[1]), pieces[0].dtype),
        in_specs=[VMEM] * len(pieces),
        out_specs=VMEM,
        compiler_params=pltpu.CompilerParams(vmem_limit_bytes=8 * MIB),
        name="stack_rows",
    )(*pieces)


def pack_inverse(structure, owns, others, first):
    nblocks = structure.shape[1]
    half_blocks = owns[0].shape[1] // BLK
    count = len(owns)
    runs, row = [], 0
    for p, own in enumerate(owns):
        at = 0
        while at < own.shape[0]:
            rows = min(own.shape[0] - at, BLK - row % BLK)
            runs.append((p, at, row // BLK, row % BLK, rows))
            at, row = at + rows, row + rows

    def body(st, *refs):
        out = refs[2 * count]
        n = lax.axis_index("narrow")
        for j in range(nblocks):
            b = pick(st, n, j, first)
            col = pl.multiple_of(lax.rem(b, half_blocks) * BLK, BLK)
            mine = lax.div(b, half_blocks) == n

            def move(sources, j=j, col=col):
                for p, at, d, top, rows in runs:
                    out[d, top : top + rows, j * BLK : (j + 1) * BLK] = sources[p][
                        at : at + rows, pl.ds(col, BLK)
                    ]

            pl.when(mine)(lambda move=move: move(refs[:count]))
            pl.when(jnp.logical_not(mine))(lambda move=move: move(refs[count : 2 * count]))

    return pl.pallas_call(
        body,
        out_shape=jax.ShapeDtypeStruct((NGRP, BLK, nblocks * BLK), owns[0].dtype),
        in_specs=[SMEM] + [VMEM] * (2 * count),
        out_specs=VMEM,
        compiler_params=pltpu.CompilerParams(vmem_limit_bytes=18 * MIB),
        name="pack_inverse",
    )(structure, *owns, *others)


def products(structure, sel, firsts, rests, chunk, near=None):
    nblocks = structure.shape[1]
    early = firsts[0].shape[0]
    first = early // BLK
    spot = slice(chunk * LANES, (chunk + 1) * LANES)

    def body(st, sel_ref, f0, f1, r0, r1, *refs):
        result, total, acc = refs[-3:]
        n = lax.axis_index("narrow")
        w = lax.axis_index("wide")
        x = lax.bitwise_and(w, 1)
        total[...] = jnp.zeros_like(total)
        depth = sel_ref.shape[2]
        rows = sel_ref[...].reshape(NGRP * BLK, depth)
        acc[...] = jnp.dot(
            rows[:, :early],
            jnp.concatenate([f0[:, spot], f1[:, spot]], axis=1),
            preferred_element_type=jnp.float32,
        ) + jnp.dot(
            rows[:, early:],
            jnp.concatenate([r0[...], r1[...]], axis=1),
            preferred_element_type=jnp.float32,
        )
        for d in range(NGRP):
            row = lax.bitwise_xor(w, (d % 2) * Y + (d // 2) * ZL)
            pos = jnp.int32(0)
            inside = jnp.int32(0)
            for j in range(nblocks):
                hit = (pick(st, n, j, first) == row).astype(jnp.int32)
                pos = pos + j * hit
                inside = inside + hit

            @pl.when(inside == 0)
            def _(d=d):
                result[d] = jnp.zeros(result.shape[1:], result.dtype)

            @pl.when(inside > 0)
            def _(d=d, pos=pos):
                for dx in range(2):
                    part = acc[d * BLK : (d + 1) * BLK, dx * LANES : (dx + 1) * LANES]
                    slot = lax.bitwise_xor(x, dx)

                    def weigh(rows, part=part, slot=slot):
                        added = jnp.sum(part * rows.astype(jnp.float32), axis=0, keepdims=True)
                        total[slot] += added

                    @pl.when(pos < first)
                    def _():
                        at = pl.multiple_of(pos * BLK, BLK)
                        weigh((f0, f1)[dx][pl.ds(at, BLK), spot])

                    @pl.when(pos >= first)
                    def _():
                        at = pl.multiple_of((pos - first) * BLK, BLK)
                        weigh((r0, r1)[dx][pl.ds(at, BLK), :])

                    at = pl.multiple_of(slot * LANES, LANES)
                    result[d, pl.ds(at, LANES), :] = (-part).T.astype(result.dtype)

        for slot in range(2):
            left, terms = total[slot], []
            for _ in range(3):
                term = left.astype(result.dtype).astype(jnp.float32)
                terms.append(term)
                left = left - term
            tile = jnp.concatenate(terms + [jnp.zeros((TAIL - 3, LANES), jnp.float32)], axis=0)
            for d in range(NGRP):
                result[d, 2 * LANES :, slot * LANES : (slot + 1) * LANES] = tile.astype(
                    result.dtype
                )
        if near is None:
            refs[0][...] = result[...]
            return
        near_ref, kept, sent = refs[:3]
        stay = n == lax.div(w, ZH)

        @pl.when(stay)
        def _():
            kept[...] = near_ref[...]
            sent[...] = result[...]

        @pl.when(jnp.logical_not(stay))
        def _():
            kept[...] = result[...]
            sent[...] = near_ref[...]

    out = jax.ShapeDtypeStruct((NGRP, 2 * LANES + TAIL, BLK), sel.dtype)
    again = () if near is None else (near,)
    return pl.pallas_call(
        body,
        out_shape=out if near is None else [out, out],
        in_specs=[SMEM] + [VMEM] * (5 + len(again)),
        out_specs=VMEM if near is None else [VMEM, VMEM],
        scratch_shapes=[
            pltpu.VMEM(out.shape, out.dtype),
            pltpu.VMEM((2, 1, LANES), jnp.float32),
            pltpu.VMEM((NGRP * BLK, 2 * LANES), jnp.float32),
        ],
        compiler_params=pltpu.CompilerParams(vmem_limit_bytes=16 * MIB),
        cost_estimate=pl.CostEstimate(flops=0, bytes_accessed=0, transcendentals=0),
        name="products",
    )(structure, sel, *firsts, *rests, *again)


def bundle(kept, back):
    def body(kept_ref, back_ref, *outs):
        for d, out in enumerate(outs):
            out[0] = kept_ref[d]
            out[1] = back_ref[d]

    shape = jax.ShapeDtypeStruct((2, *kept.shape[1:]), kept.dtype)
    return pl.pallas_call(
        body,
        out_shape=[shape] * NGRP,
        in_specs=[VMEM, VMEM],
        out_specs=[VMEM] * NGRP,
        compiler_params=pltpu.CompilerParams(vmem_limit_bytes=8 * MIB),
        name="bundle",
    )(kept, back)


def squares(factor_inv):
    sups, rows, cols = factor_inv.shape
    half = cols // 2

    def body(in_ref, out_ref):
        for k in range(sups):
            value = in_ref[k].astype(jnp.float32)
            out_ref[k : k + 1, :] = jnp.sum(value * value, axis=0, keepdims=True)

    return pl.pallas_call(
        body,
        out_shape=jax.ShapeDtypeStruct((sups, cols), jnp.float32),
        grid=(2,),
        in_specs=[pl.BlockSpec((sups, rows, half), lambda c: (0, 0, c))],
        out_specs=pl.BlockSpec((sups, half), lambda c: (0, c)),
        compiler_params=pltpu.CompilerParams(vmem_limit_bytes=8 * MIB),
        name="squares",
    )(factor_inv)


def add_sums(base, messages, chunk):
    cols = base.shape[1]

    def body(base_ref, *refs):
        out = refs[-1]
        n = lax.axis_index("narrow")
        group = lax.rem(lax.div(lax.axis_index("wide"), Y), NGRP)
        out[...] = base_ref[...]
        for d in range(NGRP):
            source = lax.bitwise_xor(group, d)
            for k in range(2):
                which = (n != k).astype(jnp.int32)
                tile = refs[d][which, 2 * LANES :, :].astype(jnp.float32)
                value = tile[0:1] + (tile[1:2] + tile[2:3])
                for xx in range(2):
                    at = source * (cols // NGRP) + (2 * xx + chunk) * LANES
                    spot = pl.ds(pl.multiple_of(at, LANES), LANES)
                    out[k : k + 1, spot] += value[:, xx * LANES : (xx + 1) * LANES]

    return pl.pallas_call(
        body,
        out_shape=jax.ShapeDtypeStruct(base.shape, jnp.float32),
        in_specs=[VMEM] * (1 + NGRP),
        out_specs=VMEM,
        compiler_params=pltpu.CompilerParams(vmem_limit_bytes=4 * MIB),
        name="add_sums",
    )(base, *messages)


def assemble(messages, chunk, held):
    tall = 4 * LANES
    rows_total = 2 * 2 * NGRP * tall

    def body(*refs):
        msg_refs = refs[:NGRP]
        out, wide_buf, narrow_buf, sem = refs[-4:]
        n = lax.axis_index("narrow")
        w = lax.axis_index("wide")
        copies = []
        for d in range(NGRP):
            source = lax.bitwise_xor(lax.rem(lax.div(w, Y), NGRP), d)
            for xx in range(2):
                slot = 2 * d + xx
                for k in range(2):
                    which = (n != k).astype(jnp.int32)
                    value = msg_refs[d][which, xx * LANES : (xx + 1) * LANES, :].astype(
                        jnp.float32
                    )
                    for lt in range(2):
                        wide_buf[slot, pl.ds(2 * lt + k, LANES, stride=4), :] = value[
                            :, lt * LANES : (lt + 1) * LANES
                        ]
                narrow_buf[slot] = wide_buf[slot].astype(narrow_buf.dtype)
                row = pl.multiple_of(((source * 2 + xx) * 2 + chunk) * tall, tall)
                copy = pltpu.make_async_copy(
                    narrow_buf.at[slot], out.at[pl.ds(row, tall), :], sem.at[slot]
                )
                copy.start()
                copies.append(copy)
        for copy in copies:
            copy.wait()

    extra = () if held is None else (held,)
    return pl.pallas_call(
        body,
        out_shape=jax.ShapeDtypeStruct((rows_total, LANES), messages[0].dtype),
        in_specs=[VMEM] * NGRP + [ANY] * len(extra),
        out_specs=ANY,
        scratch_shapes=[
            pltpu.VMEM((2 * NGRP, tall, LANES), jnp.float32),
            pltpu.VMEM((2 * NGRP, tall, LANES), messages[0].dtype),
            pltpu.SemaphoreType.DMA((2 * NGRP,)),
        ],
        input_output_aliases={NGRP: 0} if extra else {},
        compiler_params=pltpu.CompilerParams(vmem_limit_bytes=8 * MIB),
        name="assemble",
    )(*messages, *extra)


def per_device_grid(inverse, panel, factor_inv, structure):
    first = structure.shape[1] - panel.shape[1] // BLK
    size = lax.axis_size("wide")
    f_own, other, top, bottom = pack_first(structure, panel, inverse, first)
    other = swap_cores(other, "panel_swap")
    r_own = pack_rest(structure, panel, other, first)
    linv = squares(factor_inv)
    f_z = hop(f_own, ZH, "first_z")
    f_x = hop(f_own, X, "first_x")
    a_z0 = hop(top, ZL, "inv_z0")
    a_y = hop(inverse, Y, "inv_y")
    a_y, a_z0, f_z, f_x, *r_own = lax.optimization_barrier((a_y, a_z0, f_z, f_x, *r_own))
    r_z0 = hop(r_own[0], ZH, "rest0_z")
    a_z1 = hop(after(bottom, f_z), ZL, "inv_z1")
    f_xz = hop(f_z, X, "first_xz")
    r_x0 = hop(r_own[0], X, "rest0_x")
    a_yz0 = hop(a_z0, Y, "inv_yz0")
    a_yz1 = hop(a_z1, Y, "inv_yz1")
    most = stack_rows([inverse, a_y, a_z0])
    r_z0, r_x0, f_xz, a_z1, a_yz0, a_yz1, most, *r_own = lax.optimization_barrier(
        (r_z0, r_x0, f_xz, a_z1, a_yz0, a_yz1, most, *r_own)
    )
    r_z1 = hop(r_own[1], ZH, "rest1_z")
    r_xz0 = hop(r_z0, X, "rest0_xz")
    r_x1 = hop(r_own[1], X, "rest1_x")
    more = stack_rows([a_z1, a_yz0, a_yz1])
    s_most = swap_cores(most, "inv_swap")
    s_more = swap_cores(more, "inv_swap_more")
    sel = pack_inverse(structure, (most, more), (s_most, s_more), first)
    linv = after(linv, more)
    for mask in (Y, ZL):
        linv = linv + hop(linv, mask, f"squares_{mask}")
    r_z1, r_x1, linv = lax.optimization_barrier((r_z1, r_x1, linv))

    def deliver(kept, sent, c):
        messages = bundle(kept, swap_cores(sent, f"cross{c}_swap"))
        hops = {
            d: hop(messages[d], (d % 2) * Y + (d // 2) * ZL, f"cross{c}_{d}") for d in (3, 1, 2)
        }
        return [messages[0]] + [hops[d] for d in range(1, NGRP)]

    near = products(structure, sel, (f_own, f_x), (r_own[0], r_x0), 0)
    kept, sent = products(structure, sel, (f_z, f_xz), (r_z0, r_xz0), 0, near)
    messages = deliver(kept, sent, 0)
    r_xz1 = hop(r_z1, X, "rest1_xz")
    near = products(structure, sel, (f_own, f_x), (r_own[1], r_x1), 1)
    r_xz1, *messages = lax.optimization_barrier((r_xz1, *messages))
    kept, sent = products(structure, sel, (f_z, f_xz), (r_z1, r_xz1), 1, near)
    held = assemble(messages, 0, None)
    variance = add_sums(linv, messages, 0)
    messages = deliver(kept, sent, 1)
    variance = add_sums(variance, messages, 1)
    held = assemble(messages, 1, held)
    hops = [hop(variance, mask, f"variance_{mask}") for mask in (X, ZH, X | ZH)]
    variance = variance + hops[0] + hops[1] + hops[2]
    half = panel.shape[2] * size // 2
    cross = held.reshape(half, 2, 2, LANES).transpose(0, 2, 1, 3).reshape(half, 2, BLK)
    return cross, variance


def solution(mesh):
    in_specs = (P("wide", "narrow"), P(None, "narrow", "wide"), P(None, "wide", "narrow"), P())
    out_specs = (P("narrow", None, "wide"), P(None, "narrow"))

    def run(inverse, panel, factor_inv, structure):
        fits = (
            mesh.shape["wide"] == 16
            and mesh.shape["narrow"] == 2 == panel.shape[0]
            and panel.shape[2] == 16 * BLK == inverse.shape[0]
        )
        return jax.shard_map(
            per_device_grid if fits else per_device_general,
            mesh=mesh,
            in_specs=in_specs,
            out_specs=out_specs,
            check_vma=False,
        )(inverse, panel, factor_inv, structure)

    return run
```

```python
import jax
import jax.numpy as jnp
from jax import lax
from jax.experimental import pallas as pl
from jax.experimental.pallas import tpu as pltpu
from jax.sharding import PartitionSpec as P

BLK = 256
LANES = 128
ANY = pl.BlockSpec(memory_space=pl.ANY)
VMEM = pl.BlockSpec(memory_space=pltpu.VMEM)
SMEM = pl.BlockSpec(memory_space=pltpu.SMEM)


def spread(value, axis, source):
    kept = jnp.where(lax.axis_index(axis) == source, value, 0).astype(value.dtype)
    return lax.psum(kept, axis)


def block_partial(gathered, inverse, row_inside, col_inside, first_row, row_count):
    local_blocks = inverse.shape[1] // BLK
    running = jnp.zeros((row_count, BLK), jnp.float32)
    for blk_index in range(local_blocks):

        def product(blk_index=blk_index):
            panel_piece = lax.dynamic_slice(
                gathered, (blk_index * BLK, first_row), (BLK, row_count)
            )
            block_z = inverse[:, blk_index * BLK : (blk_index + 1) * BLK]
            return lax.dot_general(
                panel_piece, block_z, (((0,), (1,)), ((), ())), preferred_element_type=jnp.float32
            )

        def skipped():
            return jnp.zeros((row_count, BLK), jnp.float32)

        running = running + lax.cond(row_inside & col_inside[blk_index], product, skipped)
    return -running


def per_device_general(inverse, panel, factor_inv, structure):
    wide_count = lax.axis_size("wide")
    narrow_count = lax.axis_size("narrow")
    nsup_count = panel.shape[0]
    kw_total = panel.shape[2] * wide_count
    kw_local = kw_total // narrow_count
    local_blocks = inverse.shape[1] // BLK
    row_index = lax.axis_index("wide")
    col_first = lax.axis_index("narrow") * local_blocks
    col_ids = col_first + jnp.arange(local_blocks, dtype=jnp.int32)
    row_inside = jnp.any(structure == row_index, axis=1)
    col_inside = jnp.any(structure[:, :, None] == col_ids[None, None, :], axis=1)
    root_index = row_index // local_blocks
    offset = (row_index - root_index * local_blocks) * BLK
    cross_parts = []
    own_parts = []
    for sup_index in range(nsup_count):
        gathered_one = lax.all_gather(panel[sup_index], "wide", axis=1, tiled=True)

        def one_term(first_row, row_count, gathered_one=gathered_one, sup_index=sup_index):
            return block_partial(
                gathered_one,
                inverse,
                row_inside[sup_index],
                col_inside[sup_index],
                first_row,
                row_count,
            )

        cross_parts.append(
            lax.psum_scatter(
                one_term(jnp.int32(0), kw_local * lax.axis_size("narrow")),
                "narrow",
                scatter_dimension=0,
                tiled=True,
            )
        )
        own_parts.append(lax.dynamic_slice_in_dim(gathered_one, offset, BLK, axis=0))
    cross_f = jnp.stack(cross_parts, axis=1)
    own_rows = jnp.stack(own_parts)
    owner_panel = spread(own_rows, "narrow", root_index)
    owner_slice = lax.dynamic_slice_in_dim(
        owner_panel, lax.axis_index("narrow") * kw_local, kw_local, axis=2
    )
    weighted = jnp.einsum("kia,aki->ka", owner_slice.astype(jnp.float32), cross_f)
    linv_part = jnp.sum(jnp.square(factor_inv.astype(jnp.float32)), axis=1)
    variance = lax.psum(linv_part - weighted, "wide")
    return (cross_f.astype(jnp.bfloat16), variance)


X, Y, ZL, ZH = 1, 2, 4, 8
NGRP = 4
SPLIT = 192
TAIL = 16
DEST = (0, 3, 1, 2)
MIB = 1024 * 1024


def swap_cores(value, name):
    with jax.named_scope(name):
        return lax.ppermute(value, "narrow", [(0, 1), (1, 0)])


def hop(value, mask, name):
    size = lax.axis_size("wide")
    with jax.named_scope(name):
        return lax.ppermute(value, "wide", [(i, i ^ mask) for i in range(size)])


def after(value, *earlier):
    return lax.optimization_barrier((value, *earlier))[0]


def pick(structure_ref, n, j, first):
    nblocks = structure_ref.shape[1]
    start = jnp.where(n == 0, 0, nblocks - first)
    return structure_ref[n, lax.rem(start + j, nblocks)]


def pack_first(structure, panel, inverse, first):
    half_blocks = panel.shape[1] // BLK

    def body(st, panel_ref, inv_ref, out, *pieces):
        n = lax.axis_index("narrow")
        for j in range(first):
            row = pl.multiple_of(lax.rem(pick(st, n, j, first), half_blocks) * BLK, BLK)
            out[j * BLK : (j + 1) * BLK, :] = panel_ref[n, pl.ds(row, BLK), :]
        pieces[0][...] = inv_ref[:SPLIT, :]
        pieces[1][...] = inv_ref[SPLIT:, :]

    width = inverse.shape[1]
    return pl.pallas_call(
        body,
        out_shape=[
            jax.ShapeDtypeStruct((first * BLK, panel.shape[2]), panel.dtype),
            jax.ShapeDtypeStruct((SPLIT, width), inverse.dtype),
            jax.ShapeDtypeStruct((BLK - SPLIT, width), inverse.dtype),
        ],
        in_specs=[SMEM, VMEM, VMEM],
        out_specs=[VMEM] * 3,
        compiler_params=pltpu.CompilerParams(vmem_limit_bytes=8 * MIB),
        name="pack_first",
    )(structure, panel, inverse)


def pack_rest(structure, panel, other, first):
    nblocks = structure.shape[1]
    half_blocks = panel.shape[1] // BLK

    def body(st, panel_ref, other_ref, out0, out1):
        n = lax.axis_index("narrow")
        out0[(nblocks - first) * BLK :, :] = jnp.zeros((TAIL, LANES), out0.dtype)
        for j in range(nblocks - first):
            b = pick(st, n, first + j, first)
            row = pl.multiple_of(lax.rem(b, half_blocks) * BLK, BLK)
            mine = lax.div(b, half_blocks) == n
            rows = slice(j * BLK, (j + 1) * BLK)

            @pl.when(mine)
            def _():
                out0[rows, :] = panel_ref[n, pl.ds(row, BLK), :LANES]
                out1[rows, :] = panel_ref[n, pl.ds(row, BLK), LANES:]

            @pl.when(jnp.logical_not(mine))
            def _():
                out0[rows, :] = other_ref[pl.ds(row, BLK), :LANES]
                out1[rows, :] = other_ref[pl.ds(row, BLK), LANES:]

    rows = (nblocks - first) * BLK
    return pl.pallas_call(
        body,
        out_shape=(
            jax.ShapeDtypeStruct((rows + TAIL, LANES), panel.dtype),
            jax.ShapeDtypeStruct((rows, LANES), panel.dtype),
        ),
        in_specs=[SMEM, VMEM, VMEM],
        out_specs=[VMEM, VMEM],
        compiler_params=pltpu.CompilerParams(vmem_limit_bytes=8 * MIB),
        name="pack_rest",
    )(structure, panel, other)


def stack_rows(pieces):
    rows = sum(piece.shape[0] for piece in pieces)

    def body(*refs):
        at = 0
        for ref in refs[:-1]:
            refs[-1][at : at + ref.shape[0], :] = ref[...]
            at += ref.shape[0]

    return pl.pallas_call(
        body,
        out_shape=jax.ShapeDtypeStruct((rows, pieces[0].shape[1]), pieces[0].dtype),
        in_specs=[VMEM] * len(pieces),
        out_specs=VMEM,
        compiler_params=pltpu.CompilerParams(vmem_limit_bytes=8 * MIB),
        name="stack_rows",
    )(*pieces)


def pack_inverse(structure, owns, others, first):
    nblocks = structure.shape[1]
    half_blocks = owns[0].shape[1] // BLK
    count = len(owns)
    runs, row = [], 0
    for p, own in enumerate(owns):
        at = 0
        while at < own.shape[0]:
            rows = min(own.shape[0] - at, BLK - row % BLK)
            runs.append((p, at, row // BLK, row % BLK, rows))
            at, row = at + rows, row + rows

    def body(st, *refs):
        out = refs[2 * count]
        n = lax.axis_index("narrow")
        for j in range(nblocks):
            b = pick(st, n, j, first)
            col = pl.multiple_of(lax.rem(b, half_blocks) * BLK, BLK)
            mine = lax.div(b, half_blocks) == n

            def move(sources, j=j, col=col):
                for p, at, d, top, rows in runs:
                    out[d, top : top + rows, j * BLK : (j + 1) * BLK] = sources[p][
                        at : at + rows, pl.ds(col, BLK)
                    ]

            pl.when(mine)(lambda move=move: move(refs[:count]))
            pl.when(jnp.logical_not(mine))(lambda move=move: move(refs[count : 2 * count]))

    return pl.pallas_call(
        body,
        out_shape=jax.ShapeDtypeStruct((NGRP, BLK, nblocks * BLK), owns[0].dtype),
        in_specs=[SMEM] + [VMEM] * (2 * count),
        out_specs=VMEM,
        compiler_params=pltpu.CompilerParams(vmem_limit_bytes=18 * MIB),
        name="pack_inverse",
    )(structure, *owns, *others)


def products(structure, sel, firsts, rests, chunk, near=None):
    nblocks = structure.shape[1]
    early = firsts[0].shape[0]
    late = sel.shape[2] - early
    first = early // BLK
    spot = slice(chunk * LANES, (chunk + 1) * LANES)

    def body(st, sel_ref, f0, f1, r0, r1, *refs):
        result, total, acc = refs[-3:]
        n = lax.axis_index("narrow")
        w = lax.axis_index("wide")
        x = lax.bitwise_and(w, 1)
        total[...] = jnp.zeros_like(total)
        depth = sel_ref.shape[2]
        rows = sel_ref[...].reshape(NGRP * BLK, depth)
        acc[...] = jnp.dot(
            rows[:, :early],
            jnp.concatenate([f0[:, spot], f1[:, spot]], axis=1),
            preferred_element_type=jnp.float32,
        ) + jnp.dot(
            rows[:, early:],
            jnp.concatenate([r0[:late, :], r1[:late, :]], axis=1),
            preferred_element_type=jnp.float32,
        )
        for d in range(NGRP):
            row = lax.bitwise_xor(w, (d % 2) * Y + (d // 2) * ZL)
            pos = jnp.int32(0)
            inside = jnp.int32(0)
            for j in range(nblocks):
                hit = (pick(st, n, j, first) == row).astype(jnp.int32)
                pos = pos + j * hit
                inside = inside + hit

            @pl.when(inside == 0)
            def _(d=d):
                result[d] = jnp.zeros(result.shape[1:], result.dtype)

            @pl.when(inside > 0)
            def _(d=d, pos=pos):
                for dx in range(2):
                    part = acc[d * BLK : (d + 1) * BLK, dx * LANES : (dx + 1) * LANES]
                    slot = lax.bitwise_xor(x, dx)

                    def weigh(rows, part=part, slot=slot):
                        added = jnp.sum(part * rows.astype(jnp.float32), axis=0, keepdims=True)
                        total[slot] += added

                    @pl.when(pos < first)
                    def _():
                        at = pl.multiple_of(pos * BLK, BLK)
                        weigh((f0, f1)[dx][pl.ds(at, BLK), spot])

                    @pl.when(pos >= first)
                    def _():
                        at = pl.multiple_of((pos - first) * BLK, BLK)
                        weigh((r0, r1)[dx][pl.ds(at, BLK), :])

                    at = pl.multiple_of(slot * LANES, LANES)
                    result[d, pl.ds(at, LANES), :] = (-part).T.astype(result.dtype)

        for slot in range(2):
            left, terms = total[slot], []
            for _ in range(3):
                term = left.astype(result.dtype).astype(jnp.float32)
                terms.append(term)
                left = left - term
            tile = jnp.concatenate(terms + [jnp.zeros((TAIL - 3, LANES), jnp.float32)], axis=0)
            for d in range(NGRP):
                result[d, 2 * LANES :, slot * LANES : (slot + 1) * LANES] = tile.astype(
                    result.dtype
                )
        if near is None:
            refs[0][...] = result[...]
            return
        near_ref, kept, sent = refs[:3]
        stay = n == lax.div(w, ZH)

        @pl.when(stay)
        def _():
            kept[...] = near_ref[...]
            sent[...] = result[...]

        @pl.when(jnp.logical_not(stay))
        def _():
            kept[...] = result[...]
            sent[...] = near_ref[...]

    out = jax.ShapeDtypeStruct((NGRP, 2 * LANES + TAIL, BLK), sel.dtype)
    again = () if near is None else (near,)
    return pl.pallas_call(
        body,
        out_shape=out if near is None else [out, out],
        in_specs=[SMEM] + [VMEM] * (5 + len(again)),
        out_specs=VMEM if near is None else [VMEM, VMEM],
        scratch_shapes=[
            pltpu.VMEM(out.shape, out.dtype),
            pltpu.VMEM((2, 1, LANES), jnp.float32),
            pltpu.VMEM((NGRP * BLK, 2 * LANES), jnp.float32),
        ],
        compiler_params=pltpu.CompilerParams(vmem_limit_bytes=16 * MIB),
        cost_estimate=pl.CostEstimate(flops=0, bytes_accessed=0, transcendentals=0),
        name="products",
    )(structure, sel, *firsts, *rests, *again)


def bundle(ours, theirs):
    def body(our_ref, their_ref, *outs):
        for d, out in zip(DEST, outs):
            out[0] = our_ref[d]
            out[1] = their_ref[d]

    shape = jax.ShapeDtypeStruct((2, *ours.shape[1:]), ours.dtype)
    return pl.pallas_call(
        body,
        out_shape=[shape] * NGRP,
        in_specs=[VMEM, VMEM],
        out_specs=[VMEM] * NGRP,
        compiler_params=pltpu.CompilerParams(vmem_limit_bytes=8 * MIB),
        name="bundle",
    )(ours, theirs)


def squares(factor_inv):
    sups, rows, cols = factor_inv.shape
    half = cols // 2

    def body(in_ref, out_ref):
        for k in range(sups):
            value = in_ref[k].astype(jnp.float32)
            out_ref[k : k + 1, :] = jnp.sum(value * value, axis=0, keepdims=True)

    return pl.pallas_call(
        body,
        out_shape=jax.ShapeDtypeStruct((sups, cols), jnp.float32),
        grid=(2,),
        in_specs=[pl.BlockSpec((sups, rows, half), lambda c: (0, 0, c))],
        out_specs=pl.BlockSpec((sups, half), lambda c: (0, c)),
        compiler_params=pltpu.CompilerParams(vmem_limit_bytes=8 * MIB),
        name="squares",
    )(factor_inv)


def add_sums(base, messages, chunk):
    cols = base.shape[1]

    def body(base_ref, *refs):
        out = refs[-1]
        n = lax.axis_index("narrow")
        group = lax.rem(lax.div(lax.axis_index("wide"), Y), NGRP)
        out[...] = base_ref[...]
        for d, ref in zip(DEST, refs):
            source = lax.bitwise_xor(group, d)
            for k in range(2):
                which = (n != k).astype(jnp.int32)
                tile = ref[which, 2 * LANES :, :].astype(jnp.float32)
                value = tile[0:1] + (tile[1:2] + tile[2:3])
                for xx in range(2):
                    at = source * (cols // NGRP) + (2 * xx + chunk) * LANES
                    spot = pl.ds(pl.multiple_of(at, LANES), LANES)
                    out[k : k + 1, spot] += value[:, xx * LANES : (xx + 1) * LANES]

    return pl.pallas_call(
        body,
        out_shape=jax.ShapeDtypeStruct(base.shape, jnp.float32),
        in_specs=[VMEM] * (1 + NGRP),
        out_specs=VMEM,
        compiler_params=pltpu.CompilerParams(vmem_limit_bytes=4 * MIB),
        name="add_sums",
    )(base, *messages)


def assemble(messages, chunk, held):
    tall = 4 * LANES
    rows_total = 2 * 2 * NGRP * tall

    def body(*refs):
        msg_refs = refs[:NGRP]
        out, wide_buf, narrow_buf, sem = refs[-4:]
        n = lax.axis_index("narrow")
        w = lax.axis_index("wide")
        copies = []
        for d, msg_ref in zip(DEST, msg_refs):
            source = lax.bitwise_xor(lax.rem(lax.div(w, Y), NGRP), d)
            for xx in range(2):
                slot = 2 * d + xx
                for k in range(2):
                    which = (n != k).astype(jnp.int32)
                    value = msg_ref[which, xx * LANES : (xx + 1) * LANES, :].astype(
                        jnp.float32
                    )
                    for lt in range(2):
                        wide_buf[slot, pl.ds(2 * lt + k, LANES, stride=4), :] = value[
                            :, lt * LANES : (lt + 1) * LANES
                        ]
                narrow_buf[slot] = wide_buf[slot].astype(narrow_buf.dtype)
                row = pl.multiple_of(((source * 2 + xx) * 2 + chunk) * tall, tall)
                copy = pltpu.make_async_copy(
                    narrow_buf.at[slot], out.at[pl.ds(row, tall), :], sem.at[slot]
                )
                copy.start()
                copies.append(copy)
        for copy in copies:
            copy.wait()

    extra = () if held is None else (held,)
    return pl.pallas_call(
        body,
        out_shape=jax.ShapeDtypeStruct((rows_total, LANES), messages[0].dtype),
        in_specs=[VMEM] * NGRP + [ANY] * len(extra),
        out_specs=ANY,
        scratch_shapes=[
            pltpu.VMEM((2 * NGRP, tall, LANES), jnp.float32),
            pltpu.VMEM((2 * NGRP, tall, LANES), messages[0].dtype),
            pltpu.SemaphoreType.DMA((2 * NGRP,)),
        ],
        input_output_aliases={NGRP: 0} if extra else {},
        compiler_params=pltpu.CompilerParams(vmem_limit_bytes=8 * MIB),
        name="assemble",
    )(*messages, *extra)


def per_device_grid(inverse, panel, factor_inv, structure):
    first = structure.shape[1] - panel.shape[1] // BLK
    size = lax.axis_size("wide")
    n = lax.axis_index("narrow")
    f_own, top, bottom = pack_first(structure, panel, inverse, first)
    other = swap_cores(lax.dynamic_index_in_dim(panel, 1 - n, 0, keepdims=False), "panel_swap")
    r_own = pack_rest(structure, panel, other, first)
    linv = squares(factor_inv)
    f_z = hop(f_own, ZH, "first_z")
    f_x = hop(f_own, X, "first_x")
    a_z0 = hop(top, ZL, "inv_z0")
    a_y = hop(inverse, Y, "inv_y")
    a_y, f_z, f_x, *r_own = lax.optimization_barrier((a_y, f_z, f_x, *r_own))
    r_z0 = hop(r_own[0], ZH, "rest0_z")
    a_z1 = hop(after(bottom, f_z), ZL, "inv_z1")
    f_xz = hop(f_z, X, "first_xz")
    r_x0 = hop(r_own[0], X, "rest0_x")
    a_yz0 = hop(a_z0, Y, "inv_yz0")
    a_yz1 = hop(a_z1, Y, "inv_yz1")
    most = stack_rows([inverse, a_y, a_z0])
    r_z0, r_x0, f_xz, a_z1, a_yz0, a_yz1, most, *r_own = lax.optimization_barrier(
        (r_z0, r_x0, f_xz, a_z1, a_yz0, a_yz1, most, *r_own)
    )
    r_z1 = hop(r_own[1], ZH, "rest1_z")
    r_xz0 = hop(r_z0, X, "rest0_xz")
    r_x1 = hop(r_own[1], X, "rest1_x")
    more = stack_rows([a_z1, a_yz0, a_yz1])
    s_most = swap_cores(most, "inv_swap")
    s_more = swap_cores(more, "inv_swap_more")
    sel = pack_inverse(structure, (most, more), (s_most, s_more), first)
    linv = after(linv, more)
    for mask in (Y, ZL):
        linv = linv + hop(linv, mask, f"squares_{mask}")
    r_z1, r_x1, linv = lax.optimization_barrier((r_z1, r_x1, linv))

    def deliver(kept, sent, c):
        messages = bundle(kept, swap_cores(sent, f"cross{c}_swap"))
        return [messages[0]] + [
            hop(message, (d % 2) * Y + (d // 2) * ZL, f"cross{c}_{d}")
            for d, message in zip(DEST[1:], messages[1:])
        ]

    near = products(structure, sel, (f_own, f_x), (r_own[0], r_x0), 0)
    kept, sent = products(structure, sel, (f_z, f_xz), (r_z0, r_xz0), 0, near)
    messages = deliver(kept, sent, 0)
    r_xz1 = hop(r_z1, X, "rest1_xz")
    near = products(structure, sel, (f_own, f_x), (r_own[1], r_x1), 1)
    r_xz1, *messages = lax.optimization_barrier((r_xz1, *messages))
    kept, sent = products(structure, sel, (f_z, f_xz), (r_z1, r_xz1), 1, near)
    held = assemble(messages, 0, None)
    variance = add_sums(linv, messages, 0)
    messages = deliver(kept, sent, 1)
    variance = add_sums(variance, messages, 1)
    held = assemble(messages, 1, held)
    hops = [hop(variance, mask, f"variance_{mask}") for mask in (X, ZH, X | ZH)]
    variance = variance + hops[0] + hops[1] + hops[2]
    half = panel.shape[2] * size // 2
    cross = held.reshape(half, 2, 2, LANES).transpose(0, 2, 1, 3).reshape(half, 2, BLK)
    return cross, variance


def solution(mesh):
    in_specs = (P("wide", "narrow"), P(None, "narrow", "wide"), P(None, "wide", "narrow"), P())
    out_specs = (P("narrow", None, "wide"), P(None, "narrow"))

    def run(inverse, panel, factor_inv, structure):
        fits = (
            mesh.shape["wide"] == 16
            and mesh.shape["narrow"] == 2 == panel.shape[0]
            and panel.shape[2] == 16 * BLK == inverse.shape[0]
        )
        return jax.shard_map(
            per_device_grid if fits else per_device_general,
            mesh=mesh,
            in_specs=in_specs,
            out_specs=out_specs,
            check_vma=False,
        )(inverse, panel, factor_inv, structure)

    return run
```

```python
import jax
import jax.numpy as jnp
from jax import lax
from jax.experimental import pallas as pl
from jax.experimental.pallas import tpu as pltpu
from jax.sharding import PartitionSpec as P

BLK = 256
LANES = 128
ANY = pl.BlockSpec(memory_space=pl.ANY)
VMEM = pl.BlockSpec(memory_space=pltpu.VMEM)
SMEM = pl.BlockSpec(memory_space=pltpu.SMEM)


def spread(value, axis, source):
    kept = jnp.where(lax.axis_index(axis) == source, value, 0).astype(value.dtype)
    return lax.psum(kept, axis)


def block_partial(gathered, inverse, row_inside, col_inside, first_row, row_count):
    local_blocks = inverse.shape[1] // BLK
    running = jnp.zeros((row_count, BLK), jnp.float32)
    for blk_index in range(local_blocks):

        def product(blk_index=blk_index):
            panel_piece = lax.dynamic_slice(
                gathered, (blk_index * BLK, first_row), (BLK, row_count)
            )
            block_z = inverse[:, blk_index * BLK : (blk_index + 1) * BLK]
            return lax.dot_general(
                panel_piece, block_z, (((0,), (1,)), ((), ())), preferred_element_type=jnp.float32
            )

        def skipped():
            return jnp.zeros((row_count, BLK), jnp.float32)

        running = running + lax.cond(row_inside & col_inside[blk_index], product, skipped)
    return -running


def per_device_general(inverse, panel, factor_inv, structure):
    wide_count = lax.axis_size("wide")
    narrow_count = lax.axis_size("narrow")
    nsup_count = panel.shape[0]
    kw_total = panel.shape[2] * wide_count
    kw_local = kw_total // narrow_count
    local_blocks = inverse.shape[1] // BLK
    row_index = lax.axis_index("wide")
    col_first = lax.axis_index("narrow") * local_blocks
    col_ids = col_first + jnp.arange(local_blocks, dtype=jnp.int32)
    row_inside = jnp.any(structure == row_index, axis=1)
    col_inside = jnp.any(structure[:, :, None] == col_ids[None, None, :], axis=1)
    root_index = row_index // local_blocks
    offset = (row_index - root_index * local_blocks) * BLK
    cross_parts = []
    own_parts = []
    for sup_index in range(nsup_count):
        gathered_one = lax.all_gather(panel[sup_index], "wide", axis=1, tiled=True)

        def one_term(first_row, row_count, gathered_one=gathered_one, sup_index=sup_index):
            return block_partial(
                gathered_one,
                inverse,
                row_inside[sup_index],
                col_inside[sup_index],
                first_row,
                row_count,
            )

        cross_parts.append(
            lax.psum_scatter(
                one_term(jnp.int32(0), kw_local * lax.axis_size("narrow")),
                "narrow",
                scatter_dimension=0,
                tiled=True,
            )
        )
        own_parts.append(lax.dynamic_slice_in_dim(gathered_one, offset, BLK, axis=0))
    cross_f = jnp.stack(cross_parts, axis=1)
    own_rows = jnp.stack(own_parts)
    owner_panel = spread(own_rows, "narrow", root_index)
    owner_slice = lax.dynamic_slice_in_dim(
        owner_panel, lax.axis_index("narrow") * kw_local, kw_local, axis=2
    )
    weighted = jnp.einsum("kia,aki->ka", owner_slice.astype(jnp.float32), cross_f)
    linv_part = jnp.sum(jnp.square(factor_inv.astype(jnp.float32)), axis=1)
    variance = lax.psum(linv_part - weighted, "wide")
    return (cross_f.astype(jnp.bfloat16), variance)


X, Y, ZL, ZH = 1, 2, 4, 8
NGRP = 4
SPLIT = 192
TAIL = 16
DEST = (0, 3, 1, 2)
MIB = 1024 * 1024


def swap_cores(value, name):
    with jax.named_scope(name):
        return lax.ppermute(value, "narrow", [(0, 1), (1, 0)])


def hop(value, mask, name):
    size = lax.axis_size("wide")
    with jax.named_scope(name):
        return lax.ppermute(value, "wide", [(i, i ^ mask) for i in range(size)])


def after(value, *earlier):
    return lax.optimization_barrier((value, *earlier))[0]


def lead(values, micros):
    def body(*refs):
        pass

    return pl.pallas_call(
        body,
        out_shape=[jax.ShapeDtypeStruct(v.shape, v.dtype) for v in values],
        in_specs=[ANY] * len(values),
        out_specs=[ANY] * len(values),
        input_output_aliases={i: i for i in range(len(values))},
        cost_estimate=pl.CostEstimate(
            flops=int(micros * 1.15e9), bytes_accessed=0, transcendentals=0
        ),
        name="lead",
    )(*values)


def pick(structure_ref, n, j, first):
    nblocks = structure_ref.shape[1]
    start = jnp.where(n == 0, 0, nblocks - first)
    return structure_ref[n, lax.rem(start + j, nblocks)]


def pack_first(structure, panel, inverse, first):
    half_blocks = panel.shape[1] // BLK

    def body(st, panel_ref, inv_ref, out, *pieces):
        n = lax.axis_index("narrow")
        for j in range(first):
            row = pl.multiple_of(lax.rem(pick(st, n, j, first), half_blocks) * BLK, BLK)
            out[j * BLK : (j + 1) * BLK, :] = panel_ref[n, pl.ds(row, BLK), :]
        pieces[0][...] = inv_ref[:SPLIT, :]
        pieces[1][...] = inv_ref[SPLIT:, :]

    width = inverse.shape[1]
    return pl.pallas_call(
        body,
        out_shape=[
            jax.ShapeDtypeStruct((first * BLK, panel.shape[2]), panel.dtype),
            jax.ShapeDtypeStruct((SPLIT, width), inverse.dtype),
            jax.ShapeDtypeStruct((BLK - SPLIT, width), inverse.dtype),
        ],
        in_specs=[SMEM, VMEM, VMEM],
        out_specs=[VMEM] * 3,
        compiler_params=pltpu.CompilerParams(vmem_limit_bytes=8 * MIB),
        name="pack_first",
    )(structure, panel, inverse)


def pack_rest(structure, panel, other, first):
    nblocks = structure.shape[1]
    half_blocks = panel.shape[1] // BLK

    def body(st, panel_ref, other_ref, out0, out1):
        n = lax.axis_index("narrow")
        out0[(nblocks - first) * BLK :, :] = jnp.zeros((TAIL, LANES), out0.dtype)
        for j in range(nblocks - first):
            b = pick(st, n, first + j, first)
            row = pl.multiple_of(lax.rem(b, half_blocks) * BLK, BLK)
            mine = lax.div(b, half_blocks) == n
            rows = slice(j * BLK, (j + 1) * BLK)

            @pl.when(mine)
            def _():
                out0[rows, :] = panel_ref[n, pl.ds(row, BLK), :LANES]
                out1[rows, :] = panel_ref[n, pl.ds(row, BLK), LANES:]

            @pl.when(jnp.logical_not(mine))
            def _():
                out0[rows, :] = other_ref[pl.ds(row, BLK), :LANES]
                out1[rows, :] = other_ref[pl.ds(row, BLK), LANES:]

    rows = (nblocks - first) * BLK
    return pl.pallas_call(
        body,
        out_shape=(
            jax.ShapeDtypeStruct((rows + TAIL, LANES), panel.dtype),
            jax.ShapeDtypeStruct((rows, LANES), panel.dtype),
        ),
        in_specs=[SMEM, VMEM, VMEM],
        out_specs=[VMEM, VMEM],
        compiler_params=pltpu.CompilerParams(vmem_limit_bytes=8 * MIB),
        name="pack_rest",
    )(structure, panel, other)


def stack_rows(pieces):
    rows = sum(piece.shape[0] for piece in pieces)

    def body(*refs):
        at = 0
        for ref in refs[:-1]:
            refs[-1][at : at + ref.shape[0], :] = ref[...]
            at += ref.shape[0]

    return pl.pallas_call(
        body,
        out_shape=jax.ShapeDtypeStruct((rows, pieces[0].shape[1]), pieces[0].dtype),
        in_specs=[VMEM] * len(pieces),
        out_specs=VMEM,
        compiler_params=pltpu.CompilerParams(vmem_limit_bytes=8 * MIB),
        name="stack_rows",
    )(*pieces)


def pack_inverse(structure, owns, others, first):
    nblocks = structure.shape[1]
    half_blocks = owns[0].shape[1] // BLK
    count = len(owns)
    runs, row = [], 0
    for p, own in enumerate(owns):
        at = 0
        while at < own.shape[0]:
            rows = min(own.shape[0] - at, BLK - row % BLK)
            runs.append((p, at, row // BLK, row % BLK, rows))
            at, row = at + rows, row + rows

    def body(st, *refs):
        out = refs[2 * count]
        n = lax.axis_index("narrow")
        for j in range(nblocks):
            b = pick(st, n, j, first)
            col = pl.multiple_of(lax.rem(b, half_blocks) * BLK, BLK)
            mine = lax.div(b, half_blocks) == n

            def move(sources, j=j, col=col):
                for p, at, d, top, rows in runs:
                    out[d, top : top + rows, j * BLK : (j + 1) * BLK] = sources[p][
                        at : at + rows, pl.ds(col, BLK)
                    ]

            pl.when(mine)(lambda move=move: move(refs[:count]))
            pl.when(jnp.logical_not(mine))(lambda move=move: move(refs[count : 2 * count]))

    return pl.pallas_call(
        body,
        out_shape=jax.ShapeDtypeStruct((NGRP, BLK, nblocks * BLK), owns[0].dtype),
        in_specs=[SMEM] + [VMEM] * (2 * count),
        out_specs=VMEM,
        compiler_params=pltpu.CompilerParams(vmem_limit_bytes=18 * MIB),
        name="pack_inverse",
    )(structure, *owns, *others)


def products(structure, sel, firsts, rests, chunk, near=None):
    nblocks = structure.shape[1]
    early = firsts[0].shape[0]
    late = sel.shape[2] - early
    first = early // BLK
    spot = slice(chunk * LANES, (chunk + 1) * LANES)

    def body(st, sel_ref, f0, f1, r0, r1, *refs):
        result, total, acc = refs[-3:]
        n = lax.axis_index("narrow")
        w = lax.axis_index("wide")
        x = lax.bitwise_and(w, 1)
        total[...] = jnp.zeros_like(total)
        depth = sel_ref.shape[2]
        rows = sel_ref[...].reshape(NGRP * BLK, depth)
        acc[...] = jnp.dot(
            rows[:, :early],
            jnp.concatenate([f0[:, spot], f1[:, spot]], axis=1),
            preferred_element_type=jnp.float32,
        ) + jnp.dot(
            rows[:, early:],
            jnp.concatenate([r0[:late, :], r1[:late, :]], axis=1),
            preferred_element_type=jnp.float32,
        )
        for d in range(NGRP):
            row = lax.bitwise_xor(w, (d % 2) * Y + (d // 2) * ZL)
            pos = jnp.int32(0)
            inside = jnp.int32(0)
            for j in range(nblocks):
                hit = (pick(st, n, j, first) == row).astype(jnp.int32)
                pos = pos + j * hit
                inside = inside + hit

            @pl.when(inside == 0)
            def _(d=d):
                result[d] = jnp.zeros(result.shape[1:], result.dtype)

            @pl.when(inside > 0)
            def _(d=d, pos=pos):
                for dx in range(2):
                    part = acc[d * BLK : (d + 1) * BLK, dx * LANES : (dx + 1) * LANES]
                    slot = lax.bitwise_xor(x, dx)

                    def weigh(rows, part=part, slot=slot):
                        added = jnp.sum(part * rows.astype(jnp.float32), axis=0, keepdims=True)
                        total[slot] += added

                    @pl.when(pos < first)
                    def _():
                        at = pl.multiple_of(pos * BLK, BLK)
                        weigh((f0, f1)[dx][pl.ds(at, BLK), spot])

                    @pl.when(pos >= first)
                    def _():
                        at = pl.multiple_of((pos - first) * BLK, BLK)
                        weigh((r0, r1)[dx][pl.ds(at, BLK), :])

                    at = pl.multiple_of(slot * LANES, LANES)
                    result[d, pl.ds(at, LANES), :] = (-part).T.astype(result.dtype)

        for slot in range(2):
            left, terms = total[slot], []
            for _ in range(3):
                term = left.astype(result.dtype).astype(jnp.float32)
                terms.append(term)
                left = left - term
            tile = jnp.concatenate(terms + [jnp.zeros((TAIL - 3, LANES), jnp.float32)], axis=0)
            for d in range(NGRP):
                result[d, 2 * LANES :, slot * LANES : (slot + 1) * LANES] = tile.astype(
                    result.dtype
                )
        if near is None:
            refs[0][...] = result[...]
            return
        near_ref, kept, sent = refs[:3]
        stay = n == lax.div(w, ZH)

        @pl.when(stay)
        def _():
            kept[...] = near_ref[...]
            sent[...] = result[...]

        @pl.when(jnp.logical_not(stay))
        def _():
            kept[...] = result[...]
            sent[...] = near_ref[...]

    out = jax.ShapeDtypeStruct((NGRP, 2 * LANES + TAIL, BLK), sel.dtype)
    again = () if near is None else (near,)
    return pl.pallas_call(
        body,
        out_shape=out if near is None else [out, out],
        in_specs=[SMEM] + [VMEM] * (5 + len(again)),
        out_specs=VMEM if near is None else [VMEM, VMEM],
        scratch_shapes=[
            pltpu.VMEM(out.shape, out.dtype),
            pltpu.VMEM((2, 1, LANES), jnp.float32),
            pltpu.VMEM((NGRP * BLK, 2 * LANES), jnp.float32),
        ],
        compiler_params=pltpu.CompilerParams(vmem_limit_bytes=16 * MIB),
        cost_estimate=pl.CostEstimate(flops=0, bytes_accessed=0, transcendentals=0),
        name="products",
    )(structure, sel, *firsts, *rests, *again)


def bundle(ours, theirs):
    def body(our_ref, their_ref, *outs):
        for d, out in zip(DEST, outs):
            out[0] = our_ref[d]
            out[1] = their_ref[d]

    shape = jax.ShapeDtypeStruct((2, *ours.shape[1:]), ours.dtype)
    return pl.pallas_call(
        body,
        out_shape=[shape] * NGRP,
        in_specs=[VMEM, VMEM],
        out_specs=[VMEM] * NGRP,
        compiler_params=pltpu.CompilerParams(vmem_limit_bytes=8 * MIB),
        name="bundle",
    )(ours, theirs)


def squares(factor_inv):
    sups, rows, cols = factor_inv.shape
    half = cols // 2

    def body(in_ref, out_ref):
        for k in range(sups):
            value = in_ref[k].astype(jnp.float32)
            out_ref[k : k + 1, :] = jnp.sum(value * value, axis=0, keepdims=True)

    return pl.pallas_call(
        body,
        out_shape=jax.ShapeDtypeStruct((sups, cols), jnp.float32),
        grid=(2,),
        in_specs=[pl.BlockSpec((sups, rows, half), lambda c: (0, 0, c))],
        out_specs=pl.BlockSpec((sups, half), lambda c: (0, c)),
        compiler_params=pltpu.CompilerParams(vmem_limit_bytes=8 * MIB),
        name="squares",
    )(factor_inv)


def add_sums(base, messages, chunk):
    cols = base.shape[1]

    def body(base_ref, *refs):
        out = refs[-1]
        n = lax.axis_index("narrow")
        group = lax.rem(lax.div(lax.axis_index("wide"), Y), NGRP)
        out[...] = base_ref[...]
        for d, ref in zip(DEST, refs):
            source = lax.bitwise_xor(group, d)
            for k in range(2):
                which = (n != k).astype(jnp.int32)
                tile = ref[which, 2 * LANES :, :].astype(jnp.float32)
                value = tile[0:1] + (tile[1:2] + tile[2:3])
                for xx in range(2):
                    at = source * (cols // NGRP) + (2 * xx + chunk) * LANES
                    spot = pl.ds(pl.multiple_of(at, LANES), LANES)
                    out[k : k + 1, spot] += value[:, xx * LANES : (xx + 1) * LANES]

    return pl.pallas_call(
        body,
        out_shape=jax.ShapeDtypeStruct(base.shape, jnp.float32),
        in_specs=[VMEM] * (1 + NGRP),
        out_specs=VMEM,
        compiler_params=pltpu.CompilerParams(vmem_limit_bytes=4 * MIB),
        name="add_sums",
    )(base, *messages)


def assemble(messages, chunk, held):
    tall = 4 * LANES
    rows_total = 2 * 2 * NGRP * tall

    def body(*refs):
        msg_refs = refs[:NGRP]
        out, wide_buf, narrow_buf, sem = refs[-4:]
        n = lax.axis_index("narrow")
        w = lax.axis_index("wide")
        copies = []
        for d, msg_ref in zip(DEST, msg_refs):
            source = lax.bitwise_xor(lax.rem(lax.div(w, Y), NGRP), d)
            for xx in range(2):
                slot = 2 * d + xx
                for k in range(2):
                    which = (n != k).astype(jnp.int32)
                    value = msg_ref[which, xx * LANES : (xx + 1) * LANES, :].astype(
                        jnp.float32
                    )
                    for lt in range(2):
                        wide_buf[slot, pl.ds(2 * lt + k, LANES, stride=4), :] = value[
                            :, lt * LANES : (lt + 1) * LANES
                        ]
                narrow_buf[slot] = wide_buf[slot].astype(narrow_buf.dtype)
                row = pl.multiple_of(((source * 2 + xx) * 2 + chunk) * tall, tall)
                copy = pltpu.make_async_copy(
                    narrow_buf.at[slot], out.at[pl.ds(row, tall), :], sem.at[slot]
                )
                copy.start()
                copies.append(copy)
        for copy in copies:
            copy.wait()

    extra = () if held is None else (held,)
    return pl.pallas_call(
        body,
        out_shape=jax.ShapeDtypeStruct((rows_total, LANES), messages[0].dtype),
        in_specs=[VMEM] * NGRP + [ANY] * len(extra),
        out_specs=ANY,
        scratch_shapes=[
            pltpu.VMEM((2 * NGRP, tall, LANES), jnp.float32),
            pltpu.VMEM((2 * NGRP, tall, LANES), messages[0].dtype),
            pltpu.SemaphoreType.DMA((2 * NGRP,)),
        ],
        input_output_aliases={NGRP: 0} if extra else {},
        compiler_params=pltpu.CompilerParams(vmem_limit_bytes=8 * MIB),
        name="assemble",
    )(*messages, *extra)


def per_device_grid(inverse, panel, factor_inv, structure):
    first = structure.shape[1] - panel.shape[1] // BLK
    size = lax.axis_size("wide")
    n = lax.axis_index("narrow")
    f_own, top, bottom = pack_first(structure, panel, inverse, first)
    other = swap_cores(lax.dynamic_index_in_dim(panel, 1 - n, 0, keepdims=False), "panel_swap")
    r_own = pack_rest(structure, panel, other, first)
    linv = squares(factor_inv)
    f_z = hop(f_own, ZH, "first_z")
    f_x = hop(f_own, X, "first_x")
    a_z0 = hop(top, ZL, "inv_z0")
    a_y = hop(inverse, Y, "inv_y")
    a_y, f_z, f_x, *r_own = lax.optimization_barrier((a_y, f_z, f_x, *r_own))
    r_z1 = hop(r_own[1], ZH, "rest1_z")
    r_z0 = hop(r_own[0], ZH, "rest0_z")
    a_z1 = hop(after(bottom, f_z), ZL, "inv_z1")
    f_xz = hop(f_z, X, "first_xz")
    r_x0 = hop(r_own[0], X, "rest0_x")
    a_yz0 = hop(a_z0, Y, "inv_yz0")
    a_yz1 = hop(a_z1, Y, "inv_yz1")
    most = stack_rows([inverse, a_y, a_z0])
    r_z0, r_x0, f_xz, a_z1, a_yz0, a_yz1, most, *r_own = lax.optimization_barrier(
        (r_z0, r_x0, f_xz, a_z1, a_yz0, a_yz1, most, *r_own)
    )
    r_xz0 = hop(r_z0, X, "rest0_xz")
    r_x1 = hop(r_own[1], X, "rest1_x")
    more = stack_rows([a_z1, a_yz0, a_yz1])
    s_most = swap_cores(most, "inv_swap")
    s_more = swap_cores(more, "inv_swap_more")
    sel = pack_inverse(structure, (most, more), (s_most, s_more), first)
    linv = after(linv, more)
    for mask in (Y, ZL):
        linv = linv + hop(linv, mask, f"squares_{mask}")
    r_z1 = lead([r_z1], 20)[0]
    r_x1 = lead([r_x1], 10)[0]
    r_x1, linv = lax.optimization_barrier((r_x1, linv))

    def deliver(kept, sent, c):
        messages = bundle(kept, swap_cores(sent, f"cross{c}_swap"))
        return [messages[0]] + [
            hop(message, (d % 2) * Y + (d // 2) * ZL, f"cross{c}_{d}")
            for d, message in zip(DEST[1:], messages[1:])
        ]

    near = products(structure, sel, (f_own, f_x), (r_own[0], r_x0), 0)
    kept, sent = products(structure, sel, (f_z, f_xz), (r_z0, r_xz0), 0, near)
    messages = deliver(kept, sent, 0)
    r_xz1 = hop(after(r_z1, kept), X, "rest1_xz")
    near = products(structure, sel, (f_own, f_x), (r_own[1], r_x1), 1)
    messages[1:] = lead(messages[1:], 5)
    kept, sent = products(structure, sel, (f_z, f_xz), (r_z1, r_xz1), 1, near)
    held = assemble(messages, 0, None)
    variance = add_sums(linv, messages, 0)
    messages = deliver(after(kept, variance), sent, 1)
    variance = add_sums(variance, messages, 1)
    held = assemble(messages, 1, held)
    hops = [hop(variance, mask, f"variance_{mask}") for mask in (X, ZH, X | ZH)]
    variance = variance + hops[0] + hops[1] + hops[2]
    half = panel.shape[2] * size // 2
    cross = held.reshape(half, 2, 2, LANES).transpose(0, 2, 1, 3).reshape(half, 2, BLK)
    return cross, variance


def solution(mesh):
    in_specs = (P("wide", "narrow"), P(None, "narrow", "wide"), P(None, "wide", "narrow"), P())
    out_specs = (P("narrow", None, "wide"), P(None, "narrow"))

    def run(inverse, panel, factor_inv, structure):
        fits = (
            mesh.shape["wide"] == 16
            and mesh.shape["narrow"] == 2 == panel.shape[0]
            and panel.shape[2] == 16 * BLK == inverse.shape[0]
        )
        return jax.shard_map(
            per_device_grid if fits else per_device_general,
            mesh=mesh,
            in_specs=in_specs,
            out_specs=out_specs,
            check_vma=False,
        )(inverse, panel, factor_inv, structure)

    return run
```

```python
import jax
import jax.numpy as jnp
from jax import lax
from jax.experimental import pallas as pl
from jax.experimental.pallas import tpu as pltpu
from jax.sharding import PartitionSpec as P

BLK = 256
LANES = 128
ANY = pl.BlockSpec(memory_space=pl.ANY)
VMEM = pl.BlockSpec(memory_space=pltpu.VMEM)
SMEM = pl.BlockSpec(memory_space=pltpu.SMEM)


def spread(value, axis, source):
    kept = jnp.where(lax.axis_index(axis) == source, value, 0).astype(value.dtype)
    return lax.psum(kept, axis)


def block_partial(gathered, inverse, row_inside, col_inside, first_row, row_count):
    local_blocks = inverse.shape[1] // BLK
    running = jnp.zeros((row_count, BLK), jnp.float32)
    for blk_index in range(local_blocks):

        def product(blk_index=blk_index):
            panel_piece = lax.dynamic_slice(
                gathered, (blk_index * BLK, first_row), (BLK, row_count)
            )
            block_z = inverse[:, blk_index * BLK : (blk_index + 1) * BLK]
            return lax.dot_general(
                panel_piece, block_z, (((0,), (1,)), ((), ())), preferred_element_type=jnp.float32
            )

        def skipped():
            return jnp.zeros((row_count, BLK), jnp.float32)

        running = running + lax.cond(row_inside & col_inside[blk_index], product, skipped)
    return -running


def per_device_general(inverse, panel, factor_inv, structure):
    wide_count = lax.axis_size("wide")
    narrow_count = lax.axis_size("narrow")
    nsup_count = panel.shape[0]
    kw_total = panel.shape[2] * wide_count
    kw_local = kw_total // narrow_count
    local_blocks = inverse.shape[1] // BLK
    row_index = lax.axis_index("wide")
    col_first = lax.axis_index("narrow") * local_blocks
    col_ids = col_first + jnp.arange(local_blocks, dtype=jnp.int32)
    row_inside = jnp.any(structure == row_index, axis=1)
    col_inside = jnp.any(structure[:, :, None] == col_ids[None, None, :], axis=1)
    root_index = row_index // local_blocks
    offset = (row_index - root_index * local_blocks) * BLK
    cross_parts = []
    own_parts = []
    for sup_index in range(nsup_count):
        gathered_one = lax.all_gather(panel[sup_index], "wide", axis=1, tiled=True)

        def one_term(first_row, row_count, gathered_one=gathered_one, sup_index=sup_index):
            return block_partial(
                gathered_one,
                inverse,
                row_inside[sup_index],
                col_inside[sup_index],
                first_row,
                row_count,
            )

        cross_parts.append(
            lax.psum_scatter(
                one_term(jnp.int32(0), kw_local * lax.axis_size("narrow")),
                "narrow",
                scatter_dimension=0,
                tiled=True,
            )
        )
        own_parts.append(lax.dynamic_slice_in_dim(gathered_one, offset, BLK, axis=0))
    cross_f = jnp.stack(cross_parts, axis=1)
    own_rows = jnp.stack(own_parts)
    owner_panel = spread(own_rows, "narrow", root_index)
    owner_slice = lax.dynamic_slice_in_dim(
        owner_panel, lax.axis_index("narrow") * kw_local, kw_local, axis=2
    )
    weighted = jnp.einsum("kia,aki->ka", owner_slice.astype(jnp.float32), cross_f)
    linv_part = jnp.sum(jnp.square(factor_inv.astype(jnp.float32)), axis=1)
    variance = lax.psum(linv_part - weighted, "wide")
    return (cross_f.astype(jnp.bfloat16), variance)


X, Y, ZL, ZH = 1, 2, 4, 8
NGRP = 4
SPLIT = 192
TAIL = 16
DEST = (0, 3, 1, 2)
MIB = 1024 * 1024


def swap_cores(value, name):
    with jax.named_scope(name):
        return lax.ppermute(value, "narrow", [(0, 1), (1, 0)])


def hop(value, mask, name):
    size = lax.axis_size("wide")
    with jax.named_scope(name):
        return lax.ppermute(value, "wide", [(i, i ^ mask) for i in range(size)])


def after(value, *earlier):
    return lax.optimization_barrier((value, *earlier))[0]


def lead(values, micros):
    def body(*refs):
        pass

    return pl.pallas_call(
        body,
        out_shape=[jax.ShapeDtypeStruct(v.shape, v.dtype) for v in values],
        in_specs=[ANY] * len(values),
        out_specs=[ANY] * len(values),
        input_output_aliases={i: i for i in range(len(values))},
        compiler_params=pltpu.CompilerParams(vmem_limit_bytes=2 * MIB),
        cost_estimate=pl.CostEstimate(
            flops=int(micros * 1.15e9), bytes_accessed=0, transcendentals=0
        ),
        name="lead",
    )(*values)


def pick(structure_ref, n, j, first):
    nblocks = structure_ref.shape[1]
    start = jnp.where(n == 0, 0, nblocks - first)
    return structure_ref[n, lax.rem(start + j, nblocks)]


def pack_first(structure, panel, inverse, first):
    half_blocks = panel.shape[1] // BLK

    def body(st, panel_ref, inv_ref, out, *pieces):
        n = lax.axis_index("narrow")
        for j in range(first):
            row = pl.multiple_of(lax.rem(pick(st, n, j, first), half_blocks) * BLK, BLK)
            out[j * BLK : (j + 1) * BLK, :] = panel_ref[n, pl.ds(row, BLK), :]
        pieces[0][...] = inv_ref[:SPLIT, :]
        pieces[1][...] = inv_ref[SPLIT:, :]

    width = inverse.shape[1]
    return pl.pallas_call(
        body,
        out_shape=[
            jax.ShapeDtypeStruct((first * BLK, panel.shape[2]), panel.dtype),
            jax.ShapeDtypeStruct((SPLIT, width), inverse.dtype),
            jax.ShapeDtypeStruct((BLK - SPLIT, width), inverse.dtype),
        ],
        in_specs=[SMEM, VMEM, VMEM],
        out_specs=[VMEM] * 3,
        compiler_params=pltpu.CompilerParams(vmem_limit_bytes=8 * MIB),
        name="pack_first",
    )(structure, panel, inverse)


def pack_rest(structure, panel, other, first):
    nblocks = structure.shape[1]
    half_blocks = panel.shape[1] // BLK

    def body(st, panel_ref, other_ref, out0, out1):
        n = lax.axis_index("narrow")
        out0[(nblocks - first) * BLK :, :] = jnp.zeros((TAIL, LANES), out0.dtype)
        for j in range(nblocks - first):
            b = pick(st, n, first + j, first)
            row = pl.multiple_of(lax.rem(b, half_blocks) * BLK, BLK)
            mine = lax.div(b, half_blocks) == n
            rows = slice(j * BLK, (j + 1) * BLK)

            @pl.when(mine)
            def _():
                out0[rows, :] = panel_ref[n, pl.ds(row, BLK), :LANES]
                out1[rows, :] = panel_ref[n, pl.ds(row, BLK), LANES:]

            @pl.when(jnp.logical_not(mine))
            def _():
                out0[rows, :] = other_ref[pl.ds(row, BLK), :LANES]
                out1[rows, :] = other_ref[pl.ds(row, BLK), LANES:]

    rows = (nblocks - first) * BLK
    return pl.pallas_call(
        body,
        out_shape=(
            jax.ShapeDtypeStruct((rows + TAIL, LANES), panel.dtype),
            jax.ShapeDtypeStruct((rows, LANES), panel.dtype),
        ),
        in_specs=[SMEM, VMEM, VMEM],
        out_specs=[VMEM, VMEM],
        compiler_params=pltpu.CompilerParams(vmem_limit_bytes=8 * MIB),
        name="pack_rest",
    )(structure, panel, other)


def stack_rows(pieces):
    rows = sum(piece.shape[0] for piece in pieces)

    def body(*refs):
        at = 0
        for ref in refs[:-1]:
            refs[-1][at : at + ref.shape[0], :] = ref[...]
            at += ref.shape[0]

    return pl.pallas_call(
        body,
        out_shape=jax.ShapeDtypeStruct((rows, pieces[0].shape[1]), pieces[0].dtype),
        in_specs=[VMEM] * len(pieces),
        out_specs=VMEM,
        compiler_params=pltpu.CompilerParams(vmem_limit_bytes=8 * MIB),
        name="stack_rows",
    )(*pieces)


def pack_inverse(structure, owns, others, first):
    nblocks = structure.shape[1]
    half_blocks = owns[0].shape[1] // BLK
    count = len(owns)
    runs, row = [], 0
    for p, own in enumerate(owns):
        at = 0
        while at < own.shape[0]:
            rows = min(own.shape[0] - at, BLK - row % BLK)
            runs.append((p, at, row // BLK, row % BLK, rows))
            at, row = at + rows, row + rows

    def body(st, *refs):
        out = refs[2 * count]
        n = lax.axis_index("narrow")
        for j in range(nblocks):
            b = pick(st, n, j, first)
            col = pl.multiple_of(lax.rem(b, half_blocks) * BLK, BLK)
            mine = lax.div(b, half_blocks) == n

            def move(sources, j=j, col=col):
                for p, at, d, top, rows in runs:
                    out[d, top : top + rows, j * BLK : (j + 1) * BLK] = sources[p][
                        at : at + rows, pl.ds(col, BLK)
                    ]

            pl.when(mine)(lambda move=move: move(refs[:count]))
            pl.when(jnp.logical_not(mine))(lambda move=move: move(refs[count : 2 * count]))

    return pl.pallas_call(
        body,
        out_shape=jax.ShapeDtypeStruct((NGRP, BLK, nblocks * BLK), owns[0].dtype),
        in_specs=[SMEM] + [VMEM] * (2 * count),
        out_specs=VMEM,
        compiler_params=pltpu.CompilerParams(vmem_limit_bytes=18 * MIB),
        name="pack_inverse",
    )(structure, *owns, *others)


def products(structure, sel, firsts, rests, chunk, near=None):
    nblocks = structure.shape[1]
    early = firsts[0].shape[0]
    late = sel.shape[2] - early
    first = early // BLK
    spot = slice(chunk * LANES, (chunk + 1) * LANES)

    def body(st, sel_ref, f0, f1, r0, r1, *refs):
        result, total, acc = refs[-3:]
        n = lax.axis_index("narrow")
        w = lax.axis_index("wide")
        x = lax.bitwise_and(w, 1)
        total[...] = jnp.zeros_like(total)
        depth = sel_ref.shape[2]
        rows = sel_ref[...].reshape(NGRP * BLK, depth)
        acc[...] = jnp.dot(
            rows[:, :early],
            jnp.concatenate([f0[:, spot], f1[:, spot]], axis=1),
            preferred_element_type=jnp.float32,
        ) + jnp.dot(
            rows[:, early:],
            jnp.concatenate([r0[:late, :], r1[:late, :]], axis=1),
            preferred_element_type=jnp.float32,
        )
        for d in range(NGRP):
            row = lax.bitwise_xor(w, (d % 2) * Y + (d // 2) * ZL)
            pos = jnp.int32(0)
            inside = jnp.int32(0)
            for j in range(nblocks):
                hit = (pick(st, n, j, first) == row).astype(jnp.int32)
                pos = pos + j * hit
                inside = inside + hit

            @pl.when(inside == 0)
            def _(d=d):
                result[d] = jnp.zeros(result.shape[1:], result.dtype)

            @pl.when(inside > 0)
            def _(d=d, pos=pos):
                for dx in range(2):
                    part = acc[d * BLK : (d + 1) * BLK, dx * LANES : (dx + 1) * LANES]
                    slot = lax.bitwise_xor(x, dx)

                    def weigh(rows, part=part, slot=slot):
                        added = jnp.sum(part * rows.astype(jnp.float32), axis=0, keepdims=True)
                        total[slot] += added

                    @pl.when(pos < first)
                    def _():
                        at = pl.multiple_of(pos * BLK, BLK)
                        weigh((f0, f1)[dx][pl.ds(at, BLK), spot])

                    @pl.when(pos >= first)
                    def _():
                        at = pl.multiple_of((pos - first) * BLK, BLK)
                        weigh((r0, r1)[dx][pl.ds(at, BLK), :])

                    at = pl.multiple_of(slot * LANES, LANES)
                    result[d, pl.ds(at, LANES), :] = (-part).T.astype(result.dtype)

        for slot in range(2):
            left, terms = total[slot], []
            for _ in range(3):
                term = left.astype(result.dtype).astype(jnp.float32)
                terms.append(term)
                left = left - term
            tile = jnp.concatenate(terms + [jnp.zeros((TAIL - 3, LANES), jnp.float32)], axis=0)
            for d in range(NGRP):
                result[d, 2 * LANES :, slot * LANES : (slot + 1) * LANES] = tile.astype(
                    result.dtype
                )
        if near is None:
            refs[0][...] = result[...]
            return
        near_ref, kept, sent = refs[:3]
        stay = n == lax.div(w, ZH)

        @pl.when(stay)
        def _():
            kept[...] = near_ref[...]
            sent[...] = result[...]

        @pl.when(jnp.logical_not(stay))
        def _():
            kept[...] = result[...]
            sent[...] = near_ref[...]

    out = jax.ShapeDtypeStruct((NGRP, 2 * LANES + TAIL, BLK), sel.dtype)
    again = () if near is None else (near,)
    return pl.pallas_call(
        body,
        out_shape=out if near is None else [out, out],
        in_specs=[SMEM] + [VMEM] * (5 + len(again)),
        out_specs=VMEM if near is None else [VMEM, VMEM],
        scratch_shapes=[
            pltpu.VMEM(out.shape, out.dtype),
            pltpu.VMEM((2, 1, LANES), jnp.float32),
            pltpu.VMEM((NGRP * BLK, 2 * LANES), jnp.float32),
        ],
        compiler_params=pltpu.CompilerParams(vmem_limit_bytes=16 * MIB),
        cost_estimate=pl.CostEstimate(flops=0, bytes_accessed=0, transcendentals=0),
        name="products",
    )(structure, sel, *firsts, *rests, *again)


def bundle(ours, theirs):
    def body(our_ref, their_ref, *outs):
        for d, out in zip(DEST, outs):
            out[0] = our_ref[d]
            out[1] = their_ref[d]

    shape = jax.ShapeDtypeStruct((2, *ours.shape[1:]), ours.dtype)
    return pl.pallas_call(
        body,
        out_shape=[shape] * NGRP,
        in_specs=[VMEM, VMEM],
        out_specs=[VMEM] * NGRP,
        compiler_params=pltpu.CompilerParams(vmem_limit_bytes=8 * MIB),
        name="bundle",
    )(ours, theirs)


def squares(factor_inv):
    sups, rows, cols = factor_inv.shape
    half = cols // 2

    def body(in_ref, out_ref):
        for k in range(sups):
            value = in_ref[k].astype(jnp.float32)
            out_ref[k : k + 1, :] = jnp.sum(value * value, axis=0, keepdims=True)

    return pl.pallas_call(
        body,
        out_shape=jax.ShapeDtypeStruct((sups, cols), jnp.float32),
        grid=(2,),
        in_specs=[pl.BlockSpec((sups, rows, half), lambda c: (0, 0, c))],
        out_specs=pl.BlockSpec((sups, half), lambda c: (0, c)),
        compiler_params=pltpu.CompilerParams(vmem_limit_bytes=8 * MIB),
        name="squares",
    )(factor_inv)


def add_sums(base, messages, chunk):
    cols = base.shape[1]

    def body(base_ref, *refs):
        out = refs[-1]
        n = lax.axis_index("narrow")
        group = lax.rem(lax.div(lax.axis_index("wide"), Y), NGRP)
        out[...] = base_ref[...]
        for d, ref in zip(DEST, refs):
            source = lax.bitwise_xor(group, d)
            for k in range(2):
                which = (n != k).astype(jnp.int32)
                tile = ref[which, 2 * LANES :, :].astype(jnp.float32)
                value = tile[0:1] + (tile[1:2] + tile[2:3])
                for xx in range(2):
                    at = source * (cols // NGRP) + (2 * xx + chunk) * LANES
                    spot = pl.ds(pl.multiple_of(at, LANES), LANES)
                    out[k : k + 1, spot] += value[:, xx * LANES : (xx + 1) * LANES]

    return pl.pallas_call(
        body,
        out_shape=jax.ShapeDtypeStruct(base.shape, jnp.float32),
        in_specs=[VMEM] * (1 + NGRP),
        out_specs=VMEM,
        compiler_params=pltpu.CompilerParams(vmem_limit_bytes=4 * MIB),
        name="add_sums",
    )(base, *messages)


def assemble(messages, chunk, held):
    tall = 4 * LANES
    rows_total = 2 * 2 * NGRP * tall

    def body(*refs):
        msg_refs = refs[:NGRP]
        out, wide_buf, narrow_buf, sem = refs[-4:]
        n = lax.axis_index("narrow")
        w = lax.axis_index("wide")
        copies = []
        for d, msg_ref in zip(DEST, msg_refs):
            source = lax.bitwise_xor(lax.rem(lax.div(w, Y), NGRP), d)
            for xx in range(2):
                slot = 2 * d + xx
                for k in range(2):
                    which = (n != k).astype(jnp.int32)
                    value = msg_ref[which, xx * LANES : (xx + 1) * LANES, :].astype(
                        jnp.float32
                    )
                    for lt in range(2):
                        wide_buf[slot, pl.ds(2 * lt + k, LANES, stride=4), :] = value[
                            :, lt * LANES : (lt + 1) * LANES
                        ]
                narrow_buf[slot] = wide_buf[slot].astype(narrow_buf.dtype)
                row = pl.multiple_of(((source * 2 + xx) * 2 + chunk) * tall, tall)
                copy = pltpu.make_async_copy(
                    narrow_buf.at[slot], out.at[pl.ds(row, tall), :], sem.at[slot]
                )
                copy.start()
                copies.append(copy)
        for copy in copies:
            copy.wait()

    extra = () if held is None else (held,)
    return pl.pallas_call(
        body,
        out_shape=jax.ShapeDtypeStruct((rows_total, LANES), messages[0].dtype),
        in_specs=[VMEM] * NGRP + [ANY] * len(extra),
        out_specs=ANY,
        scratch_shapes=[
            pltpu.VMEM((2 * NGRP, tall, LANES), jnp.float32),
            pltpu.VMEM((2 * NGRP, tall, LANES), messages[0].dtype),
            pltpu.SemaphoreType.DMA((2 * NGRP,)),
        ],
        input_output_aliases={NGRP: 0} if extra else {},
        compiler_params=pltpu.CompilerParams(vmem_limit_bytes=8 * MIB),
        name="assemble",
    )(*messages, *extra)


def per_device_grid(inverse, panel, factor_inv, structure):
    first = structure.shape[1] - panel.shape[1] // BLK
    size = lax.axis_size("wide")
    n = lax.axis_index("narrow")
    f_own, top, bottom = pack_first(structure, panel, inverse, first)
    other = swap_cores(lax.dynamic_index_in_dim(panel, 1 - n, 0, keepdims=False), "panel_swap")
    r_own = pack_rest(structure, panel, other, first)
    linv = squares(factor_inv)
    f_z = hop(f_own, ZH, "first_z")
    f_x = hop(f_own, X, "first_x")
    a_z0 = hop(top, ZL, "inv_z0")
    a_y = hop(inverse, Y, "inv_y")
    a_y, f_z, f_x, *r_own = lax.optimization_barrier((a_y, f_z, f_x, *r_own))
    r_z1 = hop(r_own[1], ZH, "rest1_z")
    r_z0 = hop(r_own[0], ZH, "rest0_z")
    a_z1 = hop(after(bottom, f_z), ZL, "inv_z1")
    f_xz = hop(f_z, X, "first_xz")
    r_x0 = hop(r_own[0], X, "rest0_x")
    a_yz0 = hop(a_z0, Y, "inv_yz0")
    a_yz1 = hop(a_z1, Y, "inv_yz1")
    most = stack_rows([inverse, a_y, a_z0])
    r_z0, r_x0, f_xz, a_z1, a_yz0, a_yz1, most, *r_own = lax.optimization_barrier(
        (r_z0, r_x0, f_xz, a_z1, a_yz0, a_yz1, most, *r_own)
    )
    r_xz0 = hop(r_z0, X, "rest0_xz")
    r_x1 = hop(r_own[1], X, "rest1_x")
    more = stack_rows([a_z1, a_yz0, a_yz1])
    s_most = swap_cores(most, "inv_swap")
    s_more = swap_cores(more, "inv_swap_more")
    sel = pack_inverse(structure, (most, more), (s_most, s_more), first)
    linv = after(linv, more)
    for mask in (Y, ZL):
        linv = linv + hop(linv, mask, f"squares_{mask}")
    r_z1 = lead([r_z1], 20)[0]
    r_x1 = lead([r_x1], 10)[0]
    r_x1, linv = lax.optimization_barrier((r_x1, linv))

    def deliver(kept, sent, c):
        messages = bundle(kept, swap_cores(sent, f"cross{c}_swap"))
        return [messages[0]] + [
            hop(message, (d % 2) * Y + (d // 2) * ZL, f"cross{c}_{d}")
            for d, message in zip(DEST[1:], messages[1:])
        ]

    near = products(structure, sel, (f_own, f_x), (r_own[0], r_x0), 0)
    kept, sent = products(structure, sel, (f_z, f_xz), (r_z0, r_xz0), 0, near)
    messages = deliver(kept, sent, 0)
    r_xz1 = hop(after(r_z1, kept), X, "rest1_xz")
    near = products(structure, sel, (f_own, f_x), (r_own[1], r_x1), 1)
    messages[1:] = lead(messages[1:], 5)
    kept, sent = products(structure, sel, (f_z, f_xz), (r_z1, r_xz1), 1, near)
    held = assemble(messages, 0, None)
    variance = add_sums(linv, messages, 0)
    messages = deliver(after(kept, variance), sent, 1)
    variance = add_sums(variance, messages, 1)
    held = assemble(messages, 1, held)
    hops = [hop(variance, mask, f"variance_{mask}") for mask in (X, ZH, X | ZH)]
    variance = variance + hops[0] + hops[1] + hops[2]
    half = panel.shape[2] * size // 2
    cross = held.reshape(half, 2, 2, LANES).transpose(0, 2, 1, 3).reshape(half, 2, BLK)
    return cross, variance


def solution(mesh):
    in_specs = (P("wide", "narrow"), P(None, "narrow", "wide"), P(None, "wide", "narrow"), P())
    out_specs = (P("narrow", None, "wide"), P(None, "narrow"))

    def run(inverse, panel, factor_inv, structure):
        fits = (
            mesh.shape["wide"] == 16
            and mesh.shape["narrow"] == 2 == panel.shape[0]
            and panel.shape[2] == 16 * BLK == inverse.shape[0]
        )
        return jax.shard_map(
            per_device_grid if fits else per_device_general,
            mesh=mesh,
            in_specs=in_specs,
            out_specs=out_specs,
            check_vma=False,
        )(inverse, panel, factor_inv, structure)

    return run
```

```python
import jax
import jax.numpy as jnp
from jax import lax
from jax.experimental import pallas as pl
from jax.experimental.pallas import tpu as pltpu
from jax.sharding import PartitionSpec as P

BLK = 256
LANES = 128
ANY = pl.BlockSpec(memory_space=pl.ANY)
VMEM = pl.BlockSpec(memory_space=pltpu.VMEM)
SMEM = pl.BlockSpec(memory_space=pltpu.SMEM)


def spread(value, axis, source):
    kept = jnp.where(lax.axis_index(axis) == source, value, 0).astype(value.dtype)
    return lax.psum(kept, axis)


def block_partial(gathered, inverse, row_inside, col_inside, first_row, row_count):
    local_blocks = inverse.shape[1] // BLK
    running = jnp.zeros((row_count, BLK), jnp.float32)
    for blk_index in range(local_blocks):

        def product(blk_index=blk_index):
            panel_piece = lax.dynamic_slice(
                gathered, (blk_index * BLK, first_row), (BLK, row_count)
            )
            block_z = inverse[:, blk_index * BLK : (blk_index + 1) * BLK]
            return lax.dot_general(
                panel_piece, block_z, (((0,), (1,)), ((), ())), preferred_element_type=jnp.float32
            )

        def skipped():
            return jnp.zeros((row_count, BLK), jnp.float32)

        running = running + lax.cond(row_inside & col_inside[blk_index], product, skipped)
    return -running


def per_device_general(inverse, panel, factor_inv, structure):
    wide_count = lax.axis_size("wide")
    narrow_count = lax.axis_size("narrow")
    nsup_count = panel.shape[0]
    kw_total = panel.shape[2] * wide_count
    kw_local = kw_total // narrow_count
    local_blocks = inverse.shape[1] // BLK
    row_index = lax.axis_index("wide")
    col_first = lax.axis_index("narrow") * local_blocks
    col_ids = col_first + jnp.arange(local_blocks, dtype=jnp.int32)
    row_inside = jnp.any(structure == row_index, axis=1)
    col_inside = jnp.any(structure[:, :, None] == col_ids[None, None, :], axis=1)
    root_index = row_index // local_blocks
    offset = (row_index - root_index * local_blocks) * BLK
    cross_parts = []
    own_parts = []
    for sup_index in range(nsup_count):
        gathered_one = lax.all_gather(panel[sup_index], "wide", axis=1, tiled=True)

        def one_term(first_row, row_count, gathered_one=gathered_one, sup_index=sup_index):
            return block_partial(
                gathered_one,
                inverse,
                row_inside[sup_index],
                col_inside[sup_index],
                first_row,
                row_count,
            )

        cross_parts.append(
            lax.psum_scatter(
                one_term(jnp.int32(0), kw_local * lax.axis_size("narrow")),
                "narrow",
                scatter_dimension=0,
                tiled=True,
            )
        )
        own_parts.append(lax.dynamic_slice_in_dim(gathered_one, offset, BLK, axis=0))
    cross_f = jnp.stack(cross_parts, axis=1)
    own_rows = jnp.stack(own_parts)
    owner_panel = spread(own_rows, "narrow", root_index)
    owner_slice = lax.dynamic_slice_in_dim(
        owner_panel, lax.axis_index("narrow") * kw_local, kw_local, axis=2
    )
    weighted = jnp.einsum("kia,aki->ka", owner_slice.astype(jnp.float32), cross_f)
    linv_part = jnp.sum(jnp.square(factor_inv.astype(jnp.float32)), axis=1)
    variance = lax.psum(linv_part - weighted, "wide")
    return (cross_f.astype(jnp.bfloat16), variance)


X, Y, ZL, ZH = 1, 2, 4, 8
NGRP = 4
SPLIT = 192
TAIL = 16
DEST = (0, 3, 1, 2)
MIB = 1024 * 1024


def swap_cores(value, name):
    with jax.named_scope(name):
        return lax.ppermute(value, "narrow", [(0, 1), (1, 0)])


def hop(value, mask, name):
    size = lax.axis_size("wide")
    with jax.named_scope(name):
        return lax.ppermute(value, "wide", [(i, i ^ mask) for i in range(size)])


def after(value, *earlier):
    return lax.optimization_barrier((value, *earlier))[0]


def lead(values, micros):
    def body(*refs):
        pass

    return pl.pallas_call(
        body,
        out_shape=[jax.ShapeDtypeStruct(v.shape, v.dtype) for v in values],
        in_specs=[ANY] * len(values),
        out_specs=[ANY] * len(values),
        input_output_aliases={i: i for i in range(len(values))},
        compiler_params=pltpu.CompilerParams(vmem_limit_bytes=2 * MIB),
        cost_estimate=pl.CostEstimate(
            flops=int(micros * 1.15e9), bytes_accessed=0, transcendentals=0
        ),
        name="lead",
    )(*values)


def pick(structure_ref, n, j, first):
    nblocks = structure_ref.shape[1]
    start = jnp.where(n == 0, 0, nblocks - first)
    return structure_ref[n, lax.rem(start + j, nblocks)]


def pack_first(structure, panel, inverse, first):
    half_blocks = panel.shape[1] // BLK

    def body(st, panel_ref, inv_ref, out, *pieces):
        n = lax.axis_index("narrow")
        for j in range(first):
            row = pl.multiple_of(lax.rem(pick(st, n, j, first), half_blocks) * BLK, BLK)
            out[j * BLK : (j + 1) * BLK, :] = panel_ref[n, pl.ds(row, BLK), :]
        pieces[0][...] = inv_ref[:SPLIT, :]
        pieces[1][...] = inv_ref[SPLIT:, :]

    width = inverse.shape[1]
    return pl.pallas_call(
        body,
        out_shape=[
            jax.ShapeDtypeStruct((first * BLK, panel.shape[2]), panel.dtype),
            jax.ShapeDtypeStruct((SPLIT, width), inverse.dtype),
            jax.ShapeDtypeStruct((BLK - SPLIT, width), inverse.dtype),
        ],
        in_specs=[SMEM, VMEM, VMEM],
        out_specs=[VMEM] * 3,
        compiler_params=pltpu.CompilerParams(vmem_limit_bytes=8 * MIB),
        name="pack_first",
    )(structure, panel, inverse)


def pack_rest(structure, panel, other, first):
    nblocks = structure.shape[1]
    half_blocks = panel.shape[1] // BLK

    def body(st, panel_ref, other_ref, out0, out1):
        n = lax.axis_index("narrow")
        out0[(nblocks - first) * BLK :, :] = jnp.zeros((TAIL, LANES), out0.dtype)
        for j in range(nblocks - first):
            b = pick(st, n, first + j, first)
            row = pl.multiple_of(lax.rem(b, half_blocks) * BLK, BLK)
            mine = lax.div(b, half_blocks) == n
            rows = slice(j * BLK, (j + 1) * BLK)

            @pl.when(mine)
            def _():
                out0[rows, :] = panel_ref[n, pl.ds(row, BLK), :LANES]
                out1[rows, :] = panel_ref[n, pl.ds(row, BLK), LANES:]

            @pl.when(jnp.logical_not(mine))
            def _():
                out0[rows, :] = other_ref[pl.ds(row, BLK), :LANES]
                out1[rows, :] = other_ref[pl.ds(row, BLK), LANES:]

    rows = (nblocks - first) * BLK
    return pl.pallas_call(
        body,
        out_shape=(
            jax.ShapeDtypeStruct((rows + TAIL, LANES), panel.dtype),
            jax.ShapeDtypeStruct((rows, LANES), panel.dtype),
        ),
        in_specs=[SMEM, VMEM, VMEM],
        out_specs=[VMEM, VMEM],
        compiler_params=pltpu.CompilerParams(vmem_limit_bytes=8 * MIB),
        name="pack_rest",
    )(structure, panel, other)


def stack_rows(pieces):
    rows = sum(piece.shape[0] for piece in pieces)

    def body(*refs):
        at = 0
        for ref in refs[:-1]:
            refs[-1][at : at + ref.shape[0], :] = ref[...]
            at += ref.shape[0]

    return pl.pallas_call(
        body,
        out_shape=jax.ShapeDtypeStruct((rows, pieces[0].shape[1]), pieces[0].dtype),
        in_specs=[VMEM] * len(pieces),
        out_specs=VMEM,
        compiler_params=pltpu.CompilerParams(vmem_limit_bytes=8 * MIB),
        name="stack_rows",
    )(*pieces)


def pack_inverse(structure, owns, others, first):
    nblocks = structure.shape[1]
    half_blocks = owns[0].shape[1] // BLK
    count = len(owns)
    runs, row = [], 0
    for p, own in enumerate(owns):
        at = 0
        while at < own.shape[0]:
            rows = min(own.shape[0] - at, BLK - row % BLK)
            runs.append((p, at, row // BLK, row % BLK, rows))
            at, row = at + rows, row + rows

    def body(st, *refs):
        out = refs[2 * count]
        n = lax.axis_index("narrow")
        for j in range(nblocks):
            b = pick(st, n, j, first)
            col = pl.multiple_of(lax.rem(b, half_blocks) * BLK, BLK)
            mine = lax.div(b, half_blocks) == n

            def move(sources, j=j, col=col):
                for p, at, d, top, rows in runs:
                    out[d, top : top + rows, j * BLK : (j + 1) * BLK] = sources[p][
                        at : at + rows, pl.ds(col, BLK)
                    ]

            pl.when(mine)(lambda move=move: move(refs[:count]))
            pl.when(jnp.logical_not(mine))(lambda move=move: move(refs[count : 2 * count]))

    return pl.pallas_call(
        body,
        out_shape=jax.ShapeDtypeStruct((NGRP, BLK, nblocks * BLK), owns[0].dtype),
        in_specs=[SMEM] + [VMEM] * (2 * count),
        out_specs=VMEM,
        compiler_params=pltpu.CompilerParams(vmem_limit_bytes=18 * MIB),
        name="pack_inverse",
    )(structure, *owns, *others)


def products(structure, sel, firsts, rests, chunk, near=None):
    nblocks = structure.shape[1]
    early = firsts[0].shape[0]
    late = sel.shape[2] - early
    first = early // BLK
    spot = slice(chunk * LANES, (chunk + 1) * LANES)

    def body(st, sel_ref, f0, f1, r0, r1, *refs):
        result, total, acc = refs[-3:]
        n = lax.axis_index("narrow")
        w = lax.axis_index("wide")
        x = lax.bitwise_and(w, 1)
        total[...] = jnp.zeros_like(total)
        depth = sel_ref.shape[2]
        rows = sel_ref[...].reshape(NGRP * BLK, depth)
        acc[...] = jnp.dot(
            rows[:, :early],
            jnp.concatenate([f0[:, spot], f1[:, spot]], axis=1),
            preferred_element_type=jnp.float32,
        ) + jnp.dot(
            rows[:, early:],
            jnp.concatenate([r0[:late, :], r1[:late, :]], axis=1),
            preferred_element_type=jnp.float32,
        )
        for d in range(NGRP):
            row = lax.bitwise_xor(w, (d % 2) * Y + (d // 2) * ZL)
            pos = jnp.int32(0)
            inside = jnp.int32(0)
            for j in range(nblocks):
                hit = (pick(st, n, j, first) == row).astype(jnp.int32)
                pos = pos + j * hit
                inside = inside + hit

            @pl.when(inside == 0)
            def _(d=d):
                result[d] = jnp.zeros(result.shape[1:], result.dtype)

            @pl.when(inside > 0)
            def _(d=d, pos=pos):
                for dx in range(2):
                    part = acc[d * BLK : (d + 1) * BLK, dx * LANES : (dx + 1) * LANES]
                    slot = lax.bitwise_xor(x, dx)

                    def weigh(rows, part=part, slot=slot):
                        added = jnp.sum(part * rows.astype(jnp.float32), axis=0, keepdims=True)
                        total[slot] += added

                    @pl.when(pos < first)
                    def _():
                        at = pl.multiple_of(pos * BLK, BLK)
                        weigh((f0, f1)[dx][pl.ds(at, BLK), spot])

                    @pl.when(pos >= first)
                    def _():
                        at = pl.multiple_of((pos - first) * BLK, BLK)
                        weigh((r0, r1)[dx][pl.ds(at, BLK), :])

                    at = pl.multiple_of(slot * LANES, LANES)
                    result[d, pl.ds(at, LANES), :] = (-part).astype(result.dtype).T

        for slot in range(2):
            left, terms = total[slot], []
            for _ in range(3):
                term = left.astype(result.dtype).astype(jnp.float32)
                terms.append(term)
                left = left - term
            tile = jnp.concatenate(terms + [jnp.zeros((TAIL - 3, LANES), jnp.float32)], axis=0)
            for d in range(NGRP):
                result[d, 2 * LANES :, slot * LANES : (slot + 1) * LANES] = tile.astype(
                    result.dtype
                )
        if near is None:
            refs[0][...] = result[...]
            return
        near_ref, kept, sent = refs[:3]
        stay = n == lax.div(w, ZH)

        @pl.when(stay)
        def _():
            kept[...] = near_ref[...]
            sent[...] = result[...]

        @pl.when(jnp.logical_not(stay))
        def _():
            kept[...] = result[...]
            sent[...] = near_ref[...]

    out = jax.ShapeDtypeStruct((NGRP, 2 * LANES + TAIL, BLK), sel.dtype)
    again = () if near is None else (near,)
    return pl.pallas_call(
        body,
        out_shape=out if near is None else [out, out],
        in_specs=[SMEM] + [VMEM] * (5 + len(again)),
        out_specs=VMEM if near is None else [VMEM, VMEM],
        scratch_shapes=[
            pltpu.VMEM(out.shape, out.dtype),
            pltpu.VMEM((2, 1, LANES), jnp.float32),
            pltpu.VMEM((NGRP * BLK, 2 * LANES), jnp.float32),
        ],
        compiler_params=pltpu.CompilerParams(vmem_limit_bytes=16 * MIB),
        cost_estimate=pl.CostEstimate(flops=0, bytes_accessed=0, transcendentals=0),
        name="products",
    )(structure, sel, *firsts, *rests, *again)


def bundle(ours, theirs):
    def body(our_ref, their_ref, *outs):
        for d, out in zip(DEST, outs):
            out[0] = our_ref[d]
            out[1] = their_ref[d]

    shape = jax.ShapeDtypeStruct((2, *ours.shape[1:]), ours.dtype)
    return pl.pallas_call(
        body,
        out_shape=[shape] * NGRP,
        in_specs=[VMEM, VMEM],
        out_specs=[VMEM] * NGRP,
        compiler_params=pltpu.CompilerParams(vmem_limit_bytes=8 * MIB),
        name="bundle",
    )(ours, theirs)


def squares(factor_inv):
    sups, rows, cols = factor_inv.shape
    half = cols // 2

    def body(in_ref, out_ref):
        for k in range(sups):
            value = in_ref[k].astype(jnp.float32)
            out_ref[k : k + 1, :] = jnp.sum(value * value, axis=0, keepdims=True)

    return pl.pallas_call(
        body,
        out_shape=jax.ShapeDtypeStruct((sups, cols), jnp.float32),
        grid=(2,),
        in_specs=[pl.BlockSpec((sups, rows, half), lambda c: (0, 0, c))],
        out_specs=pl.BlockSpec((sups, half), lambda c: (0, c)),
        compiler_params=pltpu.CompilerParams(vmem_limit_bytes=8 * MIB),
        name="squares",
    )(factor_inv)


def add_sums(base, messages, chunk):
    cols = base.shape[1]

    def body(base_ref, *refs):
        out = refs[-1]
        n = lax.axis_index("narrow")
        group = lax.rem(lax.div(lax.axis_index("wide"), Y), NGRP)
        out[...] = base_ref[...]
        for d, ref in zip(DEST, refs):
            source = lax.bitwise_xor(group, d)
            for k in range(2):
                which = (n != k).astype(jnp.int32)
                tile = ref[which, 2 * LANES :, :].astype(jnp.float32)
                value = tile[0:1] + (tile[1:2] + tile[2:3])
                for xx in range(2):
                    at = source * (cols // NGRP) + (2 * xx + chunk) * LANES
                    spot = pl.ds(pl.multiple_of(at, LANES), LANES)
                    out[k : k + 1, spot] += value[:, xx * LANES : (xx + 1) * LANES]

    return pl.pallas_call(
        body,
        out_shape=jax.ShapeDtypeStruct(base.shape, jnp.float32),
        in_specs=[VMEM] * (1 + NGRP),
        out_specs=VMEM,
        compiler_params=pltpu.CompilerParams(vmem_limit_bytes=4 * MIB),
        name="add_sums",
    )(base, *messages)


def assemble(messages, chunk, held):
    tall = 4 * LANES
    rows_total = 2 * 2 * NGRP * tall

    def body(*refs):
        msg_refs = refs[:NGRP]
        out, wide_buf, narrow_buf, sem = refs[-4:]
        n = lax.axis_index("narrow")
        w = lax.axis_index("wide")
        copies = []
        for d, msg_ref in zip(DEST, msg_refs):
            source = lax.bitwise_xor(lax.rem(lax.div(w, Y), NGRP), d)
            for xx in range(2):
                slot = 2 * d + xx
                for k in range(2):
                    which = (n != k).astype(jnp.int32)
                    value = msg_ref[which, xx * LANES : (xx + 1) * LANES, :].astype(
                        jnp.float32
                    )
                    for lt in range(2):
                        wide_buf[slot, pl.ds(2 * lt + k, LANES, stride=4), :] = value[
                            :, lt * LANES : (lt + 1) * LANES
                        ]
                narrow_buf[slot] = wide_buf[slot].astype(narrow_buf.dtype)
                row = pl.multiple_of(((source * 2 + xx) * 2 + chunk) * tall, tall)
                copy = pltpu.make_async_copy(
                    narrow_buf.at[slot], out.at[pl.ds(row, tall), :], sem.at[slot]
                )
                copy.start()
                copies.append(copy)
        for copy in copies:
            copy.wait()

    extra = () if held is None else (held,)
    return pl.pallas_call(
        body,
        out_shape=jax.ShapeDtypeStruct((rows_total, LANES), messages[0].dtype),
        in_specs=[VMEM] * NGRP + [ANY] * len(extra),
        out_specs=ANY,
        scratch_shapes=[
            pltpu.VMEM((2 * NGRP, tall, LANES), jnp.float32),
            pltpu.VMEM((2 * NGRP, tall, LANES), messages[0].dtype),
            pltpu.SemaphoreType.DMA((2 * NGRP,)),
        ],
        input_output_aliases={NGRP: 0} if extra else {},
        compiler_params=pltpu.CompilerParams(vmem_limit_bytes=8 * MIB),
        name="assemble",
    )(*messages, *extra)


def per_device_grid(inverse, panel, factor_inv, structure):
    first = structure.shape[1] - panel.shape[1] // BLK
    size = lax.axis_size("wide")
    n = lax.axis_index("narrow")
    f_own, top, bottom = pack_first(structure, panel, inverse, first)
    other = swap_cores(lax.dynamic_index_in_dim(panel, 1 - n, 0, keepdims=False), "panel_swap")
    r_own = pack_rest(structure, panel, other, first)
    linv = squares(factor_inv)
    f_z = lead([hop(f_own, ZH, "first_z")], 10)[0]
    f_x = hop(f_own, X, "first_x")
    a_z0 = hop(top, ZL, "inv_z0")
    a_y = hop(inverse, Y, "inv_y")
    a_y, f_z, f_x, *r_own = lax.optimization_barrier((a_y, f_z, f_x, *r_own))
    r_z1 = hop(r_own[1], ZH, "rest1_z")
    r_z0 = hop(r_own[0], ZH, "rest0_z")
    a_z1 = hop(after(bottom, f_z), ZL, "inv_z1")
    f_xz = hop(f_z, X, "first_xz")
    r_x0 = hop(r_own[0], X, "rest0_x")
    a_yz0 = hop(a_z0, Y, "inv_yz0")
    a_yz1 = hop(a_z1, Y, "inv_yz1")
    most = stack_rows([inverse, a_y, a_z0])
    r_z0, r_x0, f_xz, a_z1, a_yz0, a_yz1, most, *r_own = lax.optimization_barrier(
        (r_z0, r_x0, f_xz, a_z1, a_yz0, a_yz1, most, *r_own)
    )
    r_xz0 = hop(r_z0, X, "rest0_xz")
    r_x1 = hop(r_own[1], X, "rest1_x")
    more = stack_rows([a_z1, a_yz0, a_yz1])
    s_most = swap_cores(most, "inv_swap")
    s_more = swap_cores(more, "inv_swap_more")
    sel = pack_inverse(structure, (most, more), (s_most, s_more), first)
    linv = after(linv, more)
    for mask in (Y, ZL):
        linv = linv + hop(linv, mask, f"squares_{mask}")
    r_z1 = lead([r_z1], 20)[0]
    r_x1 = lead([r_x1], 10)[0]
    r_x1, linv = lax.optimization_barrier((r_x1, linv))

    def deliver(kept, sent, c):
        messages = bundle(kept, swap_cores(sent, f"cross{c}_swap"))
        return [messages[0]] + [
            hop(message, (d % 2) * Y + (d // 2) * ZL, f"cross{c}_{d}")
            for d, message in zip(DEST[1:], messages[1:])
        ]

    near = products(structure, sel, (f_own, f_x), (r_own[0], r_x0), 0)
    kept, sent = products(structure, sel, (f_z, f_xz), (r_z0, r_xz0), 0, near)
    messages = deliver(kept, sent, 0)
    r_xz1 = hop(after(r_z1, kept), X, "rest1_xz")
    near = products(structure, sel, (f_own, f_x), (r_own[1], r_x1), 1)
    messages[1:] = lead(messages[1:], 5)
    kept, sent = products(structure, sel, (f_z, f_xz), (r_z1, r_xz1), 1, near)
    held = assemble(messages, 0, None)
    variance = add_sums(linv, messages, 0)
    messages = deliver(after(kept, variance), sent, 1)
    variance = add_sums(variance, messages, 1)
    held = assemble(messages, 1, held)
    hops = [hop(variance, mask, f"variance_{mask}") for mask in (X, ZH, X | ZH)]
    variance = variance + hops[0] + hops[1] + hops[2]
    half = panel.shape[2] * size // 2
    cross = held.reshape(half, 2, 2, LANES).transpose(0, 2, 1, 3).reshape(half, 2, BLK)
    return cross, variance


def solution(mesh):
    in_specs = (P("wide", "narrow"), P(None, "narrow", "wide"), P(None, "wide", "narrow"), P())
    out_specs = (P("narrow", None, "wide"), P(None, "narrow"))

    def run(inverse, panel, factor_inv, structure):
        fits = (
            mesh.shape["wide"] == 16
            and mesh.shape["narrow"] == 2 == panel.shape[0]
            and panel.shape[2] == 16 * BLK == inverse.shape[0]
        )
        return jax.shard_map(
            per_device_grid if fits else per_device_general,
            mesh=mesh,
            in_specs=in_specs,
            out_specs=out_specs,
            check_vma=False,
        )(inverse, panel, factor_inv, structure)

    return run
```

```python
import jax
import jax.numpy as jnp
from jax import lax
from jax.experimental import pallas as pl
from jax.experimental.pallas import tpu as pltpu
from jax.sharding import PartitionSpec as P

BLK = 256
LANES = 128
ANY = pl.BlockSpec(memory_space=pl.ANY)
VMEM = pl.BlockSpec(memory_space=pltpu.VMEM)
SMEM = pl.BlockSpec(memory_space=pltpu.SMEM)


def spread(value, axis, source):
    kept = jnp.where(lax.axis_index(axis) == source, value, 0).astype(value.dtype)
    return lax.psum(kept, axis)


def block_partial(gathered, inverse, row_inside, col_inside, first_row, row_count):
    local_blocks = inverse.shape[1] // BLK
    running = jnp.zeros((row_count, BLK), jnp.float32)
    for blk_index in range(local_blocks):

        def product(blk_index=blk_index):
            panel_piece = lax.dynamic_slice(
                gathered, (blk_index * BLK, first_row), (BLK, row_count)
            )
            block_z = inverse[:, blk_index * BLK : (blk_index + 1) * BLK]
            return lax.dot_general(
                panel_piece, block_z, (((0,), (1,)), ((), ())), preferred_element_type=jnp.float32
            )

        def skipped():
            return jnp.zeros((row_count, BLK), jnp.float32)

        running = running + lax.cond(row_inside & col_inside[blk_index], product, skipped)
    return -running


def per_device_general(inverse, panel, factor_inv, structure):
    wide_count = lax.axis_size("wide")
    narrow_count = lax.axis_size("narrow")
    nsup_count = panel.shape[0]
    kw_total = panel.shape[2] * wide_count
    kw_local = kw_total // narrow_count
    local_blocks = inverse.shape[1] // BLK
    row_index = lax.axis_index("wide")
    col_first = lax.axis_index("narrow") * local_blocks
    col_ids = col_first + jnp.arange(local_blocks, dtype=jnp.int32)
    row_inside = jnp.any(structure == row_index, axis=1)
    col_inside = jnp.any(structure[:, :, None] == col_ids[None, None, :], axis=1)
    root_index = row_index // local_blocks
    offset = (row_index - root_index * local_blocks) * BLK
    cross_parts = []
    own_parts = []
    for sup_index in range(nsup_count):
        gathered_one = lax.all_gather(panel[sup_index], "wide", axis=1, tiled=True)

        def one_term(first_row, row_count, gathered_one=gathered_one, sup_index=sup_index):
            return block_partial(
                gathered_one,
                inverse,
                row_inside[sup_index],
                col_inside[sup_index],
                first_row,
                row_count,
            )

        cross_parts.append(
            lax.psum_scatter(
                one_term(jnp.int32(0), kw_local * lax.axis_size("narrow")),
                "narrow",
                scatter_dimension=0,
                tiled=True,
            )
        )
        own_parts.append(lax.dynamic_slice_in_dim(gathered_one, offset, BLK, axis=0))
    cross_f = jnp.stack(cross_parts, axis=1)
    own_rows = jnp.stack(own_parts)
    owner_panel = spread(own_rows, "narrow", root_index)
    owner_slice = lax.dynamic_slice_in_dim(
        owner_panel, lax.axis_index("narrow") * kw_local, kw_local, axis=2
    )
    weighted = jnp.einsum("kia,aki->ka", owner_slice.astype(jnp.float32), cross_f)
    linv_part = jnp.sum(jnp.square(factor_inv.astype(jnp.float32)), axis=1)
    variance = lax.psum(linv_part - weighted, "wide")
    return (cross_f.astype(jnp.bfloat16), variance)


X, Y, ZL, ZH = 1, 2, 4, 8
NGRP = 4
SPLIT = 192
TAIL = 16
DEST = (0, 3, 1, 2)
MIB = 1024 * 1024


def swap_cores(value, name):
    with jax.named_scope(name):
        return lax.ppermute(value, "narrow", [(0, 1), (1, 0)])


def hop(value, mask, name):
    size = lax.axis_size("wide")
    with jax.named_scope(name):
        return lax.ppermute(value, "wide", [(i, i ^ mask) for i in range(size)])


def after(value, *earlier):
    return lax.optimization_barrier((value, *earlier))[0]


def lead(values, micros):
    def body(*refs):
        pass

    return pl.pallas_call(
        body,
        out_shape=[jax.ShapeDtypeStruct(v.shape, v.dtype) for v in values],
        in_specs=[ANY] * len(values),
        out_specs=[ANY] * len(values),
        input_output_aliases={i: i for i in range(len(values))},
        compiler_params=pltpu.CompilerParams(vmem_limit_bytes=2 * MIB),
        cost_estimate=pl.CostEstimate(
            flops=int(micros * 1.15e9), bytes_accessed=0, transcendentals=0
        ),
        name="lead",
    )(*values)


def pick(structure_ref, n, j, first):
    nblocks = structure_ref.shape[1]
    start = jnp.where(n == 0, 0, nblocks - first)
    return structure_ref[n, lax.rem(start + j, nblocks)]


def pack_first(structure, panel, inverse, first):
    half_blocks = panel.shape[1] // BLK

    def body(st, panel_ref, inv_ref, out, *pieces):
        n = lax.axis_index("narrow")
        for j in range(first):
            row = pl.multiple_of(lax.rem(pick(st, n, j, first), half_blocks) * BLK, BLK)
            out[j * BLK : (j + 1) * BLK, :] = panel_ref[n, pl.ds(row, BLK), :]
        pieces[0][...] = inv_ref[:SPLIT, :]
        pieces[1][...] = inv_ref[SPLIT:, :]

    width = inverse.shape[1]
    return pl.pallas_call(
        body,
        out_shape=[
            jax.ShapeDtypeStruct((first * BLK, panel.shape[2]), panel.dtype),
            jax.ShapeDtypeStruct((SPLIT, width), inverse.dtype),
            jax.ShapeDtypeStruct((BLK - SPLIT, width), inverse.dtype),
        ],
        in_specs=[SMEM, VMEM, VMEM],
        out_specs=[VMEM] * 3,
        compiler_params=pltpu.CompilerParams(vmem_limit_bytes=8 * MIB),
        name="pack_first",
    )(structure, panel, inverse)


def pack_rest(structure, panel, other, first):
    nblocks = structure.shape[1]
    half_blocks = panel.shape[1] // BLK

    def body(st, panel_ref, other_ref, out0, out1):
        n = lax.axis_index("narrow")
        for out in (out0, out1):
            pad = out.shape[0] - (nblocks - first) * BLK
            out[(nblocks - first) * BLK :, :] = jnp.zeros((pad, LANES), out.dtype)
        for j in range(nblocks - first):
            b = pick(st, n, first + j, first)
            row = pl.multiple_of(lax.rem(b, half_blocks) * BLK, BLK)
            mine = lax.div(b, half_blocks) == n
            rows = slice(j * BLK, (j + 1) * BLK)

            @pl.when(mine)
            def _():
                out0[rows, :] = panel_ref[n, pl.ds(row, BLK), :LANES]
                out1[rows, :] = panel_ref[n, pl.ds(row, BLK), LANES:]

            @pl.when(jnp.logical_not(mine))
            def _():
                out0[rows, :] = other_ref[pl.ds(row, BLK), :LANES]
                out1[rows, :] = other_ref[pl.ds(row, BLK), LANES:]

    rows = (nblocks - first) * BLK
    return pl.pallas_call(
        body,
        out_shape=(
            jax.ShapeDtypeStruct((rows + TAIL, LANES), panel.dtype),
            jax.ShapeDtypeStruct((rows + 2 * TAIL, LANES), panel.dtype),
        ),
        in_specs=[SMEM, VMEM, VMEM],
        out_specs=[VMEM, VMEM],
        compiler_params=pltpu.CompilerParams(vmem_limit_bytes=8 * MIB),
        name="pack_rest",
    )(structure, panel, other)


def stack_rows(pieces):
    rows = sum(piece.shape[0] for piece in pieces)

    def body(*refs):
        at = 0
        for ref in refs[:-1]:
            refs[-1][at : at + ref.shape[0], :] = ref[...]
            at += ref.shape[0]

    return pl.pallas_call(
        body,
        out_shape=jax.ShapeDtypeStruct((rows, pieces[0].shape[1]), pieces[0].dtype),
        in_specs=[VMEM] * len(pieces),
        out_specs=VMEM,
        compiler_params=pltpu.CompilerParams(vmem_limit_bytes=8 * MIB),
        name="stack_rows",
    )(*pieces)


def pack_inverse(structure, owns, others, first):
    nblocks = structure.shape[1]
    half_blocks = owns[0].shape[1] // BLK
    count = len(owns)
    runs, row = [], 0
    for p, own in enumerate(owns):
        at = 0
        while at < own.shape[0]:
            rows = min(own.shape[0] - at, BLK - row % BLK)
            runs.append((p, at, row // BLK, row % BLK, rows))
            at, row = at + rows, row + rows

    def body(st, *refs):
        out = refs[2 * count]
        n = lax.axis_index("narrow")
        for j in range(nblocks):
            b = pick(st, n, j, first)
            col = pl.multiple_of(lax.rem(b, half_blocks) * BLK, BLK)
            mine = lax.div(b, half_blocks) == n

            def move(sources, j=j, col=col):
                for p, at, d, top, rows in runs:
                    out[d, top : top + rows, j * BLK : (j + 1) * BLK] = sources[p][
                        at : at + rows, pl.ds(col, BLK)
                    ]

            pl.when(mine)(lambda move=move: move(refs[:count]))
            pl.when(jnp.logical_not(mine))(lambda move=move: move(refs[count : 2 * count]))

    return pl.pallas_call(
        body,
        out_shape=jax.ShapeDtypeStruct((NGRP, BLK, nblocks * BLK), owns[0].dtype),
        in_specs=[SMEM] + [VMEM] * (2 * count),
        out_specs=VMEM,
        compiler_params=pltpu.CompilerParams(vmem_limit_bytes=18 * MIB),
        name="pack_inverse",
    )(structure, *owns, *others)


def products(structure, sel, firsts, rests, chunk, near=None):
    nblocks = structure.shape[1]
    early = firsts[0].shape[0]
    late = sel.shape[2] - early
    first = early // BLK
    spot = slice(chunk * LANES, (chunk + 1) * LANES)

    def body(st, sel_ref, f0, f1, r0, r1, *refs):
        result, total, acc = refs[-3:]
        n = lax.axis_index("narrow")
        w = lax.axis_index("wide")
        x = lax.bitwise_and(w, 1)
        total[...] = jnp.zeros_like(total)
        depth = sel_ref.shape[2]
        rows = sel_ref[...].reshape(NGRP * BLK, depth)
        acc[...] = jnp.dot(
            rows[:, :early],
            jnp.concatenate([f0[:, spot], f1[:, spot]], axis=1),
            preferred_element_type=jnp.float32,
        ) + jnp.dot(
            rows[:, early:],
            jnp.concatenate([r0[:late, :], r1[:late, :]], axis=1),
            preferred_element_type=jnp.float32,
        )
        for d in range(NGRP):
            row = lax.bitwise_xor(w, (d % 2) * Y + (d // 2) * ZL)
            pos = jnp.int32(0)
            inside = jnp.int32(0)
            for j in range(nblocks):
                hit = (pick(st, n, j, first) == row).astype(jnp.int32)
                pos = pos + j * hit
                inside = inside + hit

            @pl.when(inside == 0)
            def _(d=d):
                result[d] = jnp.zeros(result.shape[1:], result.dtype)

            @pl.when(inside > 0)
            def _(d=d, pos=pos):
                for dx in range(2):
                    part = acc[d * BLK : (d + 1) * BLK, dx * LANES : (dx + 1) * LANES]
                    slot = lax.bitwise_xor(x, dx)

                    def weigh(rows, part=part, slot=slot):
                        added = jnp.sum(part * rows.astype(jnp.float32), axis=0, keepdims=True)
                        total[slot] += added

                    @pl.when(pos < first)
                    def _():
                        at = pl.multiple_of(pos * BLK, BLK)
                        weigh((f0, f1)[dx][pl.ds(at, BLK), spot])

                    @pl.when(pos >= first)
                    def _():
                        at = pl.multiple_of((pos - first) * BLK, BLK)
                        weigh((r0, r1)[dx][pl.ds(at, BLK), :])

                    at = pl.multiple_of(slot * LANES, LANES)
                    result[d, pl.ds(at, LANES), :] = (-part).astype(result.dtype).T

        for slot in range(2):
            left, terms = total[slot], []
            for _ in range(3):
                term = left.astype(result.dtype).astype(jnp.float32)
                terms.append(term)
                left = left - term
            tile = jnp.concatenate(terms + [jnp.zeros((TAIL - 3, LANES), jnp.float32)], axis=0)
            for d in range(NGRP):
                result[d, 2 * LANES :, slot * LANES : (slot + 1) * LANES] = tile.astype(
                    result.dtype
                )
        if near is None:
            refs[0][...] = result[...]
            return
        near_ref, kept, sent = refs[:3]
        stay = n == lax.div(w, ZH)

        @pl.when(stay)
        def _():
            kept[...] = near_ref[...]
            sent[...] = result[...]

        @pl.when(jnp.logical_not(stay))
        def _():
            kept[...] = result[...]
            sent[...] = near_ref[...]

    out = jax.ShapeDtypeStruct((NGRP, 2 * LANES + TAIL, BLK), sel.dtype)
    again = () if near is None else (near,)
    return pl.pallas_call(
        body,
        out_shape=out if near is None else [out, out],
        in_specs=[SMEM] + [VMEM] * (5 + len(again)),
        out_specs=VMEM if near is None else [VMEM, VMEM],
        scratch_shapes=[
            pltpu.VMEM(out.shape, out.dtype),
            pltpu.VMEM((2, 1, LANES), jnp.float32),
            pltpu.VMEM((NGRP * BLK, 2 * LANES), jnp.float32),
        ],
        compiler_params=pltpu.CompilerParams(vmem_limit_bytes=16 * MIB),
        cost_estimate=pl.CostEstimate(flops=0, bytes_accessed=0, transcendentals=0),
        name="products",
    )(structure, sel, *firsts, *rests, *again)


def bundle(ours, theirs):
    def body(our_ref, their_ref, *outs):
        for d, out in zip(DEST, outs):
            out[0] = our_ref[d]
            out[1] = their_ref[d]

    shape = jax.ShapeDtypeStruct((2, *ours.shape[1:]), ours.dtype)
    return pl.pallas_call(
        body,
        out_shape=[shape] * NGRP,
        in_specs=[VMEM, VMEM],
        out_specs=[VMEM] * NGRP,
        compiler_params=pltpu.CompilerParams(vmem_limit_bytes=8 * MIB),
        name="bundle",
    )(ours, theirs)


def squares(factor_inv):
    sups, rows, cols = factor_inv.shape
    half = cols // 2

    def body(in_ref, out_ref):
        for k in range(sups):
            value = in_ref[k].astype(jnp.float32)
            out_ref[k : k + 1, :] = jnp.sum(value * value, axis=0, keepdims=True)

    return pl.pallas_call(
        body,
        out_shape=jax.ShapeDtypeStruct((sups, cols), jnp.float32),
        grid=(2,),
        in_specs=[pl.BlockSpec((sups, rows, half), lambda c: (0, 0, c))],
        out_specs=pl.BlockSpec((sups, half), lambda c: (0, c)),
        compiler_params=pltpu.CompilerParams(vmem_limit_bytes=8 * MIB),
        name="squares",
    )(factor_inv)


def add_sums(base, messages, chunk):
    cols = base.shape[1]

    def body(base_ref, *refs):
        out = refs[-1]
        n = lax.axis_index("narrow")
        group = lax.rem(lax.div(lax.axis_index("wide"), Y), NGRP)
        out[...] = base_ref[...]
        for d, ref in zip(DEST, refs):
            source = lax.bitwise_xor(group, d)
            for k in range(2):
                which = (n != k).astype(jnp.int32)
                tile = ref[which, 2 * LANES :, :].astype(jnp.float32)
                value = tile[0:1] + (tile[1:2] + tile[2:3])
                for xx in range(2):
                    at = source * (cols // NGRP) + (2 * xx + chunk) * LANES
                    spot = pl.ds(pl.multiple_of(at, LANES), LANES)
                    out[k : k + 1, spot] += value[:, xx * LANES : (xx + 1) * LANES]

    return pl.pallas_call(
        body,
        out_shape=jax.ShapeDtypeStruct(base.shape, jnp.float32),
        in_specs=[VMEM] * (1 + NGRP),
        out_specs=VMEM,
        compiler_params=pltpu.CompilerParams(vmem_limit_bytes=4 * MIB),
        name="add_sums",
    )(base, *messages)


def assemble(messages, chunk, held):
    tall = 4 * LANES
    rows_total = 2 * 2 * NGRP * tall

    def body(*refs):
        msg_refs = refs[:NGRP]
        out, wide_buf, narrow_buf, sem = refs[-4:]
        n = lax.axis_index("narrow")
        w = lax.axis_index("wide")
        copies = []
        for d, msg_ref in zip(DEST, msg_refs):
            source = lax.bitwise_xor(lax.rem(lax.div(w, Y), NGRP), d)
            for xx in range(2):
                slot = 2 * d + xx
                for k in range(2):
                    which = (n != k).astype(jnp.int32)
                    value = msg_ref[which, xx * LANES : (xx + 1) * LANES, :].astype(
                        jnp.float32
                    )
                    for lt in range(2):
                        wide_buf[slot, pl.ds(2 * lt + k, LANES, stride=4), :] = value[
                            :, lt * LANES : (lt + 1) * LANES
                        ]
                narrow_buf[slot] = wide_buf[slot].astype(narrow_buf.dtype)
                row = pl.multiple_of(((source * 2 + xx) * 2 + chunk) * tall, tall)
                copy = pltpu.make_async_copy(
                    narrow_buf.at[slot], out.at[pl.ds(row, tall), :], sem.at[slot]
                )
                copy.start()
                copies.append(copy)
        for copy in copies:
            copy.wait()

    extra = () if held is None else (held,)
    return pl.pallas_call(
        body,
        out_shape=jax.ShapeDtypeStruct((rows_total, LANES), messages[0].dtype),
        in_specs=[VMEM] * NGRP + [ANY] * len(extra),
        out_specs=ANY,
        scratch_shapes=[
            pltpu.VMEM((2 * NGRP, tall, LANES), jnp.float32),
            pltpu.VMEM((2 * NGRP, tall, LANES), messages[0].dtype),
            pltpu.SemaphoreType.DMA((2 * NGRP,)),
        ],
        input_output_aliases={NGRP: 0} if extra else {},
        compiler_params=pltpu.CompilerParams(vmem_limit_bytes=8 * MIB),
        name="assemble",
    )(*messages, *extra)


def per_device_grid(inverse, panel, factor_inv, structure):
    first = structure.shape[1] - panel.shape[1] // BLK
    size = lax.axis_size("wide")
    n = lax.axis_index("narrow")
    f_own, top, bottom = pack_first(structure, panel, inverse, first)
    other = swap_cores(lax.dynamic_index_in_dim(panel, 1 - n, 0, keepdims=False), "panel_swap")
    r_own = pack_rest(structure, panel, other, first)
    linv = squares(factor_inv)
    f_z = hop(f_own, ZH, "first_z")
    f_x = hop(f_own, X, "first_x")
    a_z0 = hop(top, ZL, "inv_z0")
    a_y = hop(inverse, Y, "inv_y")
    a_y, f_z, f_x, *r_own = lax.optimization_barrier((a_y, f_z, f_x, *r_own))
    r_z1 = hop(r_own[1], ZH, "rest1_z")
    r_z0 = hop(r_own[0], ZH, "rest0_z")
    a_z1 = hop(after(bottom, f_z), ZL, "inv_z1")
    f_xz = hop(f_z, X, "first_xz")
    r_x0 = hop(r_own[0], X, "rest0_x")
    a_yz0 = hop(a_z0, Y, "inv_yz0")
    a_yz1 = hop(a_z1, Y, "inv_yz1")
    most = stack_rows([inverse, a_y, a_z0])
    r_z0, r_x0, f_xz, a_z1, a_yz0, a_yz1, most, *r_own = lax.optimization_barrier(
        (r_z0, r_x0, f_xz, a_z1, a_yz0, a_yz1, most, *r_own)
    )
    r_xz0 = hop(r_z0, X, "rest0_xz")
    r_x1 = hop(r_own[1], X, "rest1_x")
    more = stack_rows([a_z1, a_yz0, a_yz1])
    s_most = swap_cores(most, "inv_swap")
    s_more = swap_cores(more, "inv_swap_more")
    sel = pack_inverse(structure, (most, more), (s_most, s_more), first)
    linv = after(linv, more)
    for mask in (Y, ZL):
        linv = linv + hop(linv, mask, f"squares_{mask}")
    r_z1 = lead([r_z1], 20)[0]
    r_x1 = lead([r_x1], 10)[0]
    r_x1, linv = lax.optimization_barrier((r_x1, linv))

    def deliver(kept, sent, c):
        messages = bundle(kept, swap_cores(sent, f"cross{c}_swap"))
        return [messages[0]] + [
            hop(message, (d % 2) * Y + (d // 2) * ZL, f"cross{c}_{d}")
            for d, message in zip(DEST[1:], messages[1:])
        ]

    near = products(structure, sel, (f_own, f_x), (r_own[0], r_x0), 0)
    kept, sent = products(structure, sel, (f_z, f_xz), (r_z0, r_xz0), 0, near)
    messages = deliver(kept, sent, 0)
    r_xz1 = hop(after(r_z1, kept), X, "rest1_xz")
    near = products(structure, sel, (f_own, f_x), (r_own[1], r_x1), 1)
    messages[1:] = lead(messages[1:], 5)
    kept, sent = products(structure, sel, (f_z, f_xz), (r_z1, r_xz1), 1, near)
    held = assemble(messages, 0, None)
    variance = add_sums(linv, messages, 0)
    messages = deliver(after(kept, variance), sent, 1)
    variance = add_sums(variance, messages, 1)
    held = assemble(messages, 1, held)
    hops = [hop(variance, mask, f"variance_{mask}") for mask in (X, ZH, X | ZH)]
    variance = variance + hops[0] + hops[1] + hops[2]
    half = panel.shape[2] * size // 2
    cross = held.reshape(half, 2, 2, LANES).transpose(0, 2, 1, 3).reshape(half, 2, BLK)
    return cross, variance


def solution(mesh):
    in_specs = (P("wide", "narrow"), P(None, "narrow", "wide"), P(None, "wide", "narrow"), P())
    out_specs = (P("narrow", None, "wide"), P(None, "narrow"))

    def run(inverse, panel, factor_inv, structure):
        fits = (
            mesh.shape["wide"] == 16
            and mesh.shape["narrow"] == 2 == panel.shape[0]
            and panel.shape[2] == 16 * BLK == inverse.shape[0]
        )
        return jax.shard_map(
            per_device_grid if fits else per_device_general,
            mesh=mesh,
            in_specs=in_specs,
            out_specs=out_specs,
            check_vma=False,
        )(inverse, panel, factor_inv, structure)

    return run
```

```python
import jax
import jax.numpy as jnp
from jax import lax
from jax.experimental import pallas as pl
from jax.experimental.pallas import tpu as pltpu
from jax.sharding import PartitionSpec as P

BLK = 256
LANES = 128
ANY = pl.BlockSpec(memory_space=pl.ANY)
VMEM = pl.BlockSpec(memory_space=pltpu.VMEM)
SMEM = pl.BlockSpec(memory_space=pltpu.SMEM)


def spread(value, axis, source):
    kept = jnp.where(lax.axis_index(axis) == source, value, 0).astype(value.dtype)
    return lax.psum(kept, axis)


def block_partial(gathered, inverse, row_inside, col_inside, first_row, row_count):
    local_blocks = inverse.shape[1] // BLK
    running = jnp.zeros((row_count, BLK), jnp.float32)
    for blk_index in range(local_blocks):

        def product(blk_index=blk_index):
            panel_piece = lax.dynamic_slice(
                gathered, (blk_index * BLK, first_row), (BLK, row_count)
            )
            block_z = inverse[:, blk_index * BLK : (blk_index + 1) * BLK]
            return lax.dot_general(
                panel_piece, block_z, (((0,), (1,)), ((), ())), preferred_element_type=jnp.float32
            )

        def skipped():
            return jnp.zeros((row_count, BLK), jnp.float32)

        running = running + lax.cond(row_inside & col_inside[blk_index], product, skipped)
    return -running


def per_device_general(inverse, panel, factor_inv, structure):
    wide_count = lax.axis_size("wide")
    narrow_count = lax.axis_size("narrow")
    nsup_count = panel.shape[0]
    kw_total = panel.shape[2] * wide_count
    kw_local = kw_total // narrow_count
    local_blocks = inverse.shape[1] // BLK
    row_index = lax.axis_index("wide")
    col_first = lax.axis_index("narrow") * local_blocks
    col_ids = col_first + jnp.arange(local_blocks, dtype=jnp.int32)
    row_inside = jnp.any(structure == row_index, axis=1)
    col_inside = jnp.any(structure[:, :, None] == col_ids[None, None, :], axis=1)
    root_index = row_index // local_blocks
    offset = (row_index - root_index * local_blocks) * BLK
    cross_parts = []
    own_parts = []
    for sup_index in range(nsup_count):
        gathered_one = lax.all_gather(panel[sup_index], "wide", axis=1, tiled=True)

        def one_term(first_row, row_count, gathered_one=gathered_one, sup_index=sup_index):
            return block_partial(
                gathered_one,
                inverse,
                row_inside[sup_index],
                col_inside[sup_index],
                first_row,
                row_count,
            )

        cross_parts.append(
            lax.psum_scatter(
                one_term(jnp.int32(0), kw_local * lax.axis_size("narrow")),
                "narrow",
                scatter_dimension=0,
                tiled=True,
            )
        )
        own_parts.append(lax.dynamic_slice_in_dim(gathered_one, offset, BLK, axis=0))
    cross_f = jnp.stack(cross_parts, axis=1)
    own_rows = jnp.stack(own_parts)
    owner_panel = spread(own_rows, "narrow", root_index)
    owner_slice = lax.dynamic_slice_in_dim(
        owner_panel, lax.axis_index("narrow") * kw_local, kw_local, axis=2
    )
    weighted = jnp.einsum("kia,aki->ka", owner_slice.astype(jnp.float32), cross_f)
    linv_part = jnp.sum(jnp.square(factor_inv.astype(jnp.float32)), axis=1)
    variance = lax.psum(linv_part - weighted, "wide")
    return (cross_f.astype(jnp.bfloat16), variance)


X, Y, ZL, ZH = 1, 2, 4, 8
NGRP = 4
SPLIT = 192
TAIL = 16
DEST = (0, 3, 1, 2)
MIB = 1024 * 1024


def swap_cores(value, name):
    with jax.named_scope(name):
        return lax.ppermute(value, "narrow", [(0, 1), (1, 0)])


def hop(value, mask, name):
    size = lax.axis_size("wide")
    with jax.named_scope(name):
        return lax.ppermute(value, "wide", [(i, i ^ mask) for i in range(size)])


def after(value, *earlier):
    return lax.optimization_barrier((value, *earlier))[0]


def lead(values, micros):
    def body(*refs):
        pass

    return pl.pallas_call(
        body,
        out_shape=[jax.ShapeDtypeStruct(v.shape, v.dtype) for v in values],
        in_specs=[ANY] * len(values),
        out_specs=[ANY] * len(values),
        input_output_aliases={i: i for i in range(len(values))},
        compiler_params=pltpu.CompilerParams(vmem_limit_bytes=2 * MIB),
        cost_estimate=pl.CostEstimate(
            flops=int(micros * 1.15e9), bytes_accessed=0, transcendentals=0
        ),
        name="lead",
    )(*values)


def pick(structure_ref, n, j, first):
    nblocks = structure_ref.shape[1]
    start = jnp.where(n == 0, 0, nblocks - first)
    return structure_ref[n, lax.rem(start + j, nblocks)]


def pack_first(structure, panel, inverse, first):
    half_blocks = panel.shape[1] // BLK

    def body(st, panel_ref, inv_ref, out, *pieces):
        n = lax.axis_index("narrow")
        for j in range(first):
            row = pl.multiple_of(lax.rem(pick(st, n, j, first), half_blocks) * BLK, BLK)
            out[j * BLK : (j + 1) * BLK, :] = panel_ref[n, pl.ds(row, BLK), :]
        pieces[0][...] = inv_ref[:SPLIT, :]
        pieces[1][...] = inv_ref[SPLIT:, :]

    width = inverse.shape[1]
    return pl.pallas_call(
        body,
        out_shape=[
            jax.ShapeDtypeStruct((first * BLK, panel.shape[2]), panel.dtype),
            jax.ShapeDtypeStruct((SPLIT, width), inverse.dtype),
            jax.ShapeDtypeStruct((BLK - SPLIT, width), inverse.dtype),
        ],
        in_specs=[SMEM, VMEM, VMEM],
        out_specs=[VMEM] * 3,
        compiler_params=pltpu.CompilerParams(vmem_limit_bytes=8 * MIB),
        name="pack_first",
    )(structure, panel, inverse)


def pack_rest(structure, panel, other, first):
    nblocks = structure.shape[1]
    half_blocks = panel.shape[1] // BLK

    def body(st, panel_ref, other_ref, out0, out1):
        n = lax.axis_index("narrow")
        out0[(nblocks - first) * BLK :, :] = jnp.zeros((TAIL, LANES), out0.dtype)
        for j in range(nblocks - first):
            b = pick(st, n, first + j, first)
            row = pl.multiple_of(lax.rem(b, half_blocks) * BLK, BLK)
            mine = lax.div(b, half_blocks) == n
            rows = slice(j * BLK, (j + 1) * BLK)

            @pl.when(mine)
            def _():
                out0[rows, :] = panel_ref[n, pl.ds(row, BLK), :LANES]
                out1[rows, :] = panel_ref[n, pl.ds(row, BLK), LANES:]

            @pl.when(jnp.logical_not(mine))
            def _():
                out0[rows, :] = other_ref[pl.ds(row, BLK), :LANES]
                out1[rows, :] = other_ref[pl.ds(row, BLK), LANES:]

    rows = (nblocks - first) * BLK
    return pl.pallas_call(
        body,
        out_shape=(
            jax.ShapeDtypeStruct((rows + TAIL, LANES), panel.dtype),
            jax.ShapeDtypeStruct((rows, LANES), panel.dtype),
        ),
        in_specs=[SMEM, VMEM, VMEM],
        out_specs=[VMEM, VMEM],
        compiler_params=pltpu.CompilerParams(vmem_limit_bytes=8 * MIB),
        name="pack_rest",
    )(structure, panel, other)


def stack_rows(pieces):
    rows = sum(piece.shape[0] for piece in pieces)

    def body(*refs):
        at = 0
        for ref in refs[:-1]:
            refs[-1][at : at + ref.shape[0], :] = ref[...]
            at += ref.shape[0]

    return pl.pallas_call(
        body,
        out_shape=jax.ShapeDtypeStruct((rows, pieces[0].shape[1]), pieces[0].dtype),
        in_specs=[VMEM] * len(pieces),
        out_specs=VMEM,
        compiler_params=pltpu.CompilerParams(vmem_limit_bytes=8 * MIB),
        name="stack_rows",
    )(*pieces)


def pack_inverse(structure, owns, others, first):
    nblocks = structure.shape[1]
    half_blocks = owns[0].shape[1] // BLK
    count = len(owns)
    runs, row = [], 0
    for p, own in enumerate(owns):
        at = 0
        while at < own.shape[0]:
            rows = min(own.shape[0] - at, BLK - row % BLK)
            runs.append((p, at, row // BLK, row % BLK, rows))
            at, row = at + rows, row + rows

    def body(st, *refs):
        out = refs[2 * count]
        n = lax.axis_index("narrow")
        for j in range(nblocks):
            b = pick(st, n, j, first)
            col = pl.multiple_of(lax.rem(b, half_blocks) * BLK, BLK)
            mine = lax.div(b, half_blocks) == n

            def move(sources, j=j, col=col):
                for p, at, d, top, rows in runs:
                    out[d, top : top + rows, j * BLK : (j + 1) * BLK] = sources[p][
                        at : at + rows, pl.ds(col, BLK)
                    ]

            pl.when(mine)(lambda move=move: move(refs[:count]))
            pl.when(jnp.logical_not(mine))(lambda move=move: move(refs[count : 2 * count]))

    return pl.pallas_call(
        body,
        out_shape=jax.ShapeDtypeStruct((NGRP, BLK, nblocks * BLK), owns[0].dtype),
        in_specs=[SMEM] + [VMEM] * (2 * count),
        out_specs=VMEM,
        compiler_params=pltpu.CompilerParams(vmem_limit_bytes=18 * MIB),
        name="pack_inverse",
    )(structure, *owns, *others)


def products(structure, sel, firsts, rests, chunk, near=None):
    nblocks = structure.shape[1]
    early = firsts[0].shape[0]
    late = sel.shape[2] - early
    first = early // BLK
    spot = slice(chunk * LANES, (chunk + 1) * LANES)

    def body(st, sel_ref, f0, f1, r0, r1, *refs):
        result, total, acc = refs[-3:]
        n = lax.axis_index("narrow")
        w = lax.axis_index("wide")
        x = lax.bitwise_and(w, 1)
        total[...] = jnp.zeros_like(total)
        depth = sel_ref.shape[2]
        rows = sel_ref[...].reshape(NGRP * BLK, depth)
        acc[...] = jnp.dot(
            rows[:, :early],
            jnp.concatenate([f0[:, spot], f1[:, spot]], axis=1),
            preferred_element_type=jnp.float32,
        ) + jnp.dot(
            rows[:, early:],
            jnp.concatenate([r0[:late, :], r1[:late, :]], axis=1),
            preferred_element_type=jnp.float32,
        )
        for d in range(NGRP):
            row = lax.bitwise_xor(w, (d % 2) * Y + (d // 2) * ZL)
            pos = jnp.int32(0)
            inside = jnp.int32(0)
            for j in range(nblocks):
                hit = (pick(st, n, j, first) == row).astype(jnp.int32)
                pos = pos + j * hit
                inside = inside + hit

            @pl.when(inside == 0)
            def _(d=d):
                result[d] = jnp.zeros(result.shape[1:], result.dtype)

            @pl.when(inside > 0)
            def _(d=d, pos=pos):
                for dx in range(2):
                    part = acc[d * BLK : (d + 1) * BLK, dx * LANES : (dx + 1) * LANES]
                    slot = lax.bitwise_xor(x, dx)

                    def weigh(rows, part=part, slot=slot):
                        added = jnp.sum(part * rows.astype(jnp.float32), axis=0, keepdims=True)
                        total[slot] += added

                    @pl.when(pos < first)
                    def _():
                        at = pl.multiple_of(pos * BLK, BLK)
                        weigh((f0, f1)[dx][pl.ds(at, BLK), spot])

                    @pl.when(pos >= first)
                    def _():
                        at = pl.multiple_of((pos - first) * BLK, BLK)
                        weigh((r0, r1)[dx][pl.ds(at, BLK), :])

                    at = pl.multiple_of(slot * LANES, LANES)
                    result[d, pl.ds(at, LANES), :] = (-part).astype(result.dtype).T

        for slot in range(2):
            left, terms = total[slot], []
            for _ in range(3):
                term = left.astype(result.dtype).astype(jnp.float32)
                terms.append(term)
                left = left - term
            tile = jnp.concatenate(terms + [jnp.zeros((TAIL - 3, LANES), jnp.float32)], axis=0)
            for d in range(NGRP):
                result[d, 2 * LANES :, slot * LANES : (slot + 1) * LANES] = tile.astype(
                    result.dtype
                )
        if near is None:
            refs[0][...] = result[...]
            return
        near_ref, kept, sent = refs[:3]
        stay = n == lax.div(w, ZH)

        @pl.when(stay)
        def _():
            kept[...] = near_ref[...]
            sent[...] = result[...]

        @pl.when(jnp.logical_not(stay))
        def _():
            kept[...] = result[...]
            sent[...] = near_ref[...]

    out = jax.ShapeDtypeStruct((NGRP, 2 * LANES + TAIL, BLK), sel.dtype)
    again = () if near is None else (near,)
    return pl.pallas_call(
        body,
        out_shape=out if near is None else [out, out],
        in_specs=[SMEM] + [VMEM] * (5 + len(again)),
        out_specs=VMEM if near is None else [VMEM, VMEM],
        scratch_shapes=[
            pltpu.VMEM(out.shape, out.dtype),
            pltpu.VMEM((2, 1, LANES), jnp.float32),
            pltpu.VMEM((NGRP * BLK, 2 * LANES), jnp.float32),
        ],
        compiler_params=pltpu.CompilerParams(vmem_limit_bytes=16 * MIB),
        cost_estimate=pl.CostEstimate(flops=0, bytes_accessed=0, transcendentals=0),
        name="products",
    )(structure, sel, *firsts, *rests, *again)


def bundle(ours, theirs):
    def body(our_ref, their_ref, *outs):
        for d, out in zip(DEST, outs):
            out[0] = our_ref[d]
            out[1] = their_ref[d]

    shape = jax.ShapeDtypeStruct((2, *ours.shape[1:]), ours.dtype)
    return pl.pallas_call(
        body,
        out_shape=[shape] * NGRP,
        in_specs=[VMEM, VMEM],
        out_specs=[VMEM] * NGRP,
        compiler_params=pltpu.CompilerParams(vmem_limit_bytes=8 * MIB),
        name="bundle",
    )(ours, theirs)


def squares(factor_inv):
    sups, rows, cols = factor_inv.shape
    half = cols // 2

    def body(in_ref, out_ref):
        for k in range(sups):
            value = in_ref[k].astype(jnp.float32)
            out_ref[k : k + 1, :] = jnp.sum(value * value, axis=0, keepdims=True)

    return pl.pallas_call(
        body,
        out_shape=jax.ShapeDtypeStruct((sups, cols), jnp.float32),
        grid=(2,),
        in_specs=[pl.BlockSpec((sups, rows, half), lambda c: (0, 0, c))],
        out_specs=pl.BlockSpec((sups, half), lambda c: (0, c)),
        compiler_params=pltpu.CompilerParams(vmem_limit_bytes=8 * MIB),
        name="squares",
    )(factor_inv)


def add_sums(base, messages, chunk):
    cols = base.shape[1]

    def body(base_ref, *refs):
        out = refs[-1]
        n = lax.axis_index("narrow")
        group = lax.rem(lax.div(lax.axis_index("wide"), Y), NGRP)
        out[...] = base_ref[...]
        for d, ref in zip(DEST, refs):
            source = lax.bitwise_xor(group, d)
            for k in range(2):
                which = (n != k).astype(jnp.int32)
                tile = ref[which, 2 * LANES :, :].astype(jnp.float32)
                value = tile[0:1] + (tile[1:2] + tile[2:3])
                for xx in range(2):
                    at = source * (cols // NGRP) + (2 * xx + chunk) * LANES
                    spot = pl.ds(pl.multiple_of(at, LANES), LANES)
                    out[k : k + 1, spot] += value[:, xx * LANES : (xx + 1) * LANES]

    return pl.pallas_call(
        body,
        out_shape=jax.ShapeDtypeStruct(base.shape, jnp.float32),
        in_specs=[VMEM] * (1 + NGRP),
        out_specs=VMEM,
        compiler_params=pltpu.CompilerParams(vmem_limit_bytes=4 * MIB),
        name="add_sums",
    )(base, *messages)


def assemble(messages, chunk, held):
    tall = 4 * LANES
    rows_total = 2 * 2 * NGRP * tall

    def body(*refs):
        msg_refs = refs[:NGRP]
        out, wide_buf, narrow_buf, sem = refs[-4:]
        n = lax.axis_index("narrow")
        w = lax.axis_index("wide")
        copies = []
        for d, msg_ref in zip(DEST, msg_refs):
            source = lax.bitwise_xor(lax.rem(lax.div(w, Y), NGRP), d)
            for xx in range(2):
                slot = 2 * d + xx
                for k in range(2):
                    which = (n != k).astype(jnp.int32)
                    value = msg_ref[which, xx * LANES : (xx + 1) * LANES, :].astype(
                        jnp.float32
                    )
                    for lt in range(2):
                        wide_buf[slot, pl.ds(2 * lt + k, LANES, stride=4), :] = value[
                            :, lt * LANES : (lt + 1) * LANES
                        ]
                narrow_buf[slot] = wide_buf[slot].astype(narrow_buf.dtype)
                row = pl.multiple_of(((source * 2 + xx) * 2 + chunk) * tall, tall)
                copy = pltpu.make_async_copy(
                    narrow_buf.at[slot], out.at[pl.ds(row, tall), :], sem.at[slot]
                )
                copy.start()
                copies.append(copy)
        for copy in copies:
            copy.wait()

    extra = () if held is None else (held,)
    return pl.pallas_call(
        body,
        out_shape=jax.ShapeDtypeStruct((rows_total, LANES), messages[0].dtype),
        in_specs=[VMEM] * NGRP + [ANY] * len(extra),
        out_specs=ANY,
        scratch_shapes=[
            pltpu.VMEM((2 * NGRP, tall, LANES), jnp.float32),
            pltpu.VMEM((2 * NGRP, tall, LANES), messages[0].dtype),
            pltpu.SemaphoreType.DMA((2 * NGRP,)),
        ],
        input_output_aliases={NGRP: 0} if extra else {},
        compiler_params=pltpu.CompilerParams(vmem_limit_bytes=8 * MIB),
        name="assemble",
    )(*messages, *extra)


def per_device_grid(inverse, panel, factor_inv, structure):
    first = structure.shape[1] - panel.shape[1] // BLK
    size = lax.axis_size("wide")
    n = lax.axis_index("narrow")
    f_own, top, bottom = pack_first(structure, panel, inverse, first)
    other = swap_cores(lax.dynamic_index_in_dim(panel, 1 - n, 0, keepdims=False), "panel_swap")
    r_own = pack_rest(structure, panel, other, first)
    linv = squares(factor_inv)
    f_z = hop(f_own, ZH, "first_z")
    f_x = hop(f_own, X, "first_x")
    a_z0 = hop(top, ZL, "inv_z0")
    a_y = hop(inverse, Y, "inv_y")
    a_y, f_z, f_x, *r_own = lax.optimization_barrier((a_y, f_z, f_x, *r_own))
    r_z1 = hop(r_own[1], ZH, "rest1_z")
    r_z0 = hop(r_own[0], ZH, "rest0_z")
    a_z1 = hop(after(bottom, f_z), ZL, "inv_z1")
    f_xz = hop(f_z, X, "first_xz")
    r_x0 = hop(r_own[0], X, "rest0_x")
    a_yz0 = hop(a_z0, Y, "inv_yz0")
    a_yz1 = hop(a_z1, Y, "inv_yz1")
    most = stack_rows([inverse, a_y, a_z0])
    r_z0, r_x0, f_xz, a_z1, a_yz0, a_yz1, most, *r_own = lax.optimization_barrier(
        (r_z0, r_x0, f_xz, a_z1, a_yz0, a_yz1, most, *r_own)
    )
    r_xz0 = hop(r_z0, X, "rest0_xz")
    r_x1 = hop(r_own[1], X, "rest1_x")
    more = stack_rows([a_z1, a_yz0, a_yz1])
    s_most = swap_cores(most, "inv_swap")
    s_more = swap_cores(more, "inv_swap_more")
    sel = pack_inverse(structure, (most, more), (s_most, s_more), first)
    linv = after(linv, more)
    for mask in (Y, ZL):
        linv = linv + hop(linv, mask, f"squares_{mask}")
    r_z1 = lead([r_z1], 20)[0]
    r_x1 = lead([r_x1], 10)[0]
    r_x1, linv = lax.optimization_barrier((r_x1, linv))

    def deliver(kept, sent, c):
        messages = bundle(kept, swap_cores(sent, f"cross{c}_swap"))
        return [messages[0]] + [
            hop(message, (d % 2) * Y + (d // 2) * ZL, f"cross{c}_{d}")
            for d, message in zip(DEST[1:], messages[1:])
        ]

    near = products(structure, sel, (f_own, f_x), (r_own[0], r_x0), 0)
    kept, sent = products(structure, sel, (f_z, f_xz), (r_z0, r_xz0), 0, near)
    messages = deliver(kept, sent, 0)
    r_xz1 = hop(after(r_z1, kept), X, "rest1_xz")
    near = products(structure, sel, (f_own, f_x), (r_own[1], r_x1), 1)
    messages[1:] = lead(messages[1:], 5)
    kept, sent = products(structure, sel, (f_z, f_xz), (r_z1, r_xz1), 1, near)
    held = assemble(messages, 0, None)
    variance = add_sums(linv, messages, 0)
    messages = deliver(after(kept, variance), sent, 1)
    variance = add_sums(variance, messages, 1)
    held = assemble(messages, 1, held)
    hops = [hop(variance, mask, f"variance_{mask}") for mask in (X, ZH, X | ZH)]
    variance = variance + hops[0] + hops[1] + hops[2]
    half = panel.shape[2] * size // 2
    cross = held.reshape(half, 2, 2, LANES).transpose(0, 2, 1, 3).reshape(half, 2, BLK)
    return cross, variance


def solution(mesh):
    in_specs = (P("wide", "narrow"), P(None, "narrow", "wide"), P(None, "wide", "narrow"), P())
    out_specs = (P("narrow", None, "wide"), P(None, "narrow"))

    def run(inverse, panel, factor_inv, structure):
        fits = (
            mesh.shape["wide"] == 16
            and mesh.shape["narrow"] == 2 == panel.shape[0]
            and panel.shape[2] == 16 * BLK == inverse.shape[0]
        )
        return jax.shard_map(
            per_device_grid if fits else per_device_general,
            mesh=mesh,
            in_specs=in_specs,
            out_specs=out_specs,
            check_vma=False,
        )(inverse, panel, factor_inv, structure)

    return run
```
